128 devices in a mesh: trow: 16 (over x, y), tcol: 8 (over z, core).
Axes of the slice: x: 4, y: 4, z: 4, core: 2. Of those that a mesh axis runs over, the one named last changes fastest.
Arguments:
- ccd_image: bfloat16 [16, 8, 2, 512, 512], P('trow', 'tcol'), may hold values from -6 to 6
- ccd_variance: bfloat16 [16, 8, 2, 512, 512], P('trow', 'tcol'), may hold values from 0.25 to 4
- basis_taps: bfloat16 [6, 2, 21], replicated, may hold values from -1 to 1
- coef_table: float32 [8, 6], replicated, may hold values from -3 to 3
- coef_pick: int32 [16, 8, 2], P('trow', 'tcol'), may hold values from 0 to 7
- block_visit: int32 [16, 8, 2], P('trow', 'tcol'), may hold values from 0 to 7
- visit_weight: int32 [8], replicated, may hold values from 1 to 4
- patch_place: int32 [16, 8, 32], P('trow', 'tcol'), may hold values from 0 to 575, as said below
- psf_taps: float32 [2, 31], replicated, may hold values from 0.01 to 1
Outputs:
- coadd_image: float32 [16384, 8192], P('trow', 'tcol')
- significance: float32 [16384, 8192], P('trow', 'tcol')
The draws below stay inside these ranges and needn't reach their ends.
Inputs may be any that keep to these rules, and one draw needn't show every extreme that they name: `patch_place`: every entry names a tile on the sky (the target device exists). From one device at most 4 squares go to each of its eight neighbour tiles, and one neighbour gets exactly 4; the rest stay on the device's own tile.
All inputs are finite; a program needn't handle non-finite values.
Results may differ from the reference program's by a relative error of at most 0.0042.
Values may be sent and summed in bfloat16 or wider, within the bound.
No kernel may reach another device: no remote copies, remote signals or barrier semaphores. Data moves between devices by JAX's collectives and lax.ppermute only.
A program may use at most 192 MiB of HBM per device.

```python
import math
import jax
import jax.numpy as jnp
from jax import lax

BLOCK = 512
PATCH = 128
TAPS = 21
PSF_TAPS = 31
NBASIS = 6
KSETS = 8
VISITS = 8
BLK_DEV = 2
TILE_ROWS = 1024
TILE_COLS = 1024
GRID_ROWS = 16
GRID_COLS = 8
SKY_ROWS = 16384
SKY_COLS = 8192
NP = 32
CAP = 4
TPOS = 64


def draw_patch_place(key, part):
    first_key, second_key, third_key = jax.random.split(jax.random.fold_in(key, 11), 3)
    order = jnp.array([0, 1, 2, 3, 5, 6, 7, 8, 4], jnp.int32)
    step_row = order // 3 - 1
    step_col = order % 3 - 1
    rows = jnp.arange(GRID_ROWS, dtype=jnp.int32)[:, None, None]
    cols = jnp.arange(GRID_COLS, dtype=jnp.int32)[None, :, None]
    valid = (rows + step_row >= 0) & (rows + step_row < GRID_ROWS) & (cols + step_col >= 0) & (cols + step_col < GRID_COLS)
    counts = jax.random.randint(first_key, (GRID_ROWS, GRID_COLS, 9), 1, CAP + 1)
    slot_index = jnp.arange(9, dtype=jnp.int32)[None, None, :]
    forced = jnp.where(rows == 0, 6, 1)
    counts = jnp.where(slot_index == forced, CAP, counts)
    counts = jnp.where(valid & (slot_index < 8), counts, 0)
    own_count = NP - jnp.sum(counts, -1, keepdims=True)
    counts = jnp.where(slot_index == 8, own_count, counts)
    bounds = jnp.cumsum(counts, -1)
    numbers = jnp.arange(NP, dtype=jnp.int32)
    which = jnp.sum((numbers[None, None, :, None] >= bounds[:, :, None, :]).astype(jnp.int32), -1)
    which = jnp.minimum(which, 8)
    targets = jnp.sum(jnp.where(which[..., None] == jnp.arange(9, dtype=jnp.int32), order, 0), -1)
    scores = jax.random.randint(second_key, (GRID_ROWS, GRID_COLS, NP), 0, 1 << 20) * NP + numbers
    shuffle = jnp.argsort(scores, axis=-1, stable=True)
    targets = jnp.take_along_axis(targets, shuffle, -1)
    places = jax.random.randint(third_key, (GRID_ROWS, GRID_COLS, NP), 0, TPOS)
    return (targets * TPOS + places).astype(jnp.int32)


def draw_ccd_variance(key, part):
    key = jax.random.fold_in(key, 3)
    first_key = jax.random.fold_in(key, 0)
    shape = (GRID_ROWS, GRID_COLS, BLK_DEV, BLOCK, BLOCK)
    values = jnp.exp(jax.random.uniform(first_key, shape, jnp.float32, math.log(0.25), math.log(4.0)))
    return jnp.clip(values, 0.25, 4.0).astype(jnp.bfloat16)


def draw_basis_taps(key, part):
    key = jax.random.fold_in(key, 5)
    first_key, second_key, sign_key, peak_key, rest_key = jax.random.split(key, 5)
    first_axis = jax.random.permutation(first_key, TAPS)[:NBASIS]
    second_axis = jax.random.permutation(second_key, TAPS)[:NBASIS]
    positions = jnp.stack([first_axis, second_axis], 1).astype(jnp.int32)
    signs = (2 * jax.random.randint(sign_key, (NBASIS, 2), 0, 2) - 1).astype(jnp.float32)
    peaks = jax.random.uniform(peak_key, (NBASIS, 2), jnp.float32, 0.7, 1.0)
    others = jnp.clip(0.06 * jax.random.normal(rest_key, (NBASIS, 2, TAPS), jnp.float32), -0.24, 0.24)
    spots = jnp.arange(TAPS, dtype=jnp.int32)[None, None, :] == positions[:, :, None]
    return jnp.where(spots, (signs * peaks)[:, :, None], others).astype(jnp.bfloat16)


def draw_psf_taps(key, part):
    key = jax.random.fold_in(key, 7)
    middle_key, rest_key = jax.random.split(key, 2)
    centre = jnp.arange(PSF_TAPS, dtype=jnp.int32)[None, :] == PSF_TAPS // 2
    middle = jax.random.uniform(middle_key, (2, 1), jnp.float32, 0.6, 1.0)
    others = jnp.exp(jax.random.uniform(rest_key, (2, PSF_TAPS), jnp.float32, math.log(0.01), math.log(0.1)))
    return jnp.clip(jnp.where(centre, middle, others), 0.01, 1.0).astype(jnp.float32)


def place_ends(drawn, rng, least, high):
    spot = [jax.random.randint(jax.random.fold_in(rng, axis), (), 0, length) for axis, length in enumerate(drawn.shape)]
    longest = drawn.shape.index(max(drawn.shape))
    beside = spot[:longest] + [(spot[longest] + 1) % drawn.shape[longest]] + spot[longest + 1:]
    return drawn.at[tuple(spot)].set(least).at[tuple(beside)].set(high)


def level_of(stream_key, shape, cuts, least, high):
    factor_of = 1.0
    for axis_at, shards_of in cuts:
        heights = jax.random.uniform(jax.random.fold_in(jax.random.fold_in(stream_key, 6), axis_at), (shards_of,), jnp.float32, least / len(cuts), high / len(cuts))
        factor_of = factor_of * jnp.repeat(jnp.exp(heights), shape[axis_at] // shards_of).reshape((-1,) + (1,) * (len(shape) - 1 - axis_at))
    return factor_of


def scatter_about(stream_key, dims, spread, limit, cuts=(), kind=jnp.bfloat16):
    factor_of = level_of(stream_key, dims, cuts, -0.22, 0.18) if cuts else 1.0
    values = jax.random.normal(stream_key, dims, jnp.float32) * spread * factor_of
    return jnp.minimum(jnp.maximum(values, -limit), limit).astype(kind)


def setup_inputs(seed: int = 0) -> dict:
    arg_keys = jax.random.split(jax.random.key(seed), 10)
    return {
        "ccd_image": scatter_about(arg_keys[0], (GRID_ROWS, GRID_COLS, BLK_DEV, BLOCK, BLOCK), 1.0, 6.0, ((0, 16), (1, 8))),
        "ccd_variance": draw_ccd_variance(jax.random.fold_in(arg_keys[9], 71), 0),
        "basis_taps": draw_basis_taps(jax.random.fold_in(arg_keys[9], 71), 0),
        "coef_table": scatter_about(arg_keys[3], (KSETS, NBASIS), 0.5, 3.0, (), jnp.float32),
        "coef_pick": place_ends(jax.random.randint(arg_keys[4], (GRID_ROWS, GRID_COLS, BLK_DEV), 0, KSETS), jax.random.fold_in(arg_keys[4], 1), 0, KSETS - 1).astype(jnp.int32),
        "block_visit": place_ends(jax.random.randint(arg_keys[5], (GRID_ROWS, GRID_COLS, BLK_DEV), 0, VISITS), jax.random.fold_in(arg_keys[5], 1), 0, VISITS - 1).astype(jnp.int32),
        "visit_weight": place_ends(jax.random.randint(arg_keys[6], (VISITS,), 1, 5), jax.random.fold_in(arg_keys[6], 1), 1, 4).astype(jnp.int32),
        "patch_place": draw_patch_place(jax.random.fold_in(arg_keys[9], 71), 0),
        "psf_taps": draw_psf_taps(jax.random.fold_in(arg_keys[9], 71), 0),
    }


def along_last(values, kernel_taps):
    length = values.shape[-1]
    half_width = kernel_taps.shape[-1] // 2
    padded = jnp.pad(values, [(0, 0)] * (values.ndim - 1) + [(half_width, half_width)])
    summed = jnp.zeros(values.shape, jnp.float32)
    for number in range(kernel_taps.shape[-1]):
        summed = summed + kernel_taps[..., number][..., None, None] * padded[..., number:number + length]
    return summed

def along_before(values, kernel_taps):
    return jnp.swapaxes(along_last(jnp.swapaxes(values, -1, -2), kernel_taps), -1, -2)

def reference(ccd_image, ccd_variance, basis_taps, coef_table, coef_pick, block_visit, visit_weight, patch_place, psf_taps):
    taps_float = basis_taps.astype(jnp.float32)
    squared = lax.optimization_barrier((taps_float * taps_float).astype(jnp.bfloat16)).astype(jnp.float32)
    images = ccd_image.reshape(-1, BLOCK, BLOCK)
    variances = ccd_variance.reshape(-1, BLOCK, BLOCK)
    coefs = coef_table[coef_pick.reshape(-1)]
    weights = visit_weight[block_visit.reshape(-1)].astype(jnp.float32)

    def convolve_block(inputs):
        image, variance, coef_row, weight = inputs
        rows_image = along_last(image.astype(jnp.float32), taps_float[:, 0]).astype(jnp.bfloat16)
        full_image = along_before(rows_image.astype(jnp.float32), taps_float[:, 1])
        sent_image = (weight * lax.optimization_barrier(jnp.sum(coef_row[:, None, None] * full_image, 0))).astype(jnp.bfloat16)
        rows_var = along_last(variance.astype(jnp.float32), squared[:, 0]).astype(jnp.bfloat16)
        full_var = along_before(rows_var.astype(jnp.float32), squared[:, 1])
        sent_var = (weight * weight * lax.optimization_barrier(jnp.sum((coef_row * coef_row)[:, None, None] * full_var, 0))).astype(jnp.bfloat16)
        return (sent_image, sent_var)
    sent_image, sent_var = lax.map(convolve_block, (images, variances, coefs, weights))
    per_side = BLOCK // PATCH

    def to_squares(blocks):
        shaped = blocks.reshape(GRID_ROWS, GRID_COLS, BLK_DEV, per_side, PATCH, per_side, PATCH)
        return shaped.transpose(0, 1, 2, 3, 5, 4, 6).reshape(GRID_ROWS, GRID_COLS, NP, PATCH, PATCH)
    square_image = to_squares(sent_image).astype(jnp.float32)
    square_var = to_squares(sent_var).astype(jnp.float32)
    targets = patch_place // TPOS
    places = patch_place % TPOS
    patch_rows = TILE_ROWS // PATCH
    patch_cols = TILE_COLS // PATCH
    dest_row = jnp.arange(GRID_ROWS, dtype=jnp.int32)[:, None, None] + targets // 3 - 1
    dest_col = jnp.arange(GRID_COLS, dtype=jnp.int32)[None, :, None] + targets % 3 - 1
    grid_row = (dest_row * patch_rows + places // patch_cols).astype(jnp.int32)
    grid_col = (dest_col * patch_cols + places % patch_cols).astype(jnp.int32)
    empty_sky = jnp.zeros((GRID_ROWS * patch_rows, GRID_COLS * patch_cols, PATCH, PATCH), jnp.float32)
    sky_image = empty_sky.at[grid_row, grid_col].add(square_image)
    sky_var = empty_sky.at[grid_row, grid_col].add(square_var)
    coadd_image = sky_image.transpose(0, 2, 1, 3).reshape(SKY_ROWS, SKY_COLS)
    coadd_variance = sky_var.transpose(0, 2, 1, 3).reshape(SKY_ROWS, SKY_COLS)
    psf_square = psf_taps * psf_taps
    smooth = along_before(along_last(coadd_image, psf_taps[0]), psf_taps[1])
    smooth_variance = along_before(along_last(coadd_variance, psf_square[0]), psf_square[1])
    significance = smooth / jnp.sqrt(smooth_variance + 1.0)
    return (coadd_image, significance)
```

```python
import functools
import jax
import jax.numpy as jnp
from jax import lax
from jax.experimental import pallas as pl
from jax.experimental.pallas import tpu as pltpu
from jax.sharding import PartitionSpec as P

F32 = jnp.float32
BF16 = jnp.bfloat16
BLOCK = 512
PATCH = 128
TAPS = 21
RADIUS = 10
PSF = 31
REACH = 15
NBASIS = 6
NP = 32
CAP = 4
GROUP = CAP * PATCH + 16
TILE = 1024
RIM = 16
STEP = 208
MIB = 1 << 20

SMEM = functools.partial(pl.BlockSpec, memory_space=pltpu.SMEM)


def iotas(shape):
    return (lax.broadcasted_iota(jnp.int32, shape, 0), lax.broadcasted_iota(jnp.int32, shape, 1))


def dot(a, b):
    return jnp.dot(a, b, preferred_element_type=F32)


def split(x):
    high = x.astype(BF16)
    return high, (x - high.astype(F32)).astype(BF16)


def diagonals(read, count, first, step, lanes):
    rows, cols = iotas((16, lanes))
    offset = (cols - rows) & (lanes - 1)
    out = jnp.zeros((16, lanes), F32)
    for t in range(count):
        out = jnp.where(offset == (first + step * t) % lanes, read(t), out)
    return out


def toeplitz(base, m, low, high):
    lanes = base.shape[1]
    turned = pltpu.roll(base, (16 * m) % lanes, 1) if (16 * m) % lanes else base
    rows, cols = iotas(base.shape)
    offset = cols - rows - 16 * m
    return jnp.where((offset >= low) & (offset <= high), turned, 0.0)


def corner(read, count, reach):
    rows, cols = iotas((32, 128))
    left = rows < 16
    tap = rows + 112 - cols + reach - jnp.where(left, 128, 0)
    tap = jnp.where(left == (cols < 64), tap, -1)
    out = jnp.zeros((32, 128), F32)
    for t in range(count):
        out = jnp.where(tap == t, read(t), out)
    return out


def match_kernel(
    squared, table, pick, visit, weight, place, taps, x_ref,
    up_ref, down_ref, left_ref, right_ref, own_ref,
    across, edges, down, rows_ref, total, heading, rank, slots,
):
    block = pl.program_id(0)

    def read(k, axis):
        return lambda t: taps[(2 * k + axis) * TAPS + t]

    def kept(x):
        return (x * x if squared else x).astype(BF16)

    @pl.when(block == 0)
    def _():
        for g in range(8):
            for s in range(CAP):
                slots[g * CAP + s] = -1

        def order(n, counts):
            entry = place[n]
            d = entry >> 6
            heading[n] = d
            r = jnp.int32(0)
            for g in range(9):
                r = jnp.where(d == g, counts[g], r)
            rank[n] = r

            @pl.when(d != 4)
            def _():
                slots[jnp.where(d > 4, d - 1, d) * CAP + r] = entry & 63

            return tuple(counts[g] + (d == g).astype(jnp.int32) for g in range(9))

        lax.fori_loop(0, NP, order, (jnp.int32(0),) * 9)
        _, lanes = iotas((16, 128))
        for g in range(8):
            line = jnp.full((16, 128), -1.0, F32)
            for s in range(CAP):
                line = jnp.where(lanes == s, slots[g * CAP + s].astype(F32), line)
            line = line.astype(BF16)
            last = pl.ds(CAP * PATCH, 16)
            if g < 3:
                up_ref[g, last, :] = line
            elif g == 3:
                left_ref[0, last, :] = line
            elif g == 4:
                right_ref[0, last, :] = line
            else:
                down_ref[g - 5, last, :] = line
        edges[...] = jnp.zeros(edges.shape, BF16)
        for k in range(NBASIS):
            base = diagonals(read(k, 0), TAPS, RADIUS, -1, 256)
            for m in range(16):
                across[k, pl.ds(16 * m, 16), :] = kept(toeplitz(base, m, -RADIUS, RADIUS))
            edges[k // 2, pl.ds(112, 32), pl.ds(k % 2 * 128, 128)] = kept(corner(read(k, 0), TAPS, RADIUS))
            base = diagonals(read(k, 1), TAPS, -26, 1, 256)
            for m in range(18):
                down[k, pl.ds(16 * m, 16), :] = kept(toeplitz(base, m, -26, -6))

    lanes = lax.broadcasted_iota(jnp.int32, (BLOCK, 128), 1)
    for pair in range(NBASIS // 2):
        fix = dot(x_ref[0, :, 128:384], edges[pair])
        for half in range(2):
            k = 2 * pair + half
            part = fix[:, 128 * half : 128 * half + 128]
            first = dot(x_ref[0, :, :256], across[k])
            rows_ref[k, :, 0:128] = first[:, :128].astype(BF16)
            rows_ref[k, :, 128:256] = (first[:, 128:] + jnp.where(lanes >= 64, part, 0.0)).astype(BF16)
            second = dot(x_ref[0, :, 256:], across[k])
            rows_ref[k, :, 256:384] = (second[:, :128] + jnp.where(lanes < 64, part, 0.0)).astype(BF16)
            rows_ref[k, :, 384:512] = second[:, 128:].astype(BF16)
    scale = weight[visit[block]].astype(F32)
    if squared:
        scale = scale * scale
    for side in range(2):
        span = pl.ds(256 * side, 256)
        for k in range(NBASIS):
            coef = table[pick[block], k]
            if squared:
                coef = coef * coef
            top = dot(down[k, 16:288, :], rows_ref[k, 0:256, span])
            low = dot(down[k, 0:272, :], rows_ref[k, 256:512, span])
            middle = top[240:] + low[:32]
            if k == 0:
                total[0:240, span] = coef * top[:240]
                total[240:272, span] = coef * middle
                total[272:512, span] = coef * low[32:]
            else:
                total[0:240, span] += coef * top[:240]
                total[240:272, span] += coef * middle
                total[272:512, span] += coef * low[32:]
    for i in range(4):
        for j in range(4):
            square = (scale * total[128 * i : 128 * i + 128, 128 * j : 128 * j + 128]).astype(BF16)
            n = block * 16 + 4 * i + j
            d = heading[n]
            where = pl.ds(pl.multiple_of(rank[n] * PATCH, PATCH), PATCH)

            @pl.when(d < 3)
            def _():
                up_ref[d, where, :] = square

            @pl.when(d == 3)
            def _():
                left_ref[0, where, :] = square

            @pl.when(d == 4)
            def _():
                own_ref[n] = square

            @pl.when(d == 5)
            def _():
                right_ref[0, where, :] = square

            @pl.when(d > 5)
            def _():
                down_ref[d - 6, where, :] = square


def match(squared, table, pick, visit, weight, place, taps, blocks):
    whole = lambda *shape: pl.BlockSpec(shape, lambda b: (0,) * len(shape))
    return pl.pallas_call(
        functools.partial(match_kernel, squared),
        grid=(2,),
        in_specs=[SMEM()] * 6 + [pl.BlockSpec((1, BLOCK, BLOCK), lambda b: (b, 0, 0))],
        out_specs=[whole(3, GROUP, 128), whole(3, GROUP, 128), whole(1, GROUP, 128), whole(1, GROUP, 128), whole(NP, PATCH, PATCH)],
        out_shape=[
            jax.ShapeDtypeStruct(s, BF16)
            for s in ((3, GROUP, 128), (3, GROUP, 128), (1, GROUP, 128), (1, GROUP, 128), (NP, PATCH, PATCH))
        ],
        scratch_shapes=[
            pltpu.VMEM((NBASIS, 256, 256), BF16),
            pltpu.VMEM((NBASIS // 2, 256, 256), BF16),
            pltpu.VMEM((NBASIS, 288, 256), BF16),
            pltpu.VMEM((NBASIS, BLOCK, BLOCK), BF16),
            pltpu.VMEM((BLOCK, BLOCK), F32),
            pltpu.SMEM((NP,), jnp.int32),
            pltpu.SMEM((NP,), jnp.int32),
            pltpu.SMEM((8 * CAP,), jnp.int32),
        ],
        compiler_params=pltpu.CompilerParams(vmem_limit_bytes=40 * MIB),
        name="match_var" if squared else "match_img",
    )(table, pick, visit, weight, place, taps, blocks)


def ring(value, axis, step):
    count = lax.axis_size(axis)
    return lax.ppermute(value, axis, [(i, (i + step) % count) for i in range(count)])


def exchange(parcels):
    up, down, left, right = parcels
    below = ring(up, "trow", -1)
    above = ring(down, "trow", 1)
    leftward = jnp.concatenate([left, below[0:1], above[0:1]], 0)
    rightward = jnp.concatenate([right, below[2:3], above[2:3]], 0)
    return below, above, ring(leftward, "tcol", -1), ring(rightward, "tcol", 1)


def gather_kernel(place, own_ref, below_ref, above_ref, east_ref, west_ref, tile_ref, top_ref, bottom_ref, lines, spots, sem):
    groups = [(below_ref, 0), (above_ref, 0)] + [(east_ref, g) for g in range(3)] + [(west_ref, g) for g in range(3)]
    for g, (ref, at) in enumerate(groups):
        lines[pl.ds(g, 1), :] = ref[at, CAP * PATCH :, :].astype(F32)[0:1].astype(jnp.int32)
    copy = pltpu.make_async_copy(lines, spots, sem)
    copy.start()
    tile_ref[...] = jnp.zeros(tile_ref.shape, F32)

    def add(spot, square):
        rows = pl.ds(pl.multiple_of((spot >> 3) * PATCH, PATCH), PATCH)
        cols = pl.ds(pl.multiple_of((spot & 7) * PATCH, PATCH), PATCH)
        tile_ref[rows, cols] += square.astype(F32)

    def own(n, _):
        entry = place[n]

        @pl.when((entry >> 6) == 4)
        def _():
            add(entry & 63, own_ref[n])

    lax.fori_loop(0, NP, own, None)
    copy.wait()
    for g, (ref, at) in enumerate(groups):
        for s in range(CAP):
            spot = spots[g, s]

            @pl.when(spot >= 0)
            def _():
                add(spot, ref[at, s * PATCH : (s + 1) * PATCH, :])

    top_ref[...] = tile_ref[0:RIM, :]
    bottom_ref[...] = tile_ref[TILE - RIM :, :]


def gather(name, place, own, below, above, east, west):
    middle = pl.BlockSpec((1, GROUP, 128), lambda i: (1, 0, 0))
    whole = lambda *shape: pl.BlockSpec(shape, lambda i: (0,) * len(shape))
    return pl.pallas_call(
        gather_kernel,
        grid=(1,),
        in_specs=[SMEM(), whole(NP, PATCH, PATCH), middle, middle, whole(3, GROUP, 128), whole(3, GROUP, 128)],
        out_specs=[whole(TILE, TILE), whole(RIM, TILE), whole(RIM, TILE)],
        out_shape=[jax.ShapeDtypeStruct(s, F32) for s in ((TILE, TILE), (RIM, TILE), (RIM, TILE))],
        scratch_shapes=[pltpu.VMEM((8, 128), jnp.int32), pltpu.SMEM((8, 128), jnp.int32), pltpu.SemaphoreType.DMA],
        compiler_params=pltpu.CompilerParams(vmem_limit_bytes=40 * MIB),
        name=name,
    )(place, own, below, above, east, west)


def psf_reader(squared, psf, axis):
    def read(t):
        tap = psf[axis * PSF + t]
        return tap * tap if squared else tap

    return read


def column_kernel(squared, psf, tile_ref, above_ref, below_ref, out_ref, first_ref, last_ref, band, high, low):
    step = pl.program_id(0)
    here, count = lax.axis_index("trow"), lax.axis_size("trow")

    @pl.when(step == 0)
    def _():
        base = diagonals(psf_reader(squared, psf, 1), PSF, 1, 1, 256)
        for m in range(STEP // 16):
            band[0, pl.ds(16 * m, 16), :], band[1, pl.ds(16 * m, 16), :] = split(toeplitz(base, m, 1, PSF))

    def put(at, value):
        high[pl.ds(at, value.shape[0]), :], low[pl.ds(at, value.shape[0]), :] = split(value)

    put(0, jnp.where(here > 0, above_ref[...], 0.0))
    put(RIM, tile_ref[...])
    put(RIM + TILE, jnp.where(here < count - 1, below_ref[...], 0.0))
    put(2 * RIM + TILE, jnp.zeros((32, 256), F32))
    for t in range(5):
        rows = min(STEP, TILE - STEP * t)
        window = pl.ds(STEP * t, 256)
        out_ref[pl.ds(STEP * t, rows), :] = (
            dot(band[0, :rows], high[window, :]) + dot(band[0, :rows], low[window, :]) + dot(band[1, :rows], high[window, :])
        )
    lanes = lax.broadcasted_iota(jnp.int32, (128, 128), 1)

    @pl.when(step == 0)
    def _():
        first_ref[...] = sum(
            pltpu.roll(jnp.where(lanes < RIM, out_ref[128 * g : 128 * g + 128, :128], 0.0), RIM * g, 1) for g in range(8)
        )

    @pl.when(step == 3)
    def _():
        last_ref[...] = sum(
            pltpu.roll(jnp.where(lanes >= 128 - RIM, out_ref[128 * g : 128 * g + 128, 128:], 0.0), (RIM * g + RIM) % 128, 1)
            for g in range(8)
        )


def column_pass(squared, psf, tile, above, below):
    strip = pl.BlockSpec((128, 128), lambda c: (0, 0))
    rim = pl.BlockSpec((RIM, 256), lambda c: (0, c))
    chunk = pl.BlockSpec((TILE, 256), lambda c: (0, c))
    return pl.pallas_call(
        functools.partial(column_kernel, squared),
        grid=(4,),
        in_specs=[SMEM(), chunk, rim, rim],
        out_specs=[chunk, strip, strip],
        out_shape=[jax.ShapeDtypeStruct(s, F32) for s in ((TILE, TILE), (128, 128), (128, 128))],
        scratch_shapes=[pltpu.VMEM((2, STEP, 256), BF16), pltpu.VMEM((1088, 256), BF16), pltpu.VMEM((1088, 256), BF16)],
        compiler_params=pltpu.CompilerParams(vmem_limit_bytes=40 * MIB),
        name="column_var" if squared else "column_img",
    )(psf, tile, above, below)


def row_kernel(squared, psf, v_ref, west_ref, east_ref, *rest):
    if squared:
        smooth_ref, out_ref, band, ends, high, low = rest
    else:
        out_ref, band, ends, high, low = rest
    step = pl.program_id(0)
    here, count = lax.axis_index("tcol"), lax.axis_size("tcol")

    @pl.when(step == 0)
    def _():
        read = psf_reader(squared, psf, 0)
        base = diagonals(read, PSF, REACH, -1, 256)
        for m in range(16):
            band[0, pl.ds(16 * m, 16), :], band[1, pl.ds(16 * m, 16), :] = split(toeplitz(base, m, -REACH, REACH))
        ends[...] = jnp.zeros(ends.shape, BF16)
        ends[pl.ds(112, 32), 0:128], ends[pl.ds(112, 32), 128:256] = split(corner(read, PSF, REACH))

    lanes = lax.broadcasted_iota(jnp.int32, (128, 128), 1)
    high[:, 128 : 128 + TILE], low[:, 128 : 128 + TILE] = split(v_ref[...])
    for part in range(2):
        g = 2 * step + part
        rows = pl.ds(128 * part, 128)
        piece = pltpu.roll(west_ref[...], (112 + 256 - RIM * g) & 127, 1)
        piece = jnp.where((lanes >= 112) & (here > 0), piece, 0.0)
        high[rows, 0:128], low[rows, 0:128] = split(piece)
        piece = pltpu.roll(east_ref[...], (256 - RIM * g) & 127, 1)
        piece = jnp.where((lanes < RIM) & (here < count - 1), piece, 0.0)
        high[rows, 128 + TILE :], low[rows, 128 + TILE :] = split(piece)
    lanes = lax.broadcasted_iota(jnp.int32, (256, 128), 1)
    fixes = []
    for w in range(5):
        window = pl.ds(256 * w, 256)
        both = dot(high[:, window], ends[...])
        fixes.append(both[:, :128] + both[:, 128:] + dot(low[:, window], ends[:, 0:128]))
    for c in range(4):
        window = pl.ds(128 + 256 * c, 256)
        main = dot(high[:, window], band[0]) + dot(low[:, window], band[0]) + dot(high[:, window], band[1])
        for part in range(2):
            fix = jnp.where(lanes >= 64, fixes[c + 1], 0.0) if part else jnp.where(lanes < 64, fixes[c], 0.0)
            value = main[:, 128 * part : 128 * part + 128] + fix
            cols = pl.ds(256 * c + 128 * part, 128)
            if squared:
                value = smooth_ref[:, cols] / jnp.sqrt(value + 1.0)
            out_ref[:, cols] = value


def row_pass(squared, psf, v, west, east, smooth=None):
    strip = pl.BlockSpec((128, 128), lambda r: (0, 0))
    chunk = pl.BlockSpec((256, TILE), lambda r: (r, 0))
    extra = (smooth,) if squared else ()
    return pl.pallas_call(
        functools.partial(row_kernel, squared),
        grid=(4,),
        in_specs=[SMEM(), chunk, strip, strip] + [chunk] * len(extra),
        out_specs=chunk,
        out_shape=jax.ShapeDtypeStruct((TILE, TILE), F32),
        scratch_shapes=[
            pltpu.VMEM((2, 256, 256), BF16),
            pltpu.VMEM((256, 256), BF16),
            pltpu.VMEM((256, TILE + 256), BF16),
            pltpu.VMEM((256, TILE + 256), BF16),
        ],
        compiler_params=pltpu.CompilerParams(vmem_limit_bytes=40 * MIB),
        name="row_var" if squared else "row_img",
    )(psf, v, west, east, *extra)


def shards(ccd_image, ccd_variance, basis_taps, coef_table, coef_pick, block_visit, visit_weight, patch_place, psf_taps):
    place = patch_place.reshape(NP)
    taps = basis_taps.astype(F32).reshape(-1)
    psf = psf_taps.reshape(-1)
    small = (coef_table, coef_pick.reshape(2), block_visit.reshape(2), visit_weight, place, taps)

    *parcels, own_image = match(False, *small, ccd_image.reshape(2, BLOCK, BLOCK))
    *parcels_var, own_var = match(True, *small, ccd_variance.reshape(2, BLOCK, BLOCK))
    tile, top, bottom = gather("gather_img", place, own_image, *exchange(parcels))
    tile_var, top_var, bottom_var = gather("gather_var", place, own_var, *exchange(parcels_var))
    v, first, last = column_pass(False, psf, tile, ring(bottom, "trow", 1), ring(top, "trow", -1))
    smooth = row_pass(False, psf, v, ring(last, "tcol", 1), ring(first, "tcol", -1))
    v, first, last = column_pass(True, psf, tile_var, ring(bottom_var, "trow", 1), ring(top_var, "trow", -1))
    significance = row_pass(True, psf, v, ring(last, "tcol", 1), ring(first, "tcol", -1), smooth)
    return tile, significance


def solution(mesh):
    place = P("trow", "tcol", None)
    blocks = P("trow", "tcol", None, None, None)
    in_specs = (blocks, blocks, P(), P(), place, place, P(), place, P())
    out_specs = (P("trow", "tcol"), P("trow", "tcol"))
    return jax.shard_map(shards, mesh=mesh, in_specs=in_specs, out_specs=out_specs, check_vma=False)
```

```python
import functools
import jax
import jax.numpy as jnp
from jax import lax
from jax.experimental import pallas as pl
from jax.experimental.pallas import tpu as pltpu
from jax.sharding import PartitionSpec as P

F32 = jnp.float32
BF16 = jnp.bfloat16
BLOCK = 512
PATCH = 128
TAPS = 21
RADIUS = 10
PSF = 31
REACH = 15
NBASIS = 6
NP = 32
CAP = 4
GROUP = CAP * PATCH + 16
TILE = 1024
RIM = 16
STEP = 208
MIB = 1 << 20

HBM = pl.BlockSpec(memory_space=pltpu.HBM)
SMEM = functools.partial(pl.BlockSpec, memory_space=pltpu.SMEM)


def iotas(shape):
    return (lax.broadcasted_iota(jnp.int32, shape, 0), lax.broadcasted_iota(jnp.int32, shape, 1))


def dot(a, b):
    return jnp.dot(a, b, preferred_element_type=F32)


def split(x):
    high = x.astype(BF16)
    return high, (x - high.astype(F32)).astype(BF16)


def diagonals(read, count, first, step, lanes):
    rows, cols = iotas((16, lanes))
    offset = (cols - rows) & (lanes - 1)
    out = jnp.zeros((16, lanes), F32)
    for t in range(count):
        out = jnp.where(offset == (first + step * t) % lanes, read(t), out)
    return out


def toeplitz(base, m, low, high):
    lanes = base.shape[1]
    turned = pltpu.roll(base, (16 * m) % lanes, 1) if (16 * m) % lanes else base
    rows, cols = iotas(base.shape)
    offset = cols - rows - 16 * m
    return jnp.where((offset >= low) & (offset <= high), turned, 0.0)


def corner(read, count, reach):
    rows, cols = iotas((32, 128))
    left = rows < 16
    tap = rows + 112 - cols + reach - jnp.where(left, 128, 0)
    tap = jnp.where(left == (cols < 64), tap, -1)
    out = jnp.zeros((32, 128), F32)
    for t in range(count):
        out = jnp.where(tap == t, read(t), out)
    return out


def via(d):
    vertical = ((d * 11) >> 5) - 1
    sideways = d - 3 * ((d * 11) >> 5) - 1
    vertical = jnp.where((lax.axis_index("trow") & 1) == 0, -vertical, vertical)
    sideways = jnp.where((lax.axis_index("tcol") & 1) == 0, -sideways, sideways)
    return 3 * vertical + sideways + 4


def match_kernel(
    squared, table_in, pick_in, visit_in, weight_in, place_in, taps, x_in,
    up_ref, down_ref, left_ref, right_ref, own_ref,
    across, edges, down, rows_ref, total, heading, rank, slots,
    table, pick, visit, weight, place, x_ref, sems, x_sem,
):
    block = pl.program_id(0)
    small = [(table_in, table), (pick_in, pick), (visit_in, visit), (weight_in, weight), (place_in, place)]
    small = [pltpu.make_async_copy(a, b, sems.at[i]) for i, (a, b) in enumerate(small)]
    pixels = [pltpu.make_async_copy(x_in.at[b], x_ref.at[b], x_sem.at[b]) for b in range(2)]

    def read(k, axis):
        return lambda t: taps[(2 * k + axis) * TAPS + t]

    def kept(x):
        return (x * x if squared else x).astype(BF16)

    @pl.when(block == 0)
    def _():
        for copy in small + pixels:
            copy.start()
        edges[...] = jnp.zeros(edges.shape, BF16)
        for k in range(NBASIS):
            base = diagonals(read(k, 0), TAPS, RADIUS, -1, 256)
            for m in range(16):
                across[k, pl.ds(16 * m, 16), :] = kept(toeplitz(base, m, -RADIUS, RADIUS))
            edges[k // 2, pl.ds(112, 32), pl.ds(k % 2 * 128, 128)] = kept(corner(read(k, 0), TAPS, RADIUS))
            base = diagonals(read(k, 1), TAPS, -26, 1, 256)
            for m in range(18):
                down[k, pl.ds(16 * m, 16), :] = kept(toeplitz(base, m, -26, -6))
        for copy in small:
            copy.wait()
        for g in range(8):
            for s in range(CAP):
                slots[g * CAP + s] = -1

        def order(n, counts):
            entry = place[0, 0, n]
            d = via(entry >> 6)
            heading[n] = d
            r = jnp.int32(0)
            for g in range(9):
                r = jnp.where(d == g, counts[g], r)
            rank[n] = r

            @pl.when(d != 4)
            def _():
                slots[jnp.where(d > 4, d - 1, d) * CAP + r] = entry & 63

            return tuple(counts[g] + (d == g).astype(jnp.int32) for g in range(9))

        lax.fori_loop(0, NP, order, (jnp.int32(0),) * 9)
        _, lanes = iotas((16, 128))
        for g in range(8):
            line = jnp.full((16, 128), -1.0, F32)
            for s in range(CAP):
                line = jnp.where(lanes == s, slots[g * CAP + s].astype(F32), line)
            line = line.astype(BF16)
            last = pl.ds(CAP * PATCH, 16)
            if g < 3:
                up_ref[g, last, :] = line
            elif g == 3:
                left_ref[0, last, :] = line
            elif g == 4:
                right_ref[0, last, :] = line
            else:
                down_ref[g - 5, last, :] = line
        pixels[0].wait()

    @pl.when(block == 1)
    def _():
        pixels[1].wait()

    lanes = lax.broadcasted_iota(jnp.int32, (BLOCK, 128), 1)
    for pair in range(NBASIS // 2):
        fix = dot(x_ref[block, :, 128:384], edges[pair])
        for half in range(2):
            k = 2 * pair + half
            part = fix[:, 128 * half : 128 * half + 128]
            first = dot(x_ref[block, :, :256], across[k])
            rows_ref[k, :, 0:128] = first[:, :128].astype(BF16)
            rows_ref[k, :, 128:256] = (first[:, 128:] + jnp.where(lanes >= 64, part, 0.0)).astype(BF16)
            second = dot(x_ref[block, :, 256:], across[k])
            rows_ref[k, :, 256:384] = (second[:, :128] + jnp.where(lanes < 64, part, 0.0)).astype(BF16)
            rows_ref[k, :, 384:512] = second[:, 128:].astype(BF16)
    scale = weight[visit[0, 0, block]].astype(F32)
    if squared:
        scale = scale * scale
    for side in range(2):
        span = pl.ds(256 * side, 256)
        for k in range(NBASIS):
            coef = table[pick[0, 0, block], k]
            if squared:
                coef = coef * coef
            top = dot(down[k, 16:288, :], rows_ref[k, 0:256, span])
            low = dot(down[k, 0:272, :], rows_ref[k, 256:512, span])
            middle = top[240:] + low[:32]
            if k == 0:
                total[0:240, span] = coef * top[:240]
                total[240:272, span] = coef * middle
                total[272:512, span] = coef * low[32:]
            else:
                total[0:240, span] += coef * top[:240]
                total[240:272, span] += coef * middle
                total[272:512, span] += coef * low[32:]
    for i in range(4):
        for j in range(4):
            square = scale * total[128 * i : 128 * i + 128, 128 * j : 128 * j + 128]
            own_ref[block * 16 + 4 * i + j] = square.astype(BF16)

    def leave(i, _):
        n = block * 16 + i
        d = heading[n]
        where = pl.ds(pl.multiple_of(rank[n] * PATCH, PATCH), PATCH)

        @pl.when(d < 3)
        def _():
            up_ref[d, where, :] = own_ref[n]

        @pl.when(d == 3)
        def _():
            left_ref[0, where, :] = own_ref[n]

        @pl.when(d == 5)
        def _():
            right_ref[0, where, :] = own_ref[n]

        @pl.when(d > 5)
        def _():
            down_ref[d - 6, where, :] = own_ref[n]

    lax.fori_loop(0, 16, leave, None)


def match(squared, table, pick, visit, weight, place, taps, blocks):
    whole = lambda *shape: pl.BlockSpec(shape, lambda b: (0,) * len(shape))
    return pl.pallas_call(
        functools.partial(match_kernel, squared),
        grid=(2,),
        in_specs=[HBM] * 5 + [SMEM(), HBM],
        out_specs=[whole(3, GROUP, 128), whole(3, GROUP, 128), whole(1, GROUP, 128), whole(1, GROUP, 128), whole(NP, PATCH, PATCH)],
        out_shape=[
            jax.ShapeDtypeStruct(s, BF16)
            for s in ((3, GROUP, 128), (3, GROUP, 128), (1, GROUP, 128), (1, GROUP, 128), (NP, PATCH, PATCH))
        ],
        scratch_shapes=[
            pltpu.VMEM((NBASIS, 256, 256), BF16),
            pltpu.VMEM((NBASIS // 2, 256, 256), BF16),
            pltpu.VMEM((NBASIS, 288, 256), BF16),
            pltpu.VMEM((NBASIS, BLOCK, BLOCK), BF16),
            pltpu.VMEM((BLOCK, BLOCK), F32),
            pltpu.SMEM((NP,), jnp.int32),
            pltpu.SMEM((NP,), jnp.int32),
            pltpu.SMEM((8 * CAP,), jnp.int32),
            pltpu.SMEM(table.shape, F32),
            pltpu.SMEM(pick.shape, jnp.int32),
            pltpu.SMEM(visit.shape, jnp.int32),
            pltpu.SMEM(weight.shape, jnp.int32),
            pltpu.SMEM(place.shape, jnp.int32),
            pltpu.VMEM((2, BLOCK, BLOCK), BF16),
            pltpu.SemaphoreType.DMA((5,)),
            pltpu.SemaphoreType.DMA((2,)),
        ],
        compiler_params=pltpu.CompilerParams(vmem_limit_bytes=40 * MIB),
        name="match_var" if squared else "match_img",
    )(table, pick, visit, weight, place, taps, blocks)


def swap(value, axis, odd):
    rows, cols = lax.axis_size("trow"), lax.axis_size("tcol")
    pairs = []
    for r in range(rows):
        for c in range(cols):
            at, count = (r, rows) if axis == "trow" else (c, cols)
            to = ((at + 1) ^ 1) - 1 if odd else at ^ 1
            if axis == "trow":
                target = (to, c) if 0 <= to < count else (r, c ^ 1)
            else:
                target = (r, to) if 0 <= to < count else (r ^ 1, c)
            pairs.append((r * cols + c, target[0] * cols + target[1]))
    return lax.ppermute(value, ("trow", "tcol"), pairs)


def first_stage(parcels):
    return swap(parcels[0], "trow", False), swap(parcels[1], "trow", True)


def second_stage(parcels, below, above):
    _, _, left, right = parcels
    leftward = jnp.concatenate([left, below[0:1], above[0:1]], 0)
    rightward = jnp.concatenate([right, below[2:3], above[2:3]], 0)
    return below, above, swap(leftward, "tcol", False), swap(rightward, "tcol", True)


def pack(read, first):
    lanes = lax.broadcasted_iota(jnp.int32, (128, 128), 1)
    out = jnp.zeros((128, 128), F32)
    for g in range(8):
        rows = read(pl.ds(128 * g, 128))
        rows = jnp.where(lanes < RIM if first else lanes >= 128 - RIM, rows, 0.0)
        turn = RIM * g if first else (RIM * g + RIM) % 128
        out = out + (pltpu.roll(rows, turn, 1) if turn else rows)
    return out


def gather_kernel(image, place, own_ref, below_ref, above_ref, east_ref, west_ref, *rest):
    if image:
        tile_ref, up_ref, down_ref, first_ref, last_ref, lines, spots, sem = rest
    else:
        up_in, down_in, first_in, last_in, out_ref, up_ref, down_ref, first_ref, last_ref, lines, spots, sem, tile_ref = rest
    groups = [(below_ref, 0), (above_ref, 0)] + [(east_ref, g) for g in range(3)] + [(west_ref, g) for g in range(3)]
    for g, (ref, at) in enumerate(groups):
        lines[pl.ds(g, 1), :] = ref[at, CAP * PATCH :, :].astype(F32)[0:1].astype(jnp.int32)
    copy = pltpu.make_async_copy(lines, spots, sem)
    copy.start()
    tile_ref[...] = jnp.zeros(tile_ref.shape, F32)

    def add(spot, square):
        rows = pl.ds(pl.multiple_of((spot >> 3) * PATCH, PATCH), PATCH)
        cols = pl.ds(pl.multiple_of((spot & 7) * PATCH, PATCH), PATCH)
        tile_ref[rows, cols] += square.astype(F32)

    def own(n, _):
        entry = place[n]

        @pl.when((entry >> 6) == 4)
        def _():
            add(entry & 63, own_ref[n])

    lax.fori_loop(0, NP, own, None)
    copy.wait()
    for g, (ref, at) in enumerate(groups):
        for s in range(CAP):
            spot = spots[g, s]

            @pl.when(spot >= 0)
            def _():
                add(spot, ref[at, s * PATCH : (s + 1) * PATCH, :])

    first = pack(lambda rows: tile_ref[rows, :128], True)
    last = pack(lambda rows: tile_ref[rows, TILE - 128 :], False)
    even = (lax.axis_index("trow") & 1) == 0
    ends = [tile_ref[pl.ds(pl.multiple_of(jnp.where(even, a, TILE - RIM - a), RIM), RIM), :] for a in (TILE - RIM, 0)]
    if image:
        for ref, value, n in ((up_ref, ends[0], RIM), (down_ref, ends[1], RIM), (first_ref, first, 128), (last_ref, last, 128)):
            ref[pl.ds(0, n), :], ref[pl.ds(n, n), :] = split(value)
    else:
        out_ref[...] = tile_ref[...].astype(BF16)
        for ref, old, value, n in (
            (up_ref, up_in, ends[0], RIM), (down_ref, down_in, ends[1], RIM),
            (first_ref, first_in, first, 128), (last_ref, last_in, last, 128),
        ):
            ref[pl.ds(0, 2 * n), :] = old[...]
            ref[pl.ds(2 * n, n), :] = value.astype(BF16)


def gather(image, place, own, below, above, east, west, rims=()):
    middle = pl.BlockSpec((1, GROUP, 128), lambda i: (1, 0, 0))
    whole = lambda *shape: pl.BlockSpec(shape, lambda i: (0,) * len(shape))
    count = 2 if image else 3
    shapes = [(TILE, TILE), (count * RIM, TILE), (count * RIM, TILE), (count * 128, 128), (count * 128, 128)]
    return pl.pallas_call(
        functools.partial(gather_kernel, image),
        grid=(1,),
        in_specs=[SMEM(), whole(NP, PATCH, PATCH), middle, middle, whole(3, GROUP, 128), whole(3, GROUP, 128)]
        + [whole(*r.shape) for r in rims],
        out_specs=[whole(*s) for s in shapes],
        out_shape=[jax.ShapeDtypeStruct(s, F32 if image and i == 0 else BF16) for i, s in enumerate(shapes)],
        scratch_shapes=[pltpu.VMEM((8, 128), jnp.int32), pltpu.SMEM((8, 128), jnp.int32), pltpu.SemaphoreType.DMA]
        + ([] if image else [pltpu.VMEM((TILE, TILE), F32)]),
        compiler_params=pltpu.CompilerParams(vmem_limit_bytes=40 * MIB),
        name="gather_img" if image else "gather_var",
    )(place, own, below, above, east, west, *rims)


def choose(first, a, b):
    return jnp.where(first, a.astype(F32), b.astype(F32))


def turn_kernel(first_ref, last_ref, even_first, odd_first, even_last, odd_last, even_out, odd_out):
    here, count = lax.axis_index("trow"), lax.axis_size("trow")
    row_odd, col_odd = (here & 1) == 1, (lax.axis_index("tcol") & 1) == 1
    for out, flip in ((even_out, col_odd), (odd_out, jnp.logical_not(col_odd))):
        out[pl.ds(0, 384), :] = choose(flip, first_ref[...], last_ref[...]).astype(BF16)
        met = [choose(flip, a[...], b[...]) for a, b in ((even_first, even_last), (odd_first, odd_last))]
        out[pl.ds(384, 48), :] = jnp.where(here > 0, choose(row_odd, *met), 0.0).astype(BF16)
        out[pl.ds(432, 48), :] = jnp.where(here < count - 1, choose(row_odd, *met[::-1]), 0.0).astype(BF16)


def turn(first, last, even, odd):
    whole = pl.BlockSpec((384, 128), lambda i: (0, 0))
    near = pl.BlockSpec((48, 128), lambda i: (0, 0))
    far = pl.BlockSpec((48, 128), lambda i: (0, 7))
    return pl.pallas_call(
        turn_kernel,
        grid=(1,),
        in_specs=[whole, whole, near, near, far, far],
        out_specs=[pl.BlockSpec((480, 128), lambda i: (0, 0))] * 2,
        out_shape=[jax.ShapeDtypeStruct((480, 128), BF16)] * 2,
        compiler_params=pltpu.CompilerParams(vmem_limit_bytes=8 * MIB),
        name="turn",
    )(first, last, even, odd, even, odd)


def filter_kernel(
    psf, tile_ref, var_ref, row_even, row_odd, col_even, col_odd, out_ref,
    img_in, high, low, var, bands, flats, ends, v_high, v_low, v_var, out, in_sems, out_sems,
):
    row, rows_n = lax.axis_index("trow"), lax.axis_size("trow")
    col, cols_n = lax.axis_index("tcol"), lax.axis_size("tcol")
    copies = []
    for q in range(4):
        rows = pl.ds(256 * q, 256)
        inside = pl.ds(256 * q + RIM, 256)
        copies.append((
            pltpu.make_async_copy(tile_ref.at[rows, :], img_in.at[rows, :], in_sems.at[2 * q]),
            pltpu.make_async_copy(var_ref.at[rows, :], var.at[inside, pl.ds(0, TILE)], in_sems.at[2 * q + 1]),
        ))
    for pair in copies:
        for copy in pair:
            copy.start()

    peaks = []
    for axis in range(2):
        peak = psf[axis * PSF]
        for t in range(1, PSF):
            peak = jnp.maximum(peak, psf[axis * PSF + t])
        peaks.append(peak)
    scale = peaks[0] * peaks[1]

    def read(axis):
        return lambda t: psf[axis * PSF + t]

    over = [1.0 / jnp.full((16, 256), peak, F32) for peak in peaks]
    column = diagonals(read(1), PSF, 1, 1, 256) * over[1]
    flat = diagonals(read(0), PSF, REACH, -1, 256) * over[0]
    edge = corner(read(0), PSF, REACH) * over[0][0:1, :128]
    ends[...] = jnp.zeros(ends.shape, BF16)
    for squared in range(2):
        for m in range(STEP // 16):
            bands[squared, pl.ds(16 * m, 16), :] = toeplitz(column, m, 1, PSF).astype(BF16)
        for m in range(16):
            flats[squared, pl.ds(16 * m, 16), :] = toeplitz(flat, m, -REACH, REACH).astype(BF16)
        for part in range(2):
            span = pl.ds(128 * part, 128)
            ends[squared, pl.ds(128 * part, 16), span] = edge[16:].astype(BF16)
            ends[squared, pl.ds(128 * part + 112, 16), span] = edge[:16].astype(BF16)
        column, flat, edge = column * column, flat * flat, edge * edge

    lanes = lax.broadcasted_iota(jnp.int32, (128, 128), 1)
    side = pl.ds(TILE, 128)
    def met(along, at, start, rows):
        even, odd = (row_even, row_odd) if along is row else (col_even, col_odd)
        parts = even[start : start + rows, :], odd[start : start + rows, :]
        return choose((along & 1) == 1, *(parts[::-1] if at else parts))

    for i, ref in enumerate((high, low, var)):
        ref[pl.ds(0, RIM), pl.ds(0, TILE)] = jnp.where(row > 0, met(row, 0, RIM * i, RIM), 0.0).astype(BF16)
        ref[pl.ds(RIM + TILE, RIM), pl.ds(0, TILE)] = jnp.where(
            row < rows_n - 1, met(row, 1, RIM * i, RIM), 0.0
        ).astype(BF16)
        ref[pl.ds(2 * RIM + TILE, RIM * 2), :] = jnp.zeros((2 * RIM, TILE + 128), BF16)
        west, east = met(col, 0, 128 * i, 128), met(col, 1, 128 * i, 128)
        at_west, at_east = (lanes >= 128 - RIM) & (col > 0), (lanes < RIM) & (col < cols_n - 1)
        for g in range(8):
            near = pltpu.roll(east, 128 - RIM * g, 1) if g else east
            far = pltpu.roll(west, (112 - RIM * g) % 128, 1) if g != 7 else west
            ref[pl.ds(RIM + 128 * g, 128), side] = jnp.where(at_east, near, jnp.where(at_west, far, 0.0)).astype(BF16)
        for at, start in ((0, 384), (RIM + TILE, 432)):
            near, far = met(col, 1, start + RIM * i, RIM), met(col, 0, start + RIM * i, RIM)
            ref[pl.ds(at, RIM), side] = jnp.where(at_east[:RIM], near, jnp.where(at_west[:RIM], far, 0.0)).astype(BF16)

    spans = [(256 * c, 256) for c in range(4)] + [(TILE, 128)]
    ready = 0
    for t in range(5):
        count = min(STEP, TILE - STEP * t)
        while ready < 4 and 256 * ready < STEP * t + 240:
            for copy in copies[ready]:
                copy.wait()
            rows = pl.ds(RIM + 256 * ready, 256)
            high[rows, pl.ds(0, TILE)], low[rows, pl.ds(0, TILE)] = split(img_in[pl.ds(256 * ready, 256), :])
            ready += 1
        window = pl.ds(STEP * t, 256)
        target = pl.ds(STEP * t, count)
        for start, width in spans:
            span = pl.ds(start, width)
            value = dot(bands[0], high[window, span]) + dot(bands[0], low[window, span])
            v_high[target, span], v_low[target, span] = split(value[:count])
            v_var[target, span] = dot(bands[1], var[window, span])[:count].astype(BF16)

    lanes = lax.broadcasted_iota(jnp.int32, (256, 128), 1)
    near = lanes < 64
    for q in range(4):
        rows = pl.ds(256 * q, 256)
        results = []
        for squared, parts in ((0, (v_high, v_low)), (1, (v_var,))):
            def about(ref, w):
                if w == 0:
                    return ref[rows, side]
                return jnp.where(near, ref[rows, pl.ds(256 * w, 128)], ref[rows, pl.ds(256 * w - 128, 128)])

            fixes = []
            for w in (0, 2):
                both = sum(dot(jnp.concatenate([about(ref, w), about(ref, w + 1)], 1), ends[squared]) for ref in parts)
                fixes += [both[:, :128], both[:, 128:]]
            fixes.append(fixes[0])
            values = []
            for c in range(4):
                span = pl.ds(256 * c, 256)
                main = sum(dot(ref[rows, span], flats[squared]) for ref in parts)
                values.append(main[:, :128] + jnp.where(near, fixes[c], 0.0))
                values.append(main[:, 128:] + jnp.where(near, 0.0, fixes[c + 1]))
            results.append(values)
        for c in range(8):
            out[rows, pl.ds(128 * c, 128)] = scale * results[0][c] * lax.rsqrt(scale * scale * results[1][c] + 1.0)
        pltpu.make_async_copy(out.at[rows, :], out_ref.at[rows, :], out_sems.at[q]).start()
    for q in range(4):
        rows = pl.ds(256 * q, 256)
        pltpu.make_async_copy(out.at[rows, :], out_ref.at[rows, :], out_sems.at[q]).wait()


def detect(psf, tile, tile_var, *rims):
    vmem = pl.BlockSpec(memory_space=pltpu.VMEM)
    wide = TILE + 128
    return pl.pallas_call(
        filter_kernel,
        in_specs=[SMEM(), HBM, HBM, vmem, vmem, vmem, vmem],
        out_specs=HBM,
        out_shape=jax.ShapeDtypeStruct((TILE, TILE), F32),
        scratch_shapes=[pltpu.VMEM((TILE, TILE), F32)]
        + [pltpu.VMEM((1088, wide), BF16)] * 3
        + [pltpu.VMEM((2, STEP, 256), BF16), pltpu.VMEM((2, 256, 256), BF16), pltpu.VMEM((2, 256, 256), BF16)]
        + [pltpu.VMEM((TILE, wide), BF16)] * 3
        + [pltpu.VMEM((TILE, TILE), F32), pltpu.SemaphoreType.DMA((8,)), pltpu.SemaphoreType.DMA((4,))],
        compiler_params=pltpu.CompilerParams(vmem_limit_bytes=48 * MIB),
        name="filter",
    )(psf, tile, tile_var, *rims)


def shards(ccd_image, ccd_variance, basis_taps, coef_table, coef_pick, block_visit, visit_weight, patch_place, psf_taps):
    place = patch_place.reshape(NP)
    taps = basis_taps.astype(F32).reshape(-1)
    psf = psf_taps.reshape(-1)
    pin = lambda x: pltpu.with_memory_space_constraint(x, pltpu.HBM)
    small = (*map(pin, (coef_table, coef_pick, block_visit, visit_weight, patch_place)), taps)

    *parcels, own_image = match(False, *small, pin(ccd_image.reshape(2, BLOCK, BLOCK)))
    ahead = first_stage(parcels)
    taps_var, _ = lax.optimization_barrier((taps, own_image))
    *parcels_var, own_var = match(True, *small[:-1], taps_var, pin(ccd_variance.reshape(2, BLOCK, BLOCK)))
    behind = first_stage(parcels_var)
    tile, *rims = gather(True, place, own_image, *second_stage(parcels, *ahead))
    *behind, _ = lax.optimization_barrier((*behind, rims[0]))
    tile_var, up, down, first, last = gather(False, place, own_var, *second_stage(parcels_var, *behind), rims)
    rows = swap(up, "trow", False), swap(down, "trow", True)
    sides = turn(first, last, *rows)
    significance = detect(psf, tile, tile_var, *rows, swap(sides[0], "tcol", False), swap(sides[1], "tcol", True))
    return tile, significance


def solution(mesh):
    place = P("trow", "tcol", None)
    blocks = P("trow", "tcol", None, None, None)
    in_specs = (blocks, blocks, P(), P(), place, place, P(), place, P())
    out_specs = (P("trow", "tcol"), P("trow", "tcol"))
    return jax.shard_map(shards, mesh=mesh, in_specs=in_specs, out_specs=out_specs, check_vma=False)
```

```python
import functools
import jax
import jax.numpy as jnp
from jax import lax
from jax.experimental import pallas as pl
from jax.experimental.pallas import tpu as pltpu
from jax.sharding import PartitionSpec as P

F32 = jnp.float32
BF16 = jnp.bfloat16
BLOCK = 512
PATCH = 128
TAPS = 21
RADIUS = 10
PSF = 31
REACH = 15
NBASIS = 6
NP = 32
CAP = 4
GROUP = CAP * PATCH + 16
TILE = 1024
RIM = 16
STEP = 208
MIB = 1 << 20

HBM = pl.BlockSpec(memory_space=pltpu.HBM)
VMEM = pl.BlockSpec(memory_space=pltpu.VMEM)
SMEM = functools.partial(pl.BlockSpec, memory_space=pltpu.SMEM)


def iotas(shape):
    return (lax.broadcasted_iota(jnp.int32, shape, 0), lax.broadcasted_iota(jnp.int32, shape, 1))


def dot(a, b):
    return jnp.dot(a, b, preferred_element_type=F32)


def split(x):
    high = x.astype(BF16)
    return high, (x - high.astype(F32)).astype(BF16)


def diagonals(read, count, first, step, lanes):
    rows, cols = iotas((16, lanes))
    offset = (cols - rows) & (lanes - 1)
    out = jnp.zeros((16, lanes), F32)
    for t in range(count):
        out = jnp.where(offset == (first + step * t) % lanes, read(t), out)
    return out


def toeplitz(base, m, low, high):
    lanes = base.shape[1]
    turned = pltpu.roll(base, (16 * m) % lanes, 1) if (16 * m) % lanes else base
    rows, cols = iotas(base.shape)
    offset = cols - rows - 16 * m
    return jnp.where((offset >= low) & (offset <= high), turned, 0.0)


def corner(read, count, reach):
    rows, cols = iotas((32, 128))
    left = rows < 16
    tap = rows + 112 - cols + reach - jnp.where(left, 128, 0)
    tap = jnp.where(left == (cols < 64), tap, -1)
    out = jnp.zeros((32, 128), F32)
    for t in range(count):
        out = jnp.where(tap == t, read(t), out)
    return out


def via(d):
    vertical = ((d * 11) >> 5) - 1
    sideways = d - 3 * ((d * 11) >> 5) - 1
    vertical = jnp.where((lax.axis_index("trow") & 1) == 0, -vertical, vertical)
    sideways = jnp.where((lax.axis_index("tcol") & 1) == 0, -sideways, sideways)
    return 3 * vertical + sideways + 4


def match_kernel(
    squared, table_in, pick_in, visit_in, weight_in, place_in, taps, x_in,
    up_ref, down_ref, left_ref, right_ref, own_ref,
    across, edges, down, rows_ref, total, leaving, count, slot, slots,
    table, pick, visit, weight, place, x_ref, sems, x_sem,
):
    small = [(table_in, table), (pick_in, pick), (visit_in, visit), (weight_in, weight), (place_in, place)]
    small = [pltpu.make_async_copy(a, b, sems.at[i]) for i, (a, b) in enumerate(small)]
    pixels = [pltpu.make_async_copy(x_in.at[b], x_ref.at[b], x_sem.at[b]) for b in range(2)]
    for copy in small + pixels:
        copy.start()

    def read(k, axis):
        return lambda t: taps[(2 * k + axis) * TAPS + t]

    def kept(x):
        return (x * x if squared else x).astype(BF16)

    def build(k):
        base = diagonals(read(k, 0), TAPS, RADIUS, -1, 256)
        for m in range(16):
            across[k, pl.ds(16 * m, 16), :] = kept(toeplitz(base, m, -RADIUS, RADIUS))
        edges[k // 2, pl.ds(112, 32), pl.ds(k % 2 * 128, 128)] = kept(corner(read(k, 0), TAPS, RADIUS))
        base = diagonals(read(k, 1), TAPS, -26, 1, 256)
        for m in range(18):
            down[k, pl.ds(16 * m, 16), :] = kept(toeplitz(base, m, -26, -6))

    for g in range(9):
        count[g] = 0
    for s in range(8 * CAP):
        slots[s] = -1
    edges[...] = jnp.zeros(edges.shape, BF16)
    for k in range(NBASIS // 2):
        build(k)
    for copy in small:
        copy.wait()
    for n in range(NP):
        entry = place[0, 0, n]
        d = via(entry >> 6)
        r = count[d]
        count[d] = r + 1
        s = jnp.where(d == 4, 8 * CAP, jnp.where(d > 4, d - 1, d) * CAP + r)
        slot[n] = s
        slots[s] = entry & 63
    for k in range(NBASIS // 2, NBASIS):
        build(k)
    _, lanes = iotas((16, 128))
    parcels = [(up_ref, 0), (up_ref, 1), (up_ref, 2), (left_ref, 0), (right_ref, 0), (down_ref, 0), (down_ref, 1), (down_ref, 2)]
    for g, (ref, at) in enumerate(parcels):
        line = jnp.full((16, 128), -1.0, F32)
        for s in range(CAP):
            line = jnp.where(lanes == s, slots[g * CAP + s].astype(F32), line)
        ref[at, pl.ds(CAP * PATCH, 16), :] = line.astype(BF16)

    def one(block, _):
        pltpu.make_async_copy(x_in.at[block], x_ref.at[block], x_sem.at[block]).wait()
        lanes = lax.broadcasted_iota(jnp.int32, (BLOCK, 128), 1)
        for pair in range(NBASIS // 2):
            fix = dot(x_ref[block, :, 128:384], edges[pair])
            for half in range(2):
                k = 2 * pair + half
                part = fix[:, 128 * half : 128 * half + 128]
                first = dot(x_ref[block, :, :256], across[k])
                rows_ref[k, :, 0:128] = first[:, :128].astype(BF16)
                rows_ref[k, :, 128:256] = (first[:, 128:] + jnp.where(lanes >= 64, part, 0.0)).astype(BF16)
                second = dot(x_ref[block, :, 256:], across[k])
                rows_ref[k, :, 256:384] = (second[:, :128] + jnp.where(lanes < 64, part, 0.0)).astype(BF16)
                rows_ref[k, :, 384:512] = second[:, 128:].astype(BF16)
        scale = weight[visit[0, 0, block]].astype(F32)
        if squared:
            scale = scale * scale
        for side in range(2):
            span = pl.ds(256 * side, 256)
            for k in range(NBASIS):
                coef = table[pick[0, 0, block], k]
                if squared:
                    coef = coef * coef
                top = dot(down[k, 16:288, :], rows_ref[k, 0:256, span])
                low = dot(down[k, 0:272, :], rows_ref[k, 256:512, span])
                middle = top[240:] + low[:32]
                if k == 0:
                    total[0:240, span] = coef * top[:240]
                    total[240:272, span] = coef * middle
                    total[272:512, span] = coef * low[32:]
                else:
                    total[0:240, span] += coef * top[:240]
                    total[240:272, span] += coef * middle
                    total[272:512, span] += coef * low[32:]
        for i in range(4):
            for j in range(4):
                n = block * 16 + 4 * i + j
                square = (scale * total[128 * i : 128 * i + 128, 128 * j : 128 * j + 128]).astype(BF16)
                own_ref[n] = square
                leaving[slot[n]] = square

    lax.fori_loop(0, 2, one, None)
    for g, (ref, at) in enumerate(parcels):
        for s in range(CAP):
            ref[at, pl.ds(s * PATCH, PATCH), :] = leaving[g * CAP + s]


def match(squared, table, pick, visit, weight, place, taps, blocks):
    shapes = ((3, GROUP, 128), (3, GROUP, 128), (1, GROUP, 128), (1, GROUP, 128), (NP, PATCH, PATCH))
    return pl.pallas_call(
        functools.partial(match_kernel, squared),
        in_specs=[HBM] * 5 + [SMEM(), HBM],
        out_specs=[VMEM] * 5,
        out_shape=[jax.ShapeDtypeStruct(s, BF16) for s in shapes],
        scratch_shapes=[
            pltpu.VMEM((NBASIS, 256, 256), BF16),
            pltpu.VMEM((NBASIS // 2, 256, 256), BF16),
            pltpu.VMEM((NBASIS, 288, 256), BF16),
            pltpu.VMEM((NBASIS, BLOCK, BLOCK), BF16),
            pltpu.VMEM((BLOCK, BLOCK), F32),
            pltpu.VMEM((8 * CAP + 1, PATCH, PATCH), BF16),
            pltpu.SMEM((9,), jnp.int32),
            pltpu.SMEM((NP,), jnp.int32),
            pltpu.SMEM((8 * CAP + 1,), jnp.int32),
            pltpu.SMEM(table.shape, F32),
            pltpu.SMEM(pick.shape, jnp.int32),
            pltpu.SMEM(visit.shape, jnp.int32),
            pltpu.SMEM(weight.shape, jnp.int32),
            pltpu.SMEM(place.shape, jnp.int32),
            pltpu.VMEM((2, BLOCK, BLOCK), BF16),
            pltpu.SemaphoreType.DMA((5,)),
            pltpu.SemaphoreType.DMA((2,)),
        ],
        compiler_params=pltpu.CompilerParams(vmem_limit_bytes=24 * MIB),
        name="match_var" if squared else "match_img",
    )(table, pick, visit, weight, place, taps, blocks)


def swap(value, axis, odd):
    rows, cols = lax.axis_size("trow"), lax.axis_size("tcol")
    pairs = []
    for r in range(rows):
        for c in range(cols):
            at, count = (r, rows) if axis == "trow" else (c, cols)
            to = ((at + 1) ^ 1) - 1 if odd else at ^ 1
            if axis == "trow":
                target = (to, c) if 0 <= to < count else (r, c ^ 1)
            else:
                target = (r, to) if 0 <= to < count else (r ^ 1, c)
            pairs.append((r * cols + c, target[0] * cols + target[1]))
    return lax.ppermute(value, ("trow", "tcol"), pairs)


def first_stage(parcels):
    return swap(parcels[0], "trow", False), swap(parcels[1], "trow", True)


def second_stage(parcels, below, above):
    _, _, left, right = parcels
    leftward = jnp.concatenate([left, below[0:1], above[0:1]], 0)
    rightward = jnp.concatenate([right, below[2:3], above[2:3]], 0)
    return below, above, swap(leftward, "tcol", False), swap(rightward, "tcol", True)


def pack(read, first):
    lanes = lax.broadcasted_iota(jnp.int32, (128, 128), 1)
    out = jnp.zeros((128, 128), F32)
    for g in range(8):
        rows = read(pl.ds(128 * g, 128))
        rows = jnp.where(lanes < RIM if first else lanes >= 128 - RIM, rows, 0.0)
        turn = RIM * g if first else (RIM * g + RIM) % 128
        out = out + (pltpu.roll(rows, turn, 1) if turn else rows)
    return out


def add(tile_ref, spot, square):
    rows = pl.ds(pl.multiple_of((spot >> 3) * PATCH, PATCH), PATCH)
    cols = pl.ds(pl.multiple_of((spot & 7) * PATCH, PATCH), PATCH)
    tile_ref[rows, cols] += square.astype(F32)


def add_own(place, own_ref, tile_ref):
    tile_ref[...] = jnp.zeros(tile_ref.shape, F32)

    def own(n, _):
        entry = place[n]

        @pl.when((entry >> 6) == 4)
        def _():
            add(tile_ref, entry & 63, own_ref[n])

    lax.fori_loop(0, NP, own, None)


def own_sum(name, place, own):
    return pl.pallas_call(
        add_own,
        in_specs=[SMEM(), VMEM],
        out_specs=VMEM,
        out_shape=jax.ShapeDtypeStruct((TILE, TILE), F32),
        compiler_params=pltpu.CompilerParams(vmem_limit_bytes=12 * MIB),
        name=name,
    )(place, own)


def gather_kernel(image, place, start_ref, below_ref, above_ref, east_ref, west_ref, *rest):
    if image:
        tile_ref, up_ref, down_ref, first_ref, last_ref, lines, spots, sem = rest
    else:
        up_in, down_in, first_in, last_in, out_ref, up_ref, down_ref, first_ref, last_ref, lines, spots, sem, tile_ref = rest
    groups = [(below_ref, 1), (above_ref, 1)] + [(east_ref, g) for g in range(3)] + [(west_ref, g) for g in range(3)]
    for g, (ref, at) in enumerate(groups):
        lines[pl.ds(g, 1), :] = ref[at, CAP * PATCH :, :].astype(F32)[0:1].astype(jnp.int32)
    copy = pltpu.make_async_copy(lines, spots, sem)
    copy.start()
    if image:
        add_own(place, start_ref, tile_ref)
    else:
        tile_ref[...] = start_ref[...]
    copy.wait()
    for g, (ref, at) in enumerate(groups):
        for s in range(CAP):
            spot = spots[g, s]

            @pl.when(spot >= 0)
            def _():
                add(tile_ref, spot, ref[at, s * PATCH : (s + 1) * PATCH, :])

    first = pack(lambda rows: tile_ref[rows, :128], True)
    last = pack(lambda rows: tile_ref[rows, TILE - 128 :], False)
    even = (lax.axis_index("trow") & 1) == 0
    ends = [tile_ref[pl.ds(pl.multiple_of(jnp.where(even, a, TILE - RIM - a), RIM), RIM), :] for a in (TILE - RIM, 0)]
    if image:
        for ref, value, n in ((up_ref, ends[0], RIM), (down_ref, ends[1], RIM), (first_ref, first, 128), (last_ref, last, 128)):
            ref[pl.ds(0, n), :], ref[pl.ds(n, n), :] = split(value)
    else:
        out_ref[...] = tile_ref[...].astype(BF16)
        for ref, old, value, n in (
            (up_ref, up_in, ends[0], RIM), (down_ref, down_in, ends[1], RIM),
            (first_ref, first_in, first, 128), (last_ref, last_in, last, 128),
        ):
            ref[pl.ds(0, 2 * n), :] = old[...]
            ref[pl.ds(2 * n, n), :] = value.astype(BF16)


def gather(image, place, start, below, above, east, west, rims=()):
    count = 2 if image else 3
    shapes = [(TILE, TILE), (count * RIM, TILE), (count * RIM, TILE), (count * 128, 128), (count * 128, 128)]
    return pl.pallas_call(
        functools.partial(gather_kernel, image),
        in_specs=[SMEM()] + [VMEM] * (5 + len(rims)),
        out_specs=[VMEM] * len(shapes),
        out_shape=[jax.ShapeDtypeStruct(s, F32 if image and i == 0 else BF16) for i, s in enumerate(shapes)],
        scratch_shapes=[pltpu.VMEM((8, 128), jnp.int32), pltpu.SMEM((8, 128), jnp.int32), pltpu.SemaphoreType.DMA]
        + ([] if image else [pltpu.VMEM((TILE, TILE), F32)]),
        compiler_params=pltpu.CompilerParams(vmem_limit_bytes=20 * MIB),
        name="gather_img" if image else "gather_var",
    )(place, start, below, above, east, west, *rims)


def choose(first, a, b):
    return jnp.where(first, a.astype(F32), b.astype(F32))


def turn_kernel(first_ref, last_ref, even_first, odd_first, even_last, odd_last, even_out, odd_out):
    here, count = lax.axis_index("trow"), lax.axis_size("trow")
    row_odd, col_odd = (here & 1) == 1, (lax.axis_index("tcol") & 1) == 1
    for out, flip in ((even_out, col_odd), (odd_out, jnp.logical_not(col_odd))):
        out[pl.ds(0, 384), :] = choose(flip, first_ref[...], last_ref[...]).astype(BF16)
        met = [choose(flip, a[...], b[...]) for a, b in ((even_first, even_last), (odd_first, odd_last))]
        out[pl.ds(384, 48), :] = jnp.where(here > 0, choose(row_odd, *met), 0.0).astype(BF16)
        out[pl.ds(432, 48), :] = jnp.where(here < count - 1, choose(row_odd, *met[::-1]), 0.0).astype(BF16)


def turn(first, last, even, odd):
    whole = pl.BlockSpec((384, 128), lambda i: (0, 0))
    near = pl.BlockSpec((48, 128), lambda i: (0, 0))
    far = pl.BlockSpec((48, 128), lambda i: (0, 7))
    return pl.pallas_call(
        turn_kernel,
        grid=(1,),
        in_specs=[whole, whole, near, near, far, far],
        out_specs=[pl.BlockSpec((480, 128), lambda i: (0, 0))] * 2,
        out_shape=[jax.ShapeDtypeStruct((480, 128), BF16)] * 2,
        compiler_params=pltpu.CompilerParams(vmem_limit_bytes=8 * MIB),
        name="turn",
    )(first, last, even, odd, even, odd)


def filter_kernel(
    psf, tile_ref, var_ref, row_even, row_odd, col_even, col_odd, out_ref,
    img_in, high, low, var, bands, flats, ends, v_high, v_low, v_var, out, in_sems, out_sems,
):
    row, rows_n = lax.axis_index("trow"), lax.axis_size("trow")
    col, cols_n = lax.axis_index("tcol"), lax.axis_size("tcol")
    copies = []
    for q in range(4):
        rows = pl.ds(256 * q, 256)
        inside = pl.ds(256 * q + RIM, 256)
        copies.append((
            pltpu.make_async_copy(tile_ref.at[rows, :], img_in.at[rows, :], in_sems.at[2 * q]),
            pltpu.make_async_copy(var_ref.at[rows, :], var.at[inside, pl.ds(0, TILE)], in_sems.at[2 * q + 1]),
        ))
    for pair in copies:
        for copy in pair:
            copy.start()

    peaks = []
    for axis in range(2):
        peak = psf[axis * PSF]
        for t in range(1, PSF):
            peak = jnp.maximum(peak, psf[axis * PSF + t])
        peaks.append(peak)
    scale = peaks[0] * peaks[1]

    def read(axis):
        return lambda t: psf[axis * PSF + t]

    over = [1.0 / jnp.full((16, 256), peak, F32) for peak in peaks]
    column = diagonals(read(1), PSF, 1, 1, 256) * over[1]
    flat = diagonals(read(0), PSF, REACH, -1, 256) * over[0]
    edge = corner(read(0), PSF, REACH) * over[0][0:1, :128]
    ends[...] = jnp.zeros(ends.shape, BF16)
    for squared in range(2):
        for m in range(STEP // 16):
            bands[squared, pl.ds(16 * m, 16), :] = toeplitz(column, m, 1, PSF).astype(BF16)
        for m in range(16):
            flats[squared, pl.ds(16 * m, 16), :] = toeplitz(flat, m, -REACH, REACH).astype(BF16)
        for part in range(2):
            span = pl.ds(128 * part, 128)
            ends[squared, pl.ds(128 * part, 16), span] = edge[16:].astype(BF16)
            ends[squared, pl.ds(128 * part + 112, 16), span] = edge[:16].astype(BF16)
        column, flat, edge = column * column, flat * flat, edge * edge

    lanes = lax.broadcasted_iota(jnp.int32, (128, 128), 1)
    side = pl.ds(TILE, 128)
    def met(along, at, start, rows):
        even, odd = (row_even, row_odd) if along is row else (col_even, col_odd)
        parts = even[start : start + rows, :], odd[start : start + rows, :]
        return choose((along & 1) == 1, *(parts[::-1] if at else parts))

    for i, ref in enumerate((high, low, var)):
        ref[pl.ds(0, RIM), pl.ds(0, TILE)] = jnp.where(row > 0, met(row, 0, RIM * i, RIM), 0.0).astype(BF16)
        ref[pl.ds(RIM + TILE, RIM), pl.ds(0, TILE)] = jnp.where(
            row < rows_n - 1, met(row, 1, RIM * i, RIM), 0.0
        ).astype(BF16)
        ref[pl.ds(2 * RIM + TILE, RIM * 2), :] = jnp.zeros((2 * RIM, TILE + 128), BF16)
        west, east = met(col, 0, 128 * i, 128), met(col, 1, 128 * i, 128)
        at_west, at_east = (lanes >= 128 - RIM) & (col > 0), (lanes < RIM) & (col < cols_n - 1)
        for g in range(8):
            near = pltpu.roll(east, 128 - RIM * g, 1) if g else east
            far = pltpu.roll(west, (112 - RIM * g) % 128, 1) if g != 7 else west
            ref[pl.ds(RIM + 128 * g, 128), side] = jnp.where(at_east, near, jnp.where(at_west, far, 0.0)).astype(BF16)
        for at, start in ((0, 384), (RIM + TILE, 432)):
            near, far = met(col, 1, start + RIM * i, RIM), met(col, 0, start + RIM * i, RIM)
            ref[pl.ds(at, RIM), side] = jnp.where(at_east[:RIM], near, jnp.where(at_west[:RIM], far, 0.0)).astype(BF16)

    spans = [(256 * c, 256) for c in range(4)] + [(TILE, 128)]
    ready = 0
    for t in range(5):
        count = min(STEP, TILE - STEP * t)
        while ready < 4 and 256 * ready < STEP * t + 240:
            for copy in copies[ready]:
                copy.wait()
            rows = pl.ds(RIM + 256 * ready, 256)
            high[rows, pl.ds(0, TILE)], low[rows, pl.ds(0, TILE)] = split(img_in[pl.ds(256 * ready, 256), :])
            ready += 1
        window = pl.ds(STEP * t, 256)
        target = pl.ds(STEP * t, count)
        for start, width in spans:
            span = pl.ds(start, width)
            value = dot(bands[0], high[window, span]) + dot(bands[0], low[window, span])
            v_high[target, span], v_low[target, span] = split(value[:count])
            v_var[target, span] = dot(bands[1], var[window, span])[:count].astype(BF16)

    lanes = lax.broadcasted_iota(jnp.int32, (256, 128), 1)
    near = lanes < 64
    for q in range(4):
        rows = pl.ds(256 * q, 256)
        results = []
        for squared, parts in ((0, (v_high, v_low)), (1, (v_var,))):
            def about(ref, w):
                if w == 0:
                    return ref[rows, side]
                return jnp.where(near, ref[rows, pl.ds(256 * w, 128)], ref[rows, pl.ds(256 * w - 128, 128)])

            fixes = []
            for w in (0, 2):
                both = sum(dot(jnp.concatenate([about(ref, w), about(ref, w + 1)], 1), ends[squared]) for ref in parts)
                fixes += [both[:, :128], both[:, 128:]]
            fixes.append(fixes[0])
            values = []
            for c in range(4):
                span = pl.ds(256 * c, 256)
                main = sum(dot(ref[rows, span], flats[squared]) for ref in parts)
                values.append(main[:, :128] + jnp.where(near, fixes[c], 0.0))
                values.append(main[:, 128:] + jnp.where(near, 0.0, fixes[c + 1]))
            results.append(values)
        for c in range(8):
            out[rows, pl.ds(128 * c, 128)] = scale * results[0][c] * lax.rsqrt(scale * scale * results[1][c] + 1.0)
        pltpu.make_async_copy(out.at[rows, :], out_ref.at[rows, :], out_sems.at[q]).start()
    for q in range(4):
        rows = pl.ds(256 * q, 256)
        pltpu.make_async_copy(out.at[rows, :], out_ref.at[rows, :], out_sems.at[q]).wait()


def detect(psf, tile, tile_var, *rims):
    vmem = pl.BlockSpec(memory_space=pltpu.VMEM)
    wide = TILE + 128
    return pl.pallas_call(
        filter_kernel,
        in_specs=[SMEM(), HBM, HBM, vmem, vmem, vmem, vmem],
        out_specs=HBM,
        out_shape=jax.ShapeDtypeStruct((TILE, TILE), F32),
        scratch_shapes=[pltpu.VMEM((TILE, TILE), F32)]
        + [pltpu.VMEM((1088, wide), BF16)] * 3
        + [pltpu.VMEM((2, STEP, 256), BF16), pltpu.VMEM((2, 256, 256), BF16), pltpu.VMEM((2, 256, 256), BF16)]
        + [pltpu.VMEM((TILE, wide), BF16)] * 3
        + [pltpu.VMEM((TILE, TILE), F32), pltpu.SemaphoreType.DMA((8,)), pltpu.SemaphoreType.DMA((4,))],
        compiler_params=pltpu.CompilerParams(vmem_limit_bytes=32 * MIB),
        name="filter",
    )(psf, tile, tile_var, *rims)


def shards(ccd_image, ccd_variance, basis_taps, coef_table, coef_pick, block_visit, visit_weight, patch_place, psf_taps):
    place = patch_place.reshape(NP)
    taps = basis_taps.astype(F32).reshape(-1)
    psf = psf_taps.reshape(-1)
    pin = lambda x: pltpu.with_memory_space_constraint(x, pltpu.HBM)
    small = (*map(pin, (coef_table, coef_pick, block_visit, visit_weight, patch_place)), taps)

    *parcels, own_image = match(False, *small, pin(ccd_image.reshape(2, BLOCK, BLOCK)))
    ahead = first_stage(parcels)
    taps_var, own_image = lax.optimization_barrier((taps, own_image))
    *parcels_var, own_var = match(True, *small[:-1], taps_var, pin(ccd_variance.reshape(2, BLOCK, BLOCK)))
    behind = first_stage(parcels_var)
    base_var = own_sum("own_var", place, own_var)
    *ahead, base_var = lax.optimization_barrier((*ahead, base_var))
    arrived = second_stage(parcels, *ahead)
    *behind, east, west = lax.optimization_barrier((*behind, *arrived[2:]))
    arrived_var = second_stage(parcels_var, *behind)
    tile, *rims = gather(True, place, own_image, *arrived[:2], east, west)
    tile_var, up, down, first, last = gather(False, place, base_var, *arrived_var, rims)
    rows = swap(up, "trow", False), swap(down, "trow", True)
    sides = turn(first, last, *rows)
    significance = detect(psf, pin(tile), tile_var, *rows, swap(sides[0], "tcol", False), swap(sides[1], "tcol", True))
    return tile, significance


def solution(mesh):
    place = P("trow", "tcol", None)
    blocks = P("trow", "tcol", None, None, None)
    in_specs = (blocks, blocks, P(), P(), place, place, P(), place, P())
    out_specs = (P("trow", "tcol"), P("trow", "tcol"))
    return jax.shard_map(shards, mesh=mesh, in_specs=in_specs, out_specs=out_specs, check_vma=False)
```

```python
import functools
import jax
import jax.numpy as jnp
from jax import lax
from jax.experimental import pallas as pl
from jax.experimental.pallas import tpu as pltpu
from jax.sharding import PartitionSpec as P

F32 = jnp.float32
BF16 = jnp.bfloat16
BLOCK = 512
PATCH = 128
TAPS = 21
RADIUS = 10
PSF = 31
REACH = 15
NBASIS = 6
NP = 32
CAP = 4
GROUP = CAP * PATCH + 16
TILE = 1024
RIM = 16
STEP = 208
MIB = 1 << 20

HBM = pl.BlockSpec(memory_space=pltpu.HBM)
VMEM = pl.BlockSpec(memory_space=pltpu.VMEM)
SMEM = functools.partial(pl.BlockSpec, memory_space=pltpu.SMEM)


def iotas(shape):
    return (lax.broadcasted_iota(jnp.int32, shape, 0), lax.broadcasted_iota(jnp.int32, shape, 1))


def dot(a, b):
    return jnp.dot(a, b, preferred_element_type=F32)


def split(x):
    high = x.astype(BF16)
    return high, (x - high.astype(F32)).astype(BF16)


def diagonals(read, count, first, step, lanes):
    rows, cols = iotas((16, lanes))
    offset = (cols - rows) & (lanes - 1)
    out = jnp.zeros((16, lanes), F32)
    for t in range(count):
        out = jnp.where(offset == (first + step * t) % lanes, read(t), out)
    return out


def toeplitz(base, m, low, high):
    lanes = base.shape[1]
    turned = pltpu.roll(base, (16 * m) % lanes, 1) if (16 * m) % lanes else base
    rows, cols = iotas(base.shape)
    offset = cols - rows - 16 * m
    return jnp.where((offset >= low) & (offset <= high), turned, 0.0)


def corner(read, count, reach):
    rows, cols = iotas((32, 128))
    left = rows < 16
    tap = rows + 112 - cols + reach - jnp.where(left, 128, 0)
    tap = jnp.where(left == (cols < 64), tap, -1)
    out = jnp.zeros((32, 128), F32)
    for t in range(count):
        out = jnp.where(tap == t, read(t), out)
    return out


def via(d):
    vertical = ((d * 11) >> 5) - 1
    sideways = d - 3 * ((d * 11) >> 5) - 1
    vertical = jnp.where((lax.axis_index("trow") & 1) == 0, -vertical, vertical)
    sideways = jnp.where((lax.axis_index("tcol") & 1) == 0, -sideways, sideways)
    return 3 * vertical + sideways + 4


def match_kernel(
    squared, table_in, pick_in, visit_in, weight_in, place_in, taps, x_in,
    up_ref, down_ref, left_ref, right_ref, own_ref,
    across, edges, down, rows_ref, total, leaving, count, slot, slots,
    table, pick, visit, weight, place, x_ref, sems, x_sem,
):
    small = [(table_in, table), (pick_in, pick), (visit_in, visit), (weight_in, weight), (place_in, place)]
    small = [pltpu.make_async_copy(a, b, sems.at[i]) for i, (a, b) in enumerate(small)]
    pixels = [pltpu.make_async_copy(x_in.at[b], x_ref.at[b], x_sem.at[b]) for b in range(2)]
    for copy in small + pixels:
        copy.start()

    def read(k, axis):
        return lambda t: taps[(2 * k + axis) * TAPS + t]

    def kept(x):
        return (x * x if squared else x).astype(BF16)

    def build(k):
        base = diagonals(read(k, 0), TAPS, RADIUS, -1, 256)
        for m in range(16):
            across[k, pl.ds(16 * m, 16), :] = kept(toeplitz(base, m, -RADIUS, RADIUS))
        edges[k // 2, pl.ds(112, 32), pl.ds(k % 2 * 128, 128)] = kept(corner(read(k, 0), TAPS, RADIUS))
        base = diagonals(read(k, 1), TAPS, -26, 1, 256)
        for m in range(18):
            down[k, pl.ds(16 * m, 16), :] = kept(toeplitz(base, m, -26, -6))

    for g in range(9):
        count[g] = 0
    for s in range(8 * CAP):
        slots[s] = -1
    edges[...] = jnp.zeros(edges.shape, BF16)
    for k in range(NBASIS // 2):
        build(k)
    for copy in small:
        copy.wait()
    for n in range(NP):
        entry = place[0, 0, n]
        d = via(entry >> 6)
        r = count[d]
        count[d] = r + 1
        s = jnp.where(d == 4, 8 * CAP, jnp.where(d > 4, d - 1, d) * CAP + r)
        slot[n] = s
        slots[s] = entry & 63
    for k in range(NBASIS // 2, NBASIS):
        build(k)
    _, lanes = iotas((16, 128))
    parcels = [(up_ref, 0), (up_ref, 1), (up_ref, 2), (left_ref, 0), (right_ref, 0), (down_ref, 0), (down_ref, 1), (down_ref, 2)]
    for g, (ref, at) in enumerate(parcels):
        line = jnp.full((16, 128), -1.0, F32)
        for s in range(CAP):
            line = jnp.where(lanes == s, slots[g * CAP + s].astype(F32), line)
        ref[at, pl.ds(CAP * PATCH, 16), :] = line.astype(BF16)

    def one(block, _):
        pltpu.make_async_copy(x_in.at[block], x_ref.at[block], x_sem.at[block]).wait()
        lanes = lax.broadcasted_iota(jnp.int32, (BLOCK, 128), 1)
        for pair in range(NBASIS // 2):
            fix = dot(x_ref[block, :, 128:384], edges[pair])
            for half in range(2):
                k = 2 * pair + half
                part = fix[:, 128 * half : 128 * half + 128]
                first = dot(x_ref[block, :, :256], across[k])
                rows_ref[k, :, 0:128] = first[:, :128].astype(BF16)
                rows_ref[k, :, 128:256] = (first[:, 128:] + jnp.where(lanes >= 64, part, 0.0)).astype(BF16)
                second = dot(x_ref[block, :, 256:], across[k])
                rows_ref[k, :, 256:384] = (second[:, :128] + jnp.where(lanes < 64, part, 0.0)).astype(BF16)
                rows_ref[k, :, 384:512] = second[:, 128:].astype(BF16)
        scale = weight[visit[0, 0, block]].astype(F32)
        if squared:
            scale = scale * scale
        for side in range(2):
            span = pl.ds(256 * side, 256)
            for k in range(NBASIS):
                coef = table[pick[0, 0, block], k]
                if squared:
                    coef = coef * coef
                top = dot(down[k, 16:288, :], rows_ref[k, 0:256, span])
                low = dot(down[k, 0:272, :], rows_ref[k, 256:512, span])
                middle = top[240:] + low[:32]
                if k == 0:
                    total[0:240, span] = coef * top[:240]
                    total[240:272, span] = coef * middle
                    total[272:512, span] = coef * low[32:]
                else:
                    total[0:240, span] += coef * top[:240]
                    total[240:272, span] += coef * middle
                    total[272:512, span] += coef * low[32:]
        for i in range(4):
            for j in range(4):
                n = block * 16 + 4 * i + j
                square = (scale * total[128 * i : 128 * i + 128, 128 * j : 128 * j + 128]).astype(BF16)
                own_ref[n] = square
                leaving[slot[n]] = square

    lax.fori_loop(0, 2, one, None)
    for g, (ref, at) in enumerate(parcels):
        for s in range(CAP):
            ref[at, pl.ds(s * PATCH, PATCH), :] = leaving[g * CAP + s]


def match(squared, table, pick, visit, weight, place, taps, blocks):
    shapes = ((3, GROUP, 128), (3, GROUP, 128), (1, GROUP, 128), (1, GROUP, 128), (NP, PATCH, PATCH))
    return pl.pallas_call(
        functools.partial(match_kernel, squared),
        in_specs=[HBM] * 5 + [SMEM(), HBM],
        out_specs=[VMEM] * 5,
        out_shape=[jax.ShapeDtypeStruct(s, BF16) for s in shapes],
        scratch_shapes=[
            pltpu.VMEM((NBASIS, 256, 256), BF16),
            pltpu.VMEM((NBASIS // 2, 256, 256), BF16),
            pltpu.VMEM((NBASIS, 288, 256), BF16),
            pltpu.VMEM((NBASIS, BLOCK, BLOCK), BF16),
            pltpu.VMEM((BLOCK, BLOCK), F32),
            pltpu.VMEM((8 * CAP + 1, PATCH, PATCH), BF16),
            pltpu.SMEM((9,), jnp.int32),
            pltpu.SMEM((NP,), jnp.int32),
            pltpu.SMEM((8 * CAP + 1,), jnp.int32),
            pltpu.SMEM(table.shape, F32),
            pltpu.SMEM(pick.shape, jnp.int32),
            pltpu.SMEM(visit.shape, jnp.int32),
            pltpu.SMEM(weight.shape, jnp.int32),
            pltpu.SMEM(place.shape, jnp.int32),
            pltpu.VMEM((2, BLOCK, BLOCK), BF16),
            pltpu.SemaphoreType.DMA((5,)),
            pltpu.SemaphoreType.DMA((2,)),
        ],
        compiler_params=pltpu.CompilerParams(vmem_limit_bytes=24 * MIB),
        name="match_var" if squared else "match_img",
    )(table, pick, visit, weight, place, taps, blocks)


def swap(value, axis, odd):
    rows, cols = lax.axis_size("trow"), lax.axis_size("tcol")
    pairs = []
    for r in range(rows):
        for c in range(cols):
            at, count = (r, rows) if axis == "trow" else (c, cols)
            to = ((at + 1) ^ 1) - 1 if odd else at ^ 1
            if axis == "trow":
                target = (to, c) if 0 <= to < count else (r, c ^ 1)
            else:
                target = (r, to) if 0 <= to < count else (r ^ 1, c)
            pairs.append((r * cols + c, target[0] * cols + target[1]))
    return lax.ppermute(value, ("trow", "tcol"), pairs)


def first_stage(parcels):
    return swap(parcels[0], "trow", False), swap(parcels[1], "trow", True)


def second_stage(parcels, below, above):
    _, _, left, right = parcels
    leftward = jnp.concatenate([left, below[0:1], above[0:1]], 0)
    rightward = jnp.concatenate([right, below[2:3], above[2:3]], 0)
    return below, above, swap(leftward, "tcol", False), swap(rightward, "tcol", True)


def pack(read, first):
    lanes = lax.broadcasted_iota(jnp.int32, (128, 128), 1)
    out = jnp.zeros((128, 128), F32)
    for g in range(8):
        rows = read(pl.ds(128 * g, 128))
        rows = jnp.where(lanes < RIM if first else lanes >= 128 - RIM, rows, 0.0)
        turn = RIM * g if first else (RIM * g + RIM) % 128
        out = out + (pltpu.roll(rows, turn, 1) if turn else rows)
    return out


def add(tile_ref, spot, square):
    rows = pl.ds(pl.multiple_of((spot >> 3) * PATCH, PATCH), PATCH)
    cols = pl.ds(pl.multiple_of((spot & 7) * PATCH, PATCH), PATCH)
    tile_ref[rows, cols] += square.astype(F32)


def add_own(place, own_ref, tile_ref):
    tile_ref[...] = jnp.zeros(tile_ref.shape, F32)

    def own(n, _):
        entry = place[n]

        @pl.when((entry >> 6) == 4)
        def _():
            add(tile_ref, entry & 63, own_ref[n])

    lax.fori_loop(0, NP, own, None)


def own_sum(name, place, own):
    return pl.pallas_call(
        add_own,
        in_specs=[SMEM(), VMEM],
        out_specs=VMEM,
        out_shape=jax.ShapeDtypeStruct((TILE, TILE), F32),
        compiler_params=pltpu.CompilerParams(vmem_limit_bytes=12 * MIB),
        name=name,
    )(place, own)


def gather_kernel(image, place, start_ref, below_ref, above_ref, east_ref, west_ref, *rest):
    if image:
        tile_ref, up_ref, down_ref, first_ref, last_ref, lines, spots, sem = rest
    else:
        up_in, down_in, first_in, last_in, out_ref, up_ref, down_ref, first_ref, last_ref, lines, spots, sem, tile_ref = rest
    groups = [(below_ref, 1), (above_ref, 1)] + [(east_ref, g) for g in range(3)] + [(west_ref, g) for g in range(3)]
    for g, (ref, at) in enumerate(groups):
        lines[pl.ds(g, 1), :] = ref[at, CAP * PATCH :, :].astype(F32)[0:1].astype(jnp.int32)
    copy = pltpu.make_async_copy(lines, spots, sem)
    copy.start()
    if image:
        add_own(place, start_ref, tile_ref)
    else:
        tile_ref[...] = start_ref[...]
    copy.wait()
    for g, (ref, at) in enumerate(groups):
        for s in range(CAP):
            spot = spots[g, s]

            @pl.when(spot >= 0)
            def _():
                add(tile_ref, spot, ref[at, s * PATCH : (s + 1) * PATCH, :])

    first = pack(lambda rows: tile_ref[rows, :128], True)
    last = pack(lambda rows: tile_ref[rows, TILE - 128 :], False)
    even = (lax.axis_index("trow") & 1) == 0
    ends = [tile_ref[pl.ds(pl.multiple_of(jnp.where(even, a, TILE - RIM - a), RIM), RIM), :] for a in (TILE - RIM, 0)]
    if image:
        for ref, value, n in ((up_ref, ends[0], RIM), (down_ref, ends[1], RIM), (first_ref, first, 128), (last_ref, last, 128)):
            ref[pl.ds(0, n), :], ref[pl.ds(n, n), :] = split(value)
    else:
        out_ref[...] = tile_ref[...].astype(BF16)
        for ref, old, value, n in (
            (up_ref, up_in, ends[0], RIM), (down_ref, down_in, ends[1], RIM),
            (first_ref, first_in, first, 128), (last_ref, last_in, last, 128),
        ):
            ref[pl.ds(0, 2 * n), :] = old[...]
            ref[pl.ds(2 * n, n), :] = value.astype(BF16)


def gather(image, place, start, below, above, east, west, rims=()):
    count = 2 if image else 3
    shapes = [(TILE, TILE), (count * RIM, TILE), (count * RIM, TILE), (count * 128, 128), (count * 128, 128)]
    return pl.pallas_call(
        functools.partial(gather_kernel, image),
        in_specs=[SMEM()] + [VMEM] * (5 + len(rims)),
        out_specs=[VMEM] * len(shapes),
        out_shape=[jax.ShapeDtypeStruct(s, F32 if image and i == 0 else BF16) for i, s in enumerate(shapes)],
        scratch_shapes=[pltpu.VMEM((8, 128), jnp.int32), pltpu.SMEM((8, 128), jnp.int32), pltpu.SemaphoreType.DMA]
        + ([] if image else [pltpu.VMEM((TILE, TILE), F32)]),
        compiler_params=pltpu.CompilerParams(vmem_limit_bytes=20 * MIB),
        name="gather_img" if image else "gather_var",
    )(place, start, below, above, east, west, *rims)


def choose(first, a, b):
    return jnp.where(first, a.astype(F32), b.astype(F32))


def turn_kernel(first_ref, last_ref, even_first, odd_first, even_last, odd_last, even_out, odd_out):
    here, count = lax.axis_index("trow"), lax.axis_size("trow")
    row_odd, col_odd = (here & 1) == 1, (lax.axis_index("tcol") & 1) == 1
    for out, flip in ((even_out, col_odd), (odd_out, jnp.logical_not(col_odd))):
        out[pl.ds(0, 384), :] = choose(flip, first_ref[...], last_ref[...]).astype(BF16)
        met = [choose(flip, a[...], b[...]) for a, b in ((even_first, even_last), (odd_first, odd_last))]
        out[pl.ds(384, 48), :] = jnp.where(here > 0, choose(row_odd, *met), 0.0).astype(BF16)
        out[pl.ds(432, 48), :] = jnp.where(here < count - 1, choose(row_odd, *met[::-1]), 0.0).astype(BF16)


def turn(first, last, even, odd):
    whole = pl.BlockSpec((384, 128), lambda i: (0, 0))
    near = pl.BlockSpec((48, 128), lambda i: (0, 0))
    far = pl.BlockSpec((48, 128), lambda i: (0, 7))
    return pl.pallas_call(
        turn_kernel,
        grid=(1,),
        in_specs=[whole, whole, near, near, far, far],
        out_specs=[pl.BlockSpec((480, 128), lambda i: (0, 0))] * 2,
        out_shape=[jax.ShapeDtypeStruct((480, 128), BF16)] * 2,
        compiler_params=pltpu.CompilerParams(vmem_limit_bytes=8 * MIB),
        name="turn",
    )(first, last, even, odd, even, odd)


def tap(psf, axis):
    return lambda t: psf[axis * PSF + t]


def largest(psf, axis):
    peak = psf[axis * PSF]
    for t in range(1, PSF):
        peak = jnp.maximum(peak, psf[axis * PSF + t])
    return peak


def column_bands(psf, bands):
    column = diagonals(tap(psf, 1), PSF, 1, 1, 256) / jnp.full((16, 256), largest(psf, 1), F32)
    for squared in range(2):
        for m in range(STEP // 16):
            bands[squared, pl.ds(16 * m, 16), :] = toeplitz(column, m, 1, PSF).astype(BF16)
        column = column * column


def column_kernel(psf, tile_ref, var_ref, v_high, v_low, v_var, img_in, high, low, var, bands, in_sems):
    copies = []
    for q in range(4):
        rows = pl.ds(256 * q, 256)
        inside = pl.ds(256 * q + RIM, 256)
        copies.append((
            pltpu.make_async_copy(tile_ref.at[rows, :], img_in.at[rows, :], in_sems.at[2 * q]),
            pltpu.make_async_copy(var_ref.at[rows, :], var.at[inside, :], in_sems.at[2 * q + 1]),
        ))
    for pair in copies:
        for copy in pair:
            copy.start()
    column_bands(psf, bands)
    for ref in (high, low, var):
        ref[pl.ds(0, RIM), :] = jnp.zeros((RIM, TILE), BF16)
        ref[pl.ds(RIM + TILE, 3 * RIM), :] = jnp.zeros((3 * RIM, TILE), BF16)
    ready = 0
    for t in range(5):
        count = min(STEP, TILE - STEP * t)
        while ready < 4 and 256 * ready < STEP * t + 240:
            for copy in copies[ready]:
                copy.wait()
            high[pl.ds(RIM + 256 * ready, 256), :], low[pl.ds(RIM + 256 * ready, 256), :] = split(img_in[pl.ds(256 * ready, 256), :])
            ready += 1
        window = pl.ds(STEP * t, 256)
        target = pl.ds(STEP * t, count)
        for c in range(4):
            span = pl.ds(256 * c, 256)
            value = dot(bands[0], high[window, span]) + dot(bands[0], low[window, span])
            v_high[target, span], v_low[target, span] = split(value[:count])
            v_var[target, span] = dot(bands[1], var[window, span])[:count].astype(BF16)


def column_pass(psf, tile, tile_var):
    return pl.pallas_call(
        column_kernel,
        in_specs=[SMEM(), HBM, HBM],
        out_specs=[VMEM] * 3,
        out_shape=[jax.ShapeDtypeStruct((TILE, TILE), BF16)] * 3,
        scratch_shapes=[pltpu.VMEM((TILE, TILE), F32)]
        + [pltpu.VMEM((1088, TILE), BF16)] * 3
        + [pltpu.VMEM((2, STEP, 256), BF16), pltpu.SemaphoreType.DMA((8,))],
        compiler_params=pltpu.CompilerParams(vmem_limit_bytes=22 * MIB),
        name="column",
    )(psf, tile, tile_var)


def filter_kernel(
    psf, tile_ref, var_ref, v_high, v_low, v_var, row_even, row_odd, col_even, col_odd, out_ref,
    img_in, var_in, frame, sides, bands, flats, ends, v_rim, v_side, out, in_sems, out_sems,
):
    row, rows_n = lax.axis_index("trow"), lax.axis_size("trow")
    col, cols_n = lax.axis_index("tcol"), lax.axis_size("tcol")
    copies = []
    for i, start in enumerate((0, TILE - 2 * RIM)):
        rows = pl.ds(start, 2 * RIM)
        copies.append(pltpu.make_async_copy(tile_ref.at[rows, :], img_in.at[i], in_sems.at[2 * i]))
        copies.append(pltpu.make_async_copy(var_ref.at[rows, :], var_in.at[i], in_sems.at[2 * i + 1]))
    for copy in copies:
        copy.start()
    scale = largest(psf, 0) * largest(psf, 1)
    column_bands(psf, bands)
    over = 1.0 / jnp.full((16, 256), largest(psf, 0), F32)
    flat = diagonals(tap(psf, 0), PSF, REACH, -1, 256) * over
    edge = corner(tap(psf, 0), PSF, REACH) * over[0:1, :128]
    ends[...] = jnp.zeros(ends.shape, BF16)
    for squared in range(2):
        for m in range(16):
            flats[squared, pl.ds(16 * m, 16), :] = toeplitz(flat, m, -REACH, REACH).astype(BF16)
        for part in range(2):
            span = pl.ds(128 * part, 128)
            ends[squared, pl.ds(128 * part, 16), span] = edge[16:].astype(BF16)
            ends[squared, pl.ds(128 * part + 112, 16), span] = edge[:16].astype(BF16)
        flat, edge = flat * flat, edge * edge

    def met(along, at, start, rows):
        even, odd = (row_even, row_odd) if along is row else (col_even, col_odd)
        parts = even[start : start + rows, :], odd[start : start + rows, :]
        return choose((along & 1) == 1, *(parts[::-1] if at else parts))

    lanes = lax.broadcasted_iota(jnp.int32, (128, 128), 1)
    at_west, at_east = (lanes >= 128 - RIM) & (col > 0), (lanes < RIM) & (col < cols_n - 1)
    for i in range(3):
        sides[i, pl.ds(2 * RIM + TILE, 2 * RIM), :] = jnp.zeros((2 * RIM, 128), BF16)
        west, east = met(col, 0, 128 * i, 128), met(col, 1, 128 * i, 128)
        for g in range(8):
            near = pltpu.roll(east, 128 - RIM * g, 1) if g else east
            far = pltpu.roll(west, (112 - RIM * g) % 128, 1) if g != 7 else west
            sides[i, pl.ds(RIM + 128 * g, 128), :] = jnp.where(at_east, near, jnp.where(at_west, far, 0.0)).astype(BF16)
        for at, start in ((0, 384), (RIM + TILE, 432)):
            near, far = met(col, 1, start + RIM * i, RIM), met(col, 0, start + RIM * i, RIM)
            sides[i, pl.ds(at, RIM), :] = jnp.where(at_east[:RIM], near, jnp.where(at_west[:RIM], far, 0.0)).astype(BF16)
    for t in range(5):
        count = min(STEP, TILE - STEP * t)
        window = pl.ds(STEP * t, 256)
        target = pl.ds(STEP * t, count)
        value = dot(bands[0], sides[0, window, :]) + dot(bands[0], sides[1, window, :])
        v_side[0, target, :], v_side[1, target, :] = split(value[:count])
        v_side[2, target, :] = dot(bands[1], sides[2, window, :])[:count].astype(BF16)
    for copy in copies:
        copy.wait()
    for i in range(2):
        mine, theirs = (pl.ds(RIM, 2 * RIM), pl.ds(0, RIM)) if i == 0 else (pl.ds(0, 2 * RIM), pl.ds(2 * RIM, RIM))
        frame[0, mine, :], frame[1, mine, :] = split(img_in[i])
        frame[2, mine, :] = var_in[i]
        inside = row < rows_n - 1 if i else row > 0
        for j in range(3):
            frame[j, theirs, :] = jnp.where(inside, met(row, i, RIM * j, RIM), 0.0).astype(BF16)
            frame[j, pl.ds(3 * RIM, RIM), :] = jnp.zeros((RIM, TILE), BF16)
        value = dot(bands[0, :RIM, 0:64], frame[0]) + dot(bands[0, :RIM, 0:64], frame[1])
        v_rim[0, i], v_rim[1, i] = split(value)
        v_rim[2, i] = dot(bands[1, :RIM, 0:64], frame[2]).astype(BF16)

    columns = (v_high, v_low, v_var)

    def read(i, q, start, width):
        span = pl.ds(start, width)
        if q == 0:
            return jnp.concatenate([v_rim[i, 0, :, span], columns[i][RIM:256, span]], 0)
        if q == 3:
            return jnp.concatenate([columns[i][768 : TILE - RIM, span], v_rim[i, 1, :, span]], 0)
        return columns[i][256 * q : 256 * q + 256, span]

    near = lax.broadcasted_iota(jnp.int32, (256, 128), 1) < 64
    for q in range(4):
        rows = pl.ds(256 * q, 256)
        results = []
        for squared, parts in ((0, (0, 1)), (1, (2,))):
            def about(i, w):
                if w == 0:
                    return v_side[i, rows, :]
                return jnp.where(near, read(i, q, 256 * w, 128), read(i, q, 256 * w - 128, 128))

            fixes = []
            for w in (0, 2):
                both = sum(dot(jnp.concatenate([about(i, w), about(i, w + 1)], 1), ends[squared]) for i in parts)
                fixes += [both[:, :128], both[:, 128:]]
            fixes.append(fixes[0])
            values = []
            for c in range(4):
                main = sum(dot(read(i, q, 256 * c, 256), flats[squared]) for i in parts)
                values.append(main[:, :128] + jnp.where(near, fixes[c], 0.0))
                values.append(main[:, 128:] + jnp.where(near, 0.0, fixes[c + 1]))
            results.append(values)
        for c in range(8):
            out[rows, pl.ds(128 * c, 128)] = scale * results[0][c] * lax.rsqrt(scale * scale * results[1][c] + 1.0)
        pltpu.make_async_copy(out.at[rows, :], out_ref.at[rows, :], out_sems.at[q]).start()
    for q in range(4):
        rows = pl.ds(256 * q, 256)
        pltpu.make_async_copy(out.at[rows, :], out_ref.at[rows, :], out_sems.at[q]).wait()


def detect(psf, tile, tile_var, columns, *rims):
    return pl.pallas_call(
        filter_kernel,
        in_specs=[SMEM(), HBM, HBM] + [VMEM] * 7,
        out_specs=HBM,
        out_shape=jax.ShapeDtypeStruct((TILE, TILE), F32),
        scratch_shapes=[
            pltpu.VMEM((2, 2 * RIM, TILE), F32),
            pltpu.VMEM((2, 2 * RIM, TILE), BF16),
            pltpu.VMEM((3, 4 * RIM, TILE), BF16),
            pltpu.VMEM((3, 1088, 128), BF16),
            pltpu.VMEM((2, STEP, 256), BF16),
            pltpu.VMEM((2, 256, 256), BF16),
            pltpu.VMEM((2, 256, 256), BF16),
            pltpu.VMEM((3, 2, RIM, TILE), BF16),
            pltpu.VMEM((3, TILE, 128), BF16),
            pltpu.VMEM((TILE, TILE), F32),
            pltpu.SemaphoreType.DMA((4,)),
            pltpu.SemaphoreType.DMA((4,)),
        ],
        compiler_params=pltpu.CompilerParams(vmem_limit_bytes=24 * MIB),
        name="filter",
    )(psf, tile, tile_var, *columns, *rims)


def shards(ccd_image, ccd_variance, basis_taps, coef_table, coef_pick, block_visit, visit_weight, patch_place, psf_taps):
    place = patch_place.reshape(NP)
    taps = basis_taps.astype(F32).reshape(-1)
    psf = psf_taps.reshape(-1)
    pin = lambda x: pltpu.with_memory_space_constraint(x, pltpu.HBM)
    small = (*map(pin, (coef_table, coef_pick, block_visit, visit_weight, patch_place)), taps)

    *parcels, own_image = match(False, *small, pin(ccd_image.reshape(2, BLOCK, BLOCK)))
    ahead = first_stage(parcels)
    taps_var, own_image = lax.optimization_barrier((taps, own_image))
    *parcels_var, own_var = match(True, *small[:-1], taps_var, pin(ccd_variance.reshape(2, BLOCK, BLOCK)))
    behind = first_stage(parcels_var)
    base_var = own_sum("own_var", place, own_var)
    *ahead, base_var = lax.optimization_barrier((*ahead, base_var))
    arrived = second_stage(parcels, *ahead)
    *behind, east, west = lax.optimization_barrier((*behind, *arrived[2:]))
    arrived_var = second_stage(parcels_var, *behind)
    tile, *rims = gather(True, place, own_image, *arrived[:2], east, west)
    tile_var, up, down, first, last = gather(False, place, base_var, *arrived_var, rims)
    rows = swap(up, "trow", False), swap(down, "trow", True)
    tile_read = pin(tile)
    columns = list(column_pass(psf, tile_read, tile_var))
    *rows, columns[0] = lax.optimization_barrier((*rows, columns[0]))
    sides = turn(first, last, *rows)
    significance = detect(psf, tile_read, tile_var, columns, *rows, swap(sides[0], "tcol", False), swap(sides[1], "tcol", True))
    return tile, significance


def solution(mesh):
    place = P("trow", "tcol", None)
    blocks = P("trow", "tcol", None, None, None)
    in_specs = (blocks, blocks, P(), P(), place, place, P(), place, P())
    out_specs = (P("trow", "tcol"), P("trow", "tcol"))
    return jax.shard_map(shards, mesh=mesh, in_specs=in_specs, out_specs=out_specs, check_vma=False)
```

```python
import functools
import jax
import jax.numpy as jnp
from jax import lax
from jax.experimental import pallas as pl
from jax.experimental.pallas import tpu as pltpu
from jax.sharding import PartitionSpec as P

F32 = jnp.float32
BF16 = jnp.bfloat16
BLOCK = 512
PATCH = 128
TAPS = 21
RADIUS = 10
PSF = 31
REACH = 15
NBASIS = 6
NP = 32
CAP = 4
GROUP = CAP * PATCH + 16
TILE = 1024
RIM = 16
STEP = 208
MIB = 1 << 20

HBM = pl.BlockSpec(memory_space=pltpu.HBM)
VMEM = pl.BlockSpec(memory_space=pltpu.VMEM)
SMEM = functools.partial(pl.BlockSpec, memory_space=pltpu.SMEM)


def iotas(shape):
    return (lax.broadcasted_iota(jnp.int32, shape, 0), lax.broadcasted_iota(jnp.int32, shape, 1))


def dot(a, b):
    return jnp.dot(a, b, preferred_element_type=F32)


def split(x):
    high = x.astype(BF16)
    return high, (x - high.astype(F32)).astype(BF16)


def diagonals(read, count, first, step, lanes):
    rows, cols = iotas((16, lanes))
    offset = (cols - rows) & (lanes - 1)
    out = jnp.zeros((16, lanes), F32)
    for t in range(count):
        out = jnp.where(offset == (first + step * t) % lanes, read(t), out)
    return out


def toeplitz(base, m, low, high):
    lanes = base.shape[1]
    turned = pltpu.roll(base, (16 * m) % lanes, 1) if (16 * m) % lanes else base
    rows, cols = iotas(base.shape)
    offset = cols - rows - 16 * m
    return jnp.where((offset >= low) & (offset <= high), turned, 0.0)


def corner(read, count, reach):
    rows, cols = iotas((32, 128))
    left = rows < 16
    tap = rows + 112 - cols + reach - jnp.where(left, 128, 0)
    tap = jnp.where(left == (cols < 64), tap, -1)
    out = jnp.zeros((32, 128), F32)
    for t in range(count):
        out = jnp.where(tap == t, read(t), out)
    return out


def via(d):
    vertical = ((d * 11) >> 5) - 1
    sideways = d - 3 * ((d * 11) >> 5) - 1
    vertical = jnp.where((lax.axis_index("trow") & 1) == 0, -vertical, vertical)
    sideways = jnp.where((lax.axis_index("tcol") & 1) == 0, -sideways, sideways)
    return 3 * vertical + sideways + 4


def match_kernel(
    squared, table_in, pick_in, visit_in, weight_in, place_in, taps, x_in,
    up_ref, down_ref, left_ref, right_ref, own_ref,
    across, edges, down, rows_ref, total, leaving, count, slot, slots,
    table, pick, visit, weight, place, x_ref, sems, x_sem,
):
    small = [(table_in, table), (pick_in, pick), (visit_in, visit), (weight_in, weight), (place_in, place)]
    small = [pltpu.make_async_copy(a, b, sems.at[i]) for i, (a, b) in enumerate(small)]
    pixels = [pltpu.make_async_copy(x_in.at[b], x_ref.at[b], x_sem.at[b]) for b in range(2)]
    for copy in small + pixels:
        copy.start()

    def read(k, axis):
        return lambda t: taps[(2 * k + axis) * TAPS + t]

    def kept(x):
        return (x * x if squared else x).astype(BF16)

    def build(k):
        base = diagonals(read(k, 0), TAPS, RADIUS, -1, 256)
        for m in range(16):
            across[k, pl.ds(16 * m, 16), :] = kept(toeplitz(base, m, -RADIUS, RADIUS))
        edges[k // 2, pl.ds(112, 32), pl.ds(k % 2 * 128, 128)] = kept(corner(read(k, 0), TAPS, RADIUS))
        base = diagonals(read(k, 1), TAPS, -26, 1, 256)
        for m in range(18):
            down[k, pl.ds(16 * m, 16), :] = kept(toeplitz(base, m, -26, -6))

    for g in range(9):
        count[g] = 0
    for s in range(8 * CAP):
        slots[s] = -1
    edges[...] = jnp.zeros(edges.shape, BF16)
    for k in range(NBASIS // 2):
        build(k)
    for copy in small:
        copy.wait()
    for n in range(NP):
        entry = place[0, 0, n]
        d = via(entry >> 6)
        r = count[d]
        count[d] = r + 1
        s = jnp.where(d == 4, 8 * CAP, jnp.where(d > 4, d - 1, d) * CAP + r)
        slot[n] = s
        slots[s] = entry & 63
    for k in range(NBASIS // 2, NBASIS):
        build(k)
    _, lanes = iotas((16, 128))
    parcels = [(up_ref, 0), (up_ref, 1), (up_ref, 2), (left_ref, 0), (right_ref, 0), (down_ref, 0), (down_ref, 1), (down_ref, 2)]
    for g, (ref, at) in enumerate(parcels):
        line = jnp.full((16, 128), -1.0, F32)
        for s in range(CAP):
            line = jnp.where(lanes == s, slots[g * CAP + s].astype(F32), line)
        ref[at, pl.ds(CAP * PATCH, 16), :] = line.astype(BF16)

    def one(block, _):
        pltpu.make_async_copy(x_in.at[block], x_ref.at[block], x_sem.at[block]).wait()
        lanes = lax.broadcasted_iota(jnp.int32, (BLOCK, 128), 1)
        for pair in range(NBASIS // 2):
            fix = dot(x_ref[block, :, 128:384], edges[pair])
            for half in range(2):
                k = 2 * pair + half
                part = fix[:, 128 * half : 128 * half + 128]
                first = dot(x_ref[block, :, :256], across[k])
                rows_ref[k, :, 0:128] = first[:, :128].astype(BF16)
                rows_ref[k, :, 128:256] = (first[:, 128:] + jnp.where(lanes >= 64, part, 0.0)).astype(BF16)
                second = dot(x_ref[block, :, 256:], across[k])
                rows_ref[k, :, 256:384] = (second[:, :128] + jnp.where(lanes < 64, part, 0.0)).astype(BF16)
                rows_ref[k, :, 384:512] = second[:, 128:].astype(BF16)
        scale = weight[visit[0, 0, block]].astype(F32)
        if squared:
            scale = scale * scale
        for side in range(2):
            span = pl.ds(256 * side, 256)
            for k in range(NBASIS):
                coef = table[pick[0, 0, block], k]
                if squared:
                    coef = coef * coef
                top = dot(down[k, 16:288, :], rows_ref[k, 0:256, span])
                low = dot(down[k, 0:272, :], rows_ref[k, 256:512, span])
                middle = top[240:] + low[:32]
                if k == 0:
                    total[0:240, span] = coef * top[:240]
                    total[240:272, span] = coef * middle
                    total[272:512, span] = coef * low[32:]
                else:
                    total[0:240, span] += coef * top[:240]
                    total[240:272, span] += coef * middle
                    total[272:512, span] += coef * low[32:]
        for i in range(4):
            for j in range(4):
                n = block * 16 + 4 * i + j
                square = (scale * total[128 * i : 128 * i + 128, 128 * j : 128 * j + 128]).astype(BF16)
                own_ref[n] = square
                leaving[slot[n]] = square

    lax.fori_loop(0, 2, one, None)
    for g, (ref, at) in enumerate(parcels):
        for s in range(CAP):
            ref[at, pl.ds(s * PATCH, PATCH), :] = leaving[g * CAP + s]


def match(squared, table, pick, visit, weight, place, taps, blocks):
    shapes = ((3, GROUP, 128), (3, GROUP, 128), (1, GROUP, 128), (1, GROUP, 128), (NP, PATCH, PATCH))
    return pl.pallas_call(
        functools.partial(match_kernel, squared),
        in_specs=[HBM] * 5 + [SMEM(), HBM],
        out_specs=[VMEM] * 5,
        out_shape=[jax.ShapeDtypeStruct(s, BF16) for s in shapes],
        scratch_shapes=[
            pltpu.VMEM((NBASIS, 256, 256), BF16),
            pltpu.VMEM((NBASIS // 2, 256, 256), BF16),
            pltpu.VMEM((NBASIS, 288, 256), BF16),
            pltpu.VMEM((NBASIS, BLOCK, BLOCK), BF16),
            pltpu.VMEM((BLOCK, BLOCK), F32),
            pltpu.VMEM((8 * CAP + 1, PATCH, PATCH), BF16),
            pltpu.SMEM((9,), jnp.int32),
            pltpu.SMEM((NP,), jnp.int32),
            pltpu.SMEM((8 * CAP + 1,), jnp.int32),
            pltpu.SMEM(table.shape, F32),
            pltpu.SMEM(pick.shape, jnp.int32),
            pltpu.SMEM(visit.shape, jnp.int32),
            pltpu.SMEM(weight.shape, jnp.int32),
            pltpu.SMEM(place.shape, jnp.int32),
            pltpu.VMEM((2, BLOCK, BLOCK), BF16),
            pltpu.SemaphoreType.DMA((5,)),
            pltpu.SemaphoreType.DMA((2,)),
        ],
        compiler_params=pltpu.CompilerParams(vmem_limit_bytes=24 * MIB),
        name="match_var" if squared else "match_img",
    )(table, pick, visit, weight, place, taps, blocks)


def swap(value, axis, odd):
    rows, cols = lax.axis_size("trow"), lax.axis_size("tcol")
    pairs = []
    for r in range(rows):
        for c in range(cols):
            at, count = (r, rows) if axis == "trow" else (c, cols)
            to = ((at + 1) ^ 1) - 1 if odd else at ^ 1
            if axis == "trow":
                target = (to, c) if 0 <= to < count else (r, c ^ 1)
            else:
                target = (r, to) if 0 <= to < count else (r ^ 1, c)
            pairs.append((r * cols + c, target[0] * cols + target[1]))
    return lax.ppermute(value, ("trow", "tcol"), pairs)


def first_stage(parcels):
    return swap(parcels[0], "trow", False), swap(parcels[1], "trow", True)


def second_stage(parcels, below, above):
    _, _, left, right = parcels
    leftward = jnp.concatenate([left, below[0:1], above[0:1]], 0)
    rightward = jnp.concatenate([right, below[2:3], above[2:3]], 0)
    return below, above, swap(leftward, "tcol", False), swap(rightward, "tcol", True)


def pack(read, first):
    lanes = lax.broadcasted_iota(jnp.int32, (128, 128), 1)
    out = jnp.zeros((128, 128), F32)
    for g in range(8):
        rows = read(pl.ds(128 * g, 128))
        rows = jnp.where(lanes < RIM if first else lanes >= 128 - RIM, rows, 0.0)
        turn = RIM * g if first else (RIM * g + RIM) % 128
        out = out + (pltpu.roll(rows, turn, 1) if turn else rows)
    return out


def add(tile_ref, spot, square):
    rows = pl.ds(pl.multiple_of((spot >> 3) * PATCH, PATCH), PATCH)
    cols = pl.ds(pl.multiple_of((spot & 7) * PATCH, PATCH), PATCH)
    tile_ref[rows, cols] += square.astype(F32)


def add_own(place, own_ref, tile_ref):
    tile_ref[...] = jnp.zeros(tile_ref.shape, F32)

    def own(n, _):
        entry = place[n]

        @pl.when((entry >> 6) == 4)
        def _():
            add(tile_ref, entry & 63, own_ref[n])

    lax.fori_loop(0, NP, own, None)


def own_sum(name, place, own):
    return pl.pallas_call(
        add_own,
        in_specs=[SMEM(), VMEM],
        out_specs=VMEM,
        out_shape=jax.ShapeDtypeStruct((TILE, TILE), F32),
        compiler_params=pltpu.CompilerParams(vmem_limit_bytes=12 * MIB),
        name=name,
    )(place, own)


def gather_kernel(image, place, start_ref, below_ref, above_ref, east_ref, west_ref, *rest):
    if image:
        tile_ref, up_ref, down_ref, first_ref, last_ref, lines, spots, sem = rest
    else:
        up_in, down_in, first_in, last_in, out_ref, up_ref, down_ref, first_ref, last_ref, lines, spots, sem, tile_ref = rest
    groups = [(below_ref, 1), (above_ref, 1)] + [(east_ref, g) for g in range(3)] + [(west_ref, g) for g in range(3)]
    for g, (ref, at) in enumerate(groups):
        lines[pl.ds(g, 1), :] = ref[at, CAP * PATCH :, :].astype(F32)[0:1].astype(jnp.int32)
    copy = pltpu.make_async_copy(lines, spots, sem)
    copy.start()
    if image:
        add_own(place, start_ref, tile_ref)
    else:
        tile_ref[...] = start_ref[...]
    copy.wait()
    for g, (ref, at) in enumerate(groups):
        for s in range(CAP):
            spot = spots[g, s]

            @pl.when(spot >= 0)
            def _():
                add(tile_ref, spot, ref[at, s * PATCH : (s + 1) * PATCH, :])

    first = pack(lambda rows: tile_ref[rows, :128], True)
    last = pack(lambda rows: tile_ref[rows, TILE - 128 :], False)
    even = (lax.axis_index("trow") & 1) == 0
    ends = [tile_ref[pl.ds(pl.multiple_of(jnp.where(even, a, TILE - RIM - a), RIM), RIM), :] for a in (TILE - RIM, 0)]
    if image:
        for ref, value, n in ((up_ref, ends[0], RIM), (down_ref, ends[1], RIM), (first_ref, first, 128), (last_ref, last, 128)):
            ref[pl.ds(0, n), :], ref[pl.ds(n, n), :] = split(value)
    else:
        out_ref[...] = tile_ref[...].astype(BF16)
        for ref, old, value, n in (
            (up_ref, up_in, ends[0], RIM), (down_ref, down_in, ends[1], RIM),
            (first_ref, first_in, first, 128), (last_ref, last_in, last, 128),
        ):
            ref[pl.ds(0, 2 * n), :] = old[...]
            ref[pl.ds(2 * n, n), :] = value.astype(BF16)


def gather(image, place, start, below, above, east, west, rims=()):
    count = 2 if image else 3
    shapes = [(TILE, TILE), (count * RIM, TILE), (count * RIM, TILE), (count * 128, 128), (count * 128, 128)]
    return pl.pallas_call(
        functools.partial(gather_kernel, image),
        in_specs=[SMEM()] + [VMEM] * (5 + len(rims)),
        out_specs=[VMEM] * len(shapes),
        out_shape=[jax.ShapeDtypeStruct(s, F32 if image and i == 0 else BF16) for i, s in enumerate(shapes)],
        scratch_shapes=[pltpu.VMEM((8, 128), jnp.int32), pltpu.SMEM((8, 128), jnp.int32), pltpu.SemaphoreType.DMA]
        + ([] if image else [pltpu.VMEM((TILE, TILE), F32)]),
        compiler_params=pltpu.CompilerParams(vmem_limit_bytes=20 * MIB),
        name="gather_img" if image else "gather_var",
    )(place, start, below, above, east, west, *rims)


def choose(first, a, b):
    return jnp.where(first, a.astype(F32), b.astype(F32))


def turn_kernel(first_ref, last_ref, even_first, odd_first, even_last, odd_last, even_out, odd_out):
    here, count = lax.axis_index("trow"), lax.axis_size("trow")
    row_odd, col_odd = (here & 1) == 1, (lax.axis_index("tcol") & 1) == 1
    for out, flip in ((even_out, col_odd), (odd_out, jnp.logical_not(col_odd))):
        out[pl.ds(0, 384), :] = choose(flip, first_ref[...], last_ref[...]).astype(BF16)
        met = [choose(flip, a[...], b[...]) for a, b in ((even_first, even_last), (odd_first, odd_last))]
        out[pl.ds(384, 48), :] = jnp.where(here > 0, choose(row_odd, *met), 0.0).astype(BF16)
        out[pl.ds(432, 48), :] = jnp.where(here < count - 1, choose(row_odd, *met[::-1]), 0.0).astype(BF16)


def turn(first, last, even, odd):
    whole = pl.BlockSpec((384, 128), lambda i: (0, 0))
    near = pl.BlockSpec((48, 128), lambda i: (0, 0))
    far = pl.BlockSpec((48, 128), lambda i: (0, 7))
    return pl.pallas_call(
        turn_kernel,
        grid=(1,),
        in_specs=[whole, whole, near, near, far, far],
        out_specs=[pl.BlockSpec((480, 128), lambda i: (0, 0))] * 2,
        out_shape=[jax.ShapeDtypeStruct((480, 128), BF16)] * 2,
        compiler_params=pltpu.CompilerParams(vmem_limit_bytes=8 * MIB),
        name="turn",
    )(first, last, even, odd, even, odd)


def tap(psf, axis):
    return lambda t: psf[axis * PSF + t]


def largest(psf, axis):
    peak = psf[axis * PSF]
    for t in range(1, PSF):
        peak = jnp.maximum(peak, psf[axis * PSF + t])
    return peak


def column_bands(psf, bands):
    column = diagonals(tap(psf, 1), PSF, 1, 1, 256) / jnp.full((16, 256), largest(psf, 1), F32)
    for squared in range(2):
        for m in range(STEP // 16):
            bands[squared, pl.ds(16 * m, 16), :] = toeplitz(column, m, 1, PSF).astype(BF16)
        column = column * column


def column_kernel(psf, tile_ref, var_ref, v_high, v_low, v_var, img_in, high, low, var, bands, in_sems):
    copies = []
    for q in range(4):
        rows = pl.ds(256 * q, 256)
        inside = pl.ds(256 * q + RIM, 256)
        copies.append((
            pltpu.make_async_copy(tile_ref.at[rows, :], img_in.at[rows, :], in_sems.at[2 * q]),
            pltpu.make_async_copy(var_ref.at[rows, :], var.at[inside, :], in_sems.at[2 * q + 1]),
        ))
    for pair in copies:
        for copy in pair:
            copy.start()
    column_bands(psf, bands)
    for ref in (high, low, var):
        ref[pl.ds(0, RIM), :] = jnp.zeros((RIM, TILE), BF16)
        ref[pl.ds(RIM + TILE, 3 * RIM), :] = jnp.zeros((3 * RIM, TILE), BF16)
    ready = 0
    for t in range(5):
        count = min(STEP, TILE - STEP * t)
        while ready < 4 and 256 * ready < STEP * t + 240:
            for copy in copies[ready]:
                copy.wait()
            high[pl.ds(RIM + 256 * ready, 256), :], low[pl.ds(RIM + 256 * ready, 256), :] = split(img_in[pl.ds(256 * ready, 256), :])
            ready += 1
        window = pl.ds(STEP * t, 256)
        target = pl.ds(STEP * t, count)
        for c in range(4):
            span = pl.ds(256 * c, 256)
            value = dot(bands[0], high[window, span]) + dot(bands[0], low[window, span])
            v_high[target, span], v_low[target, span] = split(value[:count])
            v_var[target, span] = dot(bands[1], var[window, span])[:count].astype(BF16)


def column_pass(psf, tile, tile_var):
    return pl.pallas_call(
        column_kernel,
        in_specs=[SMEM(), HBM, HBM],
        out_specs=[VMEM] * 3,
        out_shape=[jax.ShapeDtypeStruct((TILE, TILE), BF16)] * 3,
        scratch_shapes=[pltpu.VMEM((TILE, TILE), F32)]
        + [pltpu.VMEM((1088, TILE), BF16)] * 3
        + [pltpu.VMEM((2, STEP, 256), BF16), pltpu.SemaphoreType.DMA((8,))],
        compiler_params=pltpu.CompilerParams(vmem_limit_bytes=22 * MIB),
        name="column",
    )(psf, tile, tile_var)


def row_bands(psf, flats, ends):
    over = 1.0 / jnp.full((16, 256), largest(psf, 0), F32)
    flat = diagonals(tap(psf, 0), PSF, REACH, -1, 256) * over
    edge = corner(tap(psf, 0), PSF, REACH) * over[0:1, :128]
    ends[...] = jnp.zeros(ends.shape, BF16)
    for squared in range(2):
        for m in range(16 if flats is not None else 0):
            flats[squared, pl.ds(16 * m, 16), :] = toeplitz(flat, m, -REACH, REACH).astype(BF16)
        for part in range(ends.shape[1] // 128):
            span = pl.ds(128 * part, 128)
            ends[squared, pl.ds(128 * part, 16), span] = edge[16:].astype(BF16)
            ends[squared, pl.ds(128 * part + 112, 16), span] = edge[:16].astype(BF16)
        flat, edge = flat * flat, edge * edge


def met(along, even, odd, at, start, rows):
    parts = even[start : start + rows, :], odd[start : start + rows, :]
    return choose((along & 1) == 1, *(parts[::-1] if at else parts))


def significance(scale, smooth, variance):
    return scale * smooth * lax.rsqrt(scale * scale * variance + 1.0)


def row_kernel(
    psf, tile_ref, var_ref, v_high, v_low, v_var, row_even, row_odd, out_ref, part_ref,
    img_in, var_in, frame, bands, flats, ends, v_rim, out, in_sems, out_sems,
):
    row, rows_n = lax.axis_index("trow"), lax.axis_size("trow")
    copies = []
    for i, start in enumerate((0, TILE - 2 * RIM)):
        rows = pl.ds(start, 2 * RIM)
        copies.append(pltpu.make_async_copy(tile_ref.at[rows, :], img_in.at[i], in_sems.at[2 * i]))
        copies.append(pltpu.make_async_copy(var_ref.at[rows, :], var_in.at[i], in_sems.at[2 * i + 1]))
    for copy in copies:
        copy.start()
    scale = largest(psf, 0) * largest(psf, 1)
    column_bands(psf, bands)
    row_bands(psf, flats, ends)
    for copy in copies:
        copy.wait()
    for i in range(2):
        mine, theirs = (pl.ds(RIM, 2 * RIM), pl.ds(0, RIM)) if i == 0 else (pl.ds(0, 2 * RIM), pl.ds(2 * RIM, RIM))
        frame[0, mine, :], frame[1, mine, :] = split(img_in[i])
        frame[2, mine, :] = var_in[i]
        inside = row < rows_n - 1 if i else row > 0
        for j in range(3):
            frame[j, theirs, :] = jnp.where(inside, met(row, row_even, row_odd, i, RIM * j, RIM), 0.0).astype(BF16)
            frame[j, pl.ds(3 * RIM, RIM), :] = jnp.zeros((RIM, TILE), BF16)
        value = dot(bands[0, :RIM, 0:64], frame[0]) + dot(bands[0, :RIM, 0:64], frame[1])
        v_rim[0, i], v_rim[1, i] = split(value)
        v_rim[2, i] = dot(bands[1, :RIM, 0:64], frame[2]).astype(BF16)

    columns = (v_high, v_low, v_var)

    def read(i, q, start, width):
        span = pl.ds(start, width)
        if q == 0:
            return jnp.concatenate([v_rim[i, 0, :, span], columns[i][RIM:256, span]], 0)
        if q == 3:
            return jnp.concatenate([columns[i][768 : TILE - RIM, span], v_rim[i, 1, :, span]], 0)
        return columns[i][256 * q : 256 * q + 256, span]

    near = lax.broadcasted_iota(jnp.int32, (256, 128), 1) < 64
    inner = pl.ds(128, TILE - 256)
    for q in range(4):
        rows = pl.ds(256 * q, 256)
        results = []
        for squared, parts in ((0, (0, 1)), (1, (2,))):
            def about(i, w):
                return jnp.where(near, read(i, q, 256 * w, 128), read(i, q, 256 * w - 128, 128))

            both = sum(dot(jnp.concatenate([about(i, 1), about(i, 2)], 1), ends[squared]) for i in parts)
            last = sum(dot(about(i, 3), ends[squared, 0:128, 0:128]) for i in parts)
            fixes = [None, both[:, :128], both[:, 128:], last, None]
            values = []
            for c in range(4):
                main = sum(dot(read(i, q, 256 * c, 256), flats[squared]) for i in parts)
                values.append(main[:, :128] + jnp.where(near, fixes[c], 0.0) if c > 0 else main[:, :128])
                values.append(main[:, 128:] + jnp.where(near, 0.0, fixes[c + 1]) if c < 3 else main[:, 128:])
            results.append(values)
            part_ref[squared, rows, 0:128] = values[0]
            part_ref[squared, rows, 128:256] = values[7]
        for c in range(1, 7):
            out[rows, pl.ds(128 * c, 128)] = significance(scale, results[0][c], results[1][c])
        pltpu.make_async_copy(out.at[rows, inner], out_ref.at[rows, inner], out_sems.at[q]).start()
    for q in range(4):
        rows = pl.ds(256 * q, 256)
        pltpu.make_async_copy(out.at[rows, inner], out_ref.at[rows, inner], out_sems.at[q]).wait()


def row_pass(psf, tile, tile_var, columns, *rims):
    return pl.pallas_call(
        row_kernel,
        in_specs=[SMEM(), HBM, HBM] + [VMEM] * 5,
        out_specs=[HBM, VMEM],
        out_shape=[jax.ShapeDtypeStruct((TILE, TILE), F32), jax.ShapeDtypeStruct((2, TILE, 256), F32)],
        scratch_shapes=[
            pltpu.VMEM((2, 2 * RIM, TILE), F32),
            pltpu.VMEM((2, 2 * RIM, TILE), BF16),
            pltpu.VMEM((3, 4 * RIM, TILE), BF16),
            pltpu.VMEM((2, STEP, 256), BF16),
            pltpu.VMEM((2, 256, 256), BF16),
            pltpu.VMEM((2, 256, 256), BF16),
            pltpu.VMEM((3, 2, RIM, TILE), BF16),
            pltpu.VMEM((TILE, TILE), F32),
            pltpu.SemaphoreType.DMA((4,)),
            pltpu.SemaphoreType.DMA((4,)),
        ],
        compiler_params=pltpu.CompilerParams(vmem_limit_bytes=24 * MIB),
        name="row",
    )(psf, tile, tile_var, *columns, *rims)


def side_kernel(psf, held, part_ref, col_even, col_odd, out_ref, sides, bands, ends, v_side, out, out_sems):
    col, cols_n = lax.axis_index("tcol"), lax.axis_size("tcol")
    scale = largest(psf, 0) * largest(psf, 1)
    column_bands(psf, bands)
    row_bands(psf, None, ends)
    lanes = lax.broadcasted_iota(jnp.int32, (128, 128), 1)
    at_west, at_east = (lanes >= 128 - RIM) & (col > 0), (lanes < RIM) & (col < cols_n - 1)
    for i in range(3):
        sides[i, pl.ds(2 * RIM + TILE, 2 * RIM), :] = jnp.zeros((2 * RIM, 128), BF16)
        west, east = (met(col, col_even, col_odd, at, 128 * i, 128) for at in range(2))
        for g in range(8):
            near = pltpu.roll(east, 128 - RIM * g, 1) if g else east
            far = pltpu.roll(west, (112 - RIM * g) % 128, 1) if g != 7 else west
            sides[i, pl.ds(RIM + 128 * g, 128), :] = jnp.where(at_east, near, jnp.where(at_west, far, 0.0)).astype(BF16)
        for at, start in ((0, 384), (RIM + TILE, 432)):
            far, near = (met(col, col_even, col_odd, side, start + RIM * i, RIM) for side in range(2))
            sides[i, pl.ds(at, RIM), :] = jnp.where(at_east[:RIM], near, jnp.where(at_west[:RIM], far, 0.0)).astype(BF16)
    for t in range(5):
        count = min(STEP, TILE - STEP * t)
        window = pl.ds(STEP * t, 256)
        target = pl.ds(STEP * t, count)
        value = dot(bands[0], sides[0, window, :]) + dot(bands[0], sides[1, window, :])
        v_side[0, target, :], v_side[1, target, :] = split(value[:count])
        v_side[2, target, :] = dot(bands[1], sides[2, window, :])[:count].astype(BF16)
    near = lax.broadcasted_iota(jnp.int32, (256, 128), 1) < 64
    copies = []
    for q in range(4):
        rows = pl.ds(256 * q, 256)
        smooth = dot(v_side[0, rows, :], ends[0]) + dot(v_side[1, rows, :], ends[0])
        variance = dot(v_side[2, rows, :], ends[1])
        for side, start in ((0, 0), (1, TILE - 128)):
            fixes = [jnp.where(near, 0.0, x) if side else jnp.where(near, x, 0.0) for x in (smooth, variance)]
            span = pl.ds(128 * side, 128)
            sums = [part_ref[squared, rows, span] + fixes[squared] for squared in range(2)]
            out[rows, span] = significance(scale, *sums)
            copy = pltpu.make_async_copy(out.at[rows, span], out_ref.at[rows, pl.ds(start, 128)], out_sems.at[2 * q + side])
            copy.start()
            copies.append(copy)
    for copy in copies:
        copy.wait()


def side_pass(psf, held, part, *rims):
    return pl.pallas_call(
        side_kernel,
        in_specs=[SMEM(), HBM] + [VMEM] * 3,
        out_specs=HBM,
        out_shape=jax.ShapeDtypeStruct((TILE, TILE), F32),
        scratch_shapes=[
            pltpu.VMEM((3, 1088, 128), BF16),
            pltpu.VMEM((2, STEP, 256), BF16),
            pltpu.VMEM((2, 128, 128), BF16),
            pltpu.VMEM((3, TILE, 128), BF16),
            pltpu.VMEM((TILE, 256), F32),
            pltpu.SemaphoreType.DMA((8,)),
        ],
        input_output_aliases={1: 0},
        compiler_params=pltpu.CompilerParams(vmem_limit_bytes=12 * MIB),
        name="side",
    )(psf, held, part, *rims)


def shards(ccd_image, ccd_variance, basis_taps, coef_table, coef_pick, block_visit, visit_weight, patch_place, psf_taps):
    place = patch_place.reshape(NP)
    taps = basis_taps.astype(F32).reshape(-1)
    psf = psf_taps.reshape(-1)
    pin = lambda x: pltpu.with_memory_space_constraint(x, pltpu.HBM)
    small = (*map(pin, (coef_table, coef_pick, block_visit, visit_weight, patch_place)), taps)

    *parcels, own_image = match(False, *small, pin(ccd_image.reshape(2, BLOCK, BLOCK)))
    ahead = first_stage(parcels)
    taps_var, own_image = lax.optimization_barrier((taps, own_image))
    *parcels_var, own_var = match(True, *small[:-1], taps_var, pin(ccd_variance.reshape(2, BLOCK, BLOCK)))
    behind = first_stage(parcels_var)
    base_var = own_sum("own_var", place, own_var)
    *ahead, base_var = lax.optimization_barrier((*ahead, base_var))
    arrived = second_stage(parcels, *ahead)
    *behind, east, west = lax.optimization_barrier((*behind, *arrived[2:]))
    arrived_var = second_stage(parcels_var, *behind)
    tile, *rims = gather(True, place, own_image, *arrived[:2], east, west)
    tile_var, up, down, first, last = gather(False, place, base_var, *arrived_var, rims)
    rows = swap(up, "trow", False), swap(down, "trow", True)
    tile_read = pin(tile)
    columns = list(column_pass(psf, tile_read, tile_var))
    *rows, columns[0] = lax.optimization_barrier((*rows, columns[0]))
    sides = turn(first, last, *rows)
    met_sides = swap(sides[0], "tcol", False), swap(sides[1], "tcol", True)
    held, part = row_pass(psf, tile_read, tile_var, columns, *rows)
    *met_sides, part = lax.optimization_barrier((*met_sides, part))
    return tile, side_pass(psf, held, part, *met_sides)


def solution(mesh):
    place = P("trow", "tcol", None)
    blocks = P("trow", "tcol", None, None, None)
    in_specs = (blocks, blocks, P(), P(), place, place, P(), place, P())
    out_specs = (P("trow", "tcol"), P("trow", "tcol"))
    return jax.shard_map(shards, mesh=mesh, in_specs=in_specs, out_specs=out_specs, check_vma=False)
```

```python
import functools
import jax
import jax.numpy as jnp
from jax import lax
from jax.experimental import pallas as pl
from jax.experimental.pallas import tpu as pltpu
from jax.sharding import PartitionSpec as P

F32 = jnp.float32
BF16 = jnp.bfloat16
BLOCK = 512
PATCH = 128
TAPS = 21
RADIUS = 10
PSF = 31
REACH = 15
NBASIS = 6
NP = 32
CAP = 4
GROUP = CAP * PATCH + 16
TILE = 1024
RIM = 16
STEP = 208
MIB = 1 << 20

HBM = pl.BlockSpec(memory_space=pltpu.HBM)
VMEM = pl.BlockSpec(memory_space=pltpu.VMEM)
SMEM = functools.partial(pl.BlockSpec, memory_space=pltpu.SMEM)


def iotas(shape):
    return (lax.broadcasted_iota(jnp.int32, shape, 0), lax.broadcasted_iota(jnp.int32, shape, 1))


def dot(a, b):
    return jnp.dot(a, b, preferred_element_type=F32)


def split(x):
    high = x.astype(BF16)
    return high, (x - high.astype(F32)).astype(BF16)


def diagonals(read, count, first, step, lanes):
    rows, cols = iotas((16, lanes))
    offset = (cols - rows) & (lanes - 1)
    out = jnp.zeros((16, lanes), F32)
    for t in range(count):
        out = jnp.where(offset == (first + step * t) % lanes, read(t), out)
    return out


def toeplitz(base, m, low, high):
    lanes = base.shape[1]
    turned = pltpu.roll(base, (16 * m) % lanes, 1) if (16 * m) % lanes else base
    rows, cols = iotas(base.shape)
    offset = cols - rows - 16 * m
    return jnp.where((offset >= low) & (offset <= high), turned, 0.0)


def corner(read, count, reach):
    rows, cols = iotas((32, 128))
    left = rows < 16
    tap = rows + 112 - cols + reach - jnp.where(left, 128, 0)
    tap = jnp.where(left == (cols < 64), tap, -1)
    out = jnp.zeros((32, 128), F32)
    for t in range(count):
        out = jnp.where(tap == t, read(t), out)
    return out


def via(d):
    vertical = ((d * 11) >> 5) - 1
    sideways = d - 3 * ((d * 11) >> 5) - 1
    vertical = jnp.where((lax.axis_index("trow") & 1) == 0, -vertical, vertical)
    sideways = jnp.where((lax.axis_index("tcol") & 1) == 0, -sideways, sideways)
    return 3 * vertical + sideways + 4


def match_kernel(
    squared, table_in, pick_in, visit_in, weight_in, place_in, taps, x_in,
    up_ref, down_ref, left_ref, right_ref, own_ref,
    across, edges, down, rows_ref, total, leaving, count, slot, slots,
    table, pick, visit, weight, place, x_ref, sems, x_sem,
):
    small = [(table_in, table), (pick_in, pick), (visit_in, visit), (weight_in, weight), (place_in, place)]
    small = [pltpu.make_async_copy(a, b, sems.at[i]) for i, (a, b) in enumerate(small)]
    pixels = [pltpu.make_async_copy(x_in.at[b], x_ref.at[b], x_sem.at[b]) for b in range(2)]
    for copy in small + pixels:
        copy.start()

    def read(k, axis):
        return lambda t: taps[(2 * k + axis) * TAPS + t]

    def kept(x):
        return (x * x if squared else x).astype(BF16)

    def build(k):
        base = diagonals(read(k, 0), TAPS, RADIUS, -1, 256)
        for m in range(16):
            across[k, pl.ds(16 * m, 16), :] = kept(toeplitz(base, m, -RADIUS, RADIUS))
        edges[k // 2, pl.ds(112, 32), pl.ds(k % 2 * 128, 128)] = kept(corner(read(k, 0), TAPS, RADIUS))
        base = diagonals(read(k, 1), TAPS, -26, 1, 256)
        for m in range(18):
            down[k, pl.ds(16 * m, 16), :] = kept(toeplitz(base, m, -26, -6))

    for g in range(9):
        count[g] = 0
    for s in range(8 * CAP):
        slots[s] = -1
    edges[...] = jnp.zeros(edges.shape, BF16)
    for k in range(NBASIS // 2):
        build(k)
    for copy in small:
        copy.wait()
    for n in range(NP):
        entry = place[0, 0, n]
        d = via(entry >> 6)
        r = count[d]
        count[d] = r + 1
        s = jnp.where(d == 4, 8 * CAP, jnp.where(d > 4, d - 1, d) * CAP + r)
        slot[n] = s
        slots[s] = entry & 63
    for k in range(NBASIS // 2, NBASIS):
        build(k)
    _, lanes = iotas((16, 128))
    parcels = [(up_ref, 0), (up_ref, 1), (up_ref, 2), (left_ref, 0), (right_ref, 0), (down_ref, 0), (down_ref, 1), (down_ref, 2)]
    for g, (ref, at) in enumerate(parcels):
        line = jnp.full((16, 128), -1.0, F32)
        for s in range(CAP):
            line = jnp.where(lanes == s, slots[g * CAP + s].astype(F32), line)
        ref[at, pl.ds(CAP * PATCH, 16), :] = line.astype(BF16)

    def one(block, _):
        pltpu.make_async_copy(x_in.at[block], x_ref.at[block], x_sem.at[block]).wait()
        lanes = lax.broadcasted_iota(jnp.int32, (BLOCK, 128), 1)
        for pair in range(NBASIS // 2):
            fix = dot(x_ref[block, :, 128:384], edges[pair])
            for half in range(2):
                k = 2 * pair + half
                part = fix[:, 128 * half : 128 * half + 128]
                first = dot(x_ref[block, :, :256], across[k])
                rows_ref[k, :, 0:128] = first[:, :128].astype(BF16)
                rows_ref[k, :, 128:256] = (first[:, 128:] + jnp.where(lanes >= 64, part, 0.0)).astype(BF16)
                second = dot(x_ref[block, :, 256:], across[k])
                rows_ref[k, :, 256:384] = (second[:, :128] + jnp.where(lanes < 64, part, 0.0)).astype(BF16)
                rows_ref[k, :, 384:512] = second[:, 128:].astype(BF16)
        scale = weight[visit[0, 0, block]].astype(F32)
        if squared:
            scale = scale * scale
        for side in range(2):
            span = pl.ds(256 * side, 256)
            for k in range(NBASIS):
                coef = table[pick[0, 0, block], k]
                if squared:
                    coef = coef * coef
                top = dot(down[k, 16:288, :], rows_ref[k, 0:256, span])
                low = dot(down[k, 0:272, :], rows_ref[k, 256:512, span])
                middle = top[240:] + low[:32]
                if k == 0:
                    total[0:240, span] = coef * top[:240]
                    total[240:272, span] = coef * middle
                    total[272:512, span] = coef * low[32:]
                else:
                    total[0:240, span] += coef * top[:240]
                    total[240:272, span] += coef * middle
                    total[272:512, span] += coef * low[32:]
        for i in range(4):
            for j in range(4):
                n = block * 16 + 4 * i + j
                square = (scale * total[128 * i : 128 * i + 128, 128 * j : 128 * j + 128]).astype(BF16)
                own_ref[n] = square
                leaving[slot[n]] = square

    lax.fori_loop(0, 2, one, None)
    for g, (ref, at) in enumerate(parcels):
        for s in range(CAP):
            ref[at, pl.ds(s * PATCH, PATCH), :] = leaving[g * CAP + s]


def match(squared, table, pick, visit, weight, place, taps, blocks):
    shapes = ((3, GROUP, 128), (3, GROUP, 128), (1, GROUP, 128), (1, GROUP, 128), (NP, PATCH, PATCH))
    return pl.pallas_call(
        functools.partial(match_kernel, squared),
        in_specs=[HBM] * 5 + [SMEM(), HBM],
        out_specs=[VMEM] * 5,
        out_shape=[jax.ShapeDtypeStruct(s, BF16) for s in shapes],
        scratch_shapes=[
            pltpu.VMEM((NBASIS, 256, 256), BF16),
            pltpu.VMEM((NBASIS // 2, 256, 256), BF16),
            pltpu.VMEM((NBASIS, 288, 256), BF16),
            pltpu.VMEM((NBASIS, BLOCK, BLOCK), BF16),
            pltpu.VMEM((BLOCK, BLOCK), F32),
            pltpu.VMEM((8 * CAP + 1, PATCH, PATCH), BF16),
            pltpu.SMEM((9,), jnp.int32),
            pltpu.SMEM((NP,), jnp.int32),
            pltpu.SMEM((8 * CAP + 1,), jnp.int32),
            pltpu.SMEM(table.shape, F32),
            pltpu.SMEM(pick.shape, jnp.int32),
            pltpu.SMEM(visit.shape, jnp.int32),
            pltpu.SMEM(weight.shape, jnp.int32),
            pltpu.SMEM(place.shape, jnp.int32),
            pltpu.VMEM((2, BLOCK, BLOCK), BF16),
            pltpu.SemaphoreType.DMA((5,)),
            pltpu.SemaphoreType.DMA((2,)),
        ],
        compiler_params=pltpu.CompilerParams(vmem_limit_bytes=24 * MIB),
        name="match_var" if squared else "match_img",
    )(table, pick, visit, weight, place, taps, blocks)


def swap(value, axis, odd):
    rows, cols = lax.axis_size("trow"), lax.axis_size("tcol")
    pairs = []
    for r in range(rows):
        for c in range(cols):
            at, count = (r, rows) if axis == "trow" else (c, cols)
            to = ((at + 1) ^ 1) - 1 if odd else at ^ 1
            if axis == "trow":
                target = (to, c) if 0 <= to < count else (r, c ^ 1)
            else:
                target = (r, to) if 0 <= to < count else (r ^ 1, c)
            pairs.append((r * cols + c, target[0] * cols + target[1]))
    return lax.ppermute(value, ("trow", "tcol"), pairs)


def first_stage(parcels):
    return swap(parcels[0], "trow", False), swap(parcels[1], "trow", True)


def second_stage(parcels, below, above):
    _, _, left, right = parcels
    leftward = jnp.concatenate([left, below[0:1], above[0:1]], 0)
    rightward = jnp.concatenate([right, below[2:3], above[2:3]], 0)
    east = swap(rightward, "tcol", True)
    return below, above, east, swap(leftward, "tcol", False)


def pack(read, first):
    lanes = lax.broadcasted_iota(jnp.int32, (128, 128), 1)
    out = jnp.zeros((128, 128), F32)
    for g in range(8):
        rows = read(pl.ds(128 * g, 128))
        rows = jnp.where(lanes < RIM if first else lanes >= 128 - RIM, rows, 0.0)
        turn = RIM * g if first else (RIM * g + RIM) % 128
        out = out + (pltpu.roll(rows, turn, 1) if turn else rows)
    return out


def add(tile_ref, spot, square):
    rows = pl.ds(pl.multiple_of((spot >> 3) * PATCH, PATCH), PATCH)
    cols = pl.ds(pl.multiple_of((spot & 7) * PATCH, PATCH), PATCH)
    tile_ref[rows, cols] += square.astype(F32)


def add_own(place, own_ref, tile_ref):
    tile_ref[...] = jnp.zeros(tile_ref.shape, F32)

    def own(n, _):
        entry = place[n]

        @pl.when((entry >> 6) == 4)
        def _():
            add(tile_ref, entry & 63, own_ref[n])

    lax.fori_loop(0, NP, own, None)


def own_sum(name, place, own):
    return pl.pallas_call(
        add_own,
        in_specs=[SMEM(), VMEM],
        out_specs=VMEM,
        out_shape=jax.ShapeDtypeStruct((TILE, TILE), F32),
        compiler_params=pltpu.CompilerParams(vmem_limit_bytes=12 * MIB),
        name=name,
    )(place, own)


def gather_kernel(image, place, start_ref, below_ref, above_ref, east_ref, west_ref, *rest):
    if image:
        tile_ref, up_ref, down_ref, first_ref, last_ref, lines, spots, sem = rest
    else:
        up_in, down_in, first_in, last_in, out_ref, up_ref, down_ref, first_ref, last_ref, lines, spots, sem, tile_ref = rest
    groups = [(below_ref, 1), (above_ref, 1)] + [(east_ref, g) for g in range(3)] + [(west_ref, g) for g in range(3)]
    for g, (ref, at) in enumerate(groups):
        lines[pl.ds(g, 1), :] = ref[at, CAP * PATCH :, :].astype(F32)[0:1].astype(jnp.int32)
    copy = pltpu.make_async_copy(lines, spots, sem)
    copy.start()
    if image:
        add_own(place, start_ref, tile_ref)
    else:
        tile_ref[...] = start_ref[...]
    copy.wait()
    for g, (ref, at) in enumerate(groups):
        for s in range(CAP):
            spot = spots[g, s]

            @pl.when(spot >= 0)
            def _():
                add(tile_ref, spot, ref[at, s * PATCH : (s + 1) * PATCH, :])

    first = pack(lambda rows: tile_ref[rows, :128], True)
    last = pack(lambda rows: tile_ref[rows, TILE - 128 :], False)
    even = (lax.axis_index("trow") & 1) == 0
    ends = [tile_ref[pl.ds(pl.multiple_of(jnp.where(even, a, TILE - RIM - a), RIM), RIM), :] for a in (TILE - RIM, 0)]
    if image:
        for ref, value, n in ((up_ref, ends[0], RIM), (down_ref, ends[1], RIM), (first_ref, first, 128), (last_ref, last, 128)):
            ref[pl.ds(0, n), :], ref[pl.ds(n, n), :] = split(value)
    else:
        out_ref[...] = tile_ref[...].astype(BF16)
        for ref, old, value, n in (
            (up_ref, up_in, ends[0], RIM), (down_ref, down_in, ends[1], RIM),
            (first_ref, first_in, first, 128), (last_ref, last_in, last, 128),
        ):
            ref[pl.ds(0, 2 * n), :] = old[...]
            ref[pl.ds(2 * n, n), :] = value.astype(BF16)


def gather(image, place, start, below, above, east, west, rims=()):
    count = 2 if image else 3
    shapes = [(TILE, TILE), (count * RIM, TILE), (count * RIM, TILE), (count * 128, 128), (count * 128, 128)]
    return pl.pallas_call(
        functools.partial(gather_kernel, image),
        in_specs=[SMEM()] + [VMEM] * (5 + len(rims)),
        out_specs=[VMEM] * len(shapes),
        out_shape=[jax.ShapeDtypeStruct(s, F32 if image and i == 0 else BF16) for i, s in enumerate(shapes)],
        scratch_shapes=[pltpu.VMEM((8, 128), jnp.int32), pltpu.SMEM((8, 128), jnp.int32), pltpu.SemaphoreType.DMA]
        + ([] if image else [pltpu.VMEM((TILE, TILE), F32)]),
        compiler_params=pltpu.CompilerParams(vmem_limit_bytes=20 * MIB),
        name="gather_img" if image else "gather_var",
    )(place, start, below, above, east, west, *rims)


def choose(first, a, b):
    return jnp.where(first, a.astype(F32), b.astype(F32))


def turn_kernel(first_ref, last_ref, even_first, odd_first, even_last, odd_last, even_out, odd_out):
    here, count = lax.axis_index("trow"), lax.axis_size("trow")
    row_odd, col_odd = (here & 1) == 1, (lax.axis_index("tcol") & 1) == 1
    for out, flip in ((even_out, col_odd), (odd_out, jnp.logical_not(col_odd))):
        out[pl.ds(0, 384), :] = choose(flip, first_ref[...], last_ref[...]).astype(BF16)
        met = [choose(flip, a[...], b[...]) for a, b in ((even_first, even_last), (odd_first, odd_last))]
        out[pl.ds(384, 48), :] = jnp.where(here > 0, choose(row_odd, *met), 0.0).astype(BF16)
        out[pl.ds(432, 48), :] = jnp.where(here < count - 1, choose(row_odd, *met[::-1]), 0.0).astype(BF16)


def turn(first, last, even, odd):
    whole = pl.BlockSpec((384, 128), lambda i: (0, 0))
    near = pl.BlockSpec((48, 128), lambda i: (0, 0))
    far = pl.BlockSpec((48, 128), lambda i: (0, 7))
    return pl.pallas_call(
        turn_kernel,
        grid=(1,),
        in_specs=[whole, whole, near, near, far, far],
        out_specs=[pl.BlockSpec((480, 128), lambda i: (0, 0))] * 2,
        out_shape=[jax.ShapeDtypeStruct((480, 128), BF16)] * 2,
        compiler_params=pltpu.CompilerParams(vmem_limit_bytes=8 * MIB),
        name="turn",
    )(first, last, even, odd, even, odd)


def tap(psf, axis):
    return lambda t: psf[axis * PSF + t]


def largest(psf, axis):
    peak = psf[axis * PSF]
    for t in range(1, PSF):
        peak = jnp.maximum(peak, psf[axis * PSF + t])
    return peak


def column_bands(psf, bands):
    column = diagonals(tap(psf, 1), PSF, 1, 1, 256) / jnp.full((16, 256), largest(psf, 1), F32)
    for squared in range(2):
        for m in range(STEP // 16):
            bands[squared, pl.ds(16 * m, 16), :] = toeplitz(column, m, 1, PSF).astype(BF16)
        column = column * column


def column_kernel(psf, tile_ref, var_ref, v_high, v_low, v_var, img_in, high, low, var, bands, in_sems):
    copies = []
    for q in range(4):
        rows = pl.ds(256 * q, 256)
        inside = pl.ds(256 * q + RIM, 256)
        copies.append((
            pltpu.make_async_copy(tile_ref.at[rows, :], img_in.at[rows, :], in_sems.at[2 * q]),
            pltpu.make_async_copy(var_ref.at[rows, :], var.at[inside, :], in_sems.at[2 * q + 1]),
        ))
    for pair in copies:
        for copy in pair:
            copy.start()
    column_bands(psf, bands)
    for ref in (high, low, var):
        ref[pl.ds(0, RIM), :] = jnp.zeros((RIM, TILE), BF16)
        ref[pl.ds(RIM + TILE, 3 * RIM), :] = jnp.zeros((3 * RIM, TILE), BF16)
    ready = 0
    for t in range(5):
        count = min(STEP, TILE - STEP * t)
        while ready < 4 and 256 * ready < STEP * t + 240:
            for copy in copies[ready]:
                copy.wait()
            high[pl.ds(RIM + 256 * ready, 256), :], low[pl.ds(RIM + 256 * ready, 256), :] = split(img_in[pl.ds(256 * ready, 256), :])
            ready += 1
        window = pl.ds(STEP * t, 256)
        target = pl.ds(STEP * t, count)
        for c in range(4):
            span = pl.ds(256 * c, 256)
            value = dot(bands[0], high[window, span]) + dot(bands[0], low[window, span])
            v_high[target, span], v_low[target, span] = split(value[:count])
            v_var[target, span] = dot(bands[1], var[window, span])[:count].astype(BF16)


def column_pass(psf, tile, tile_var):
    return pl.pallas_call(
        column_kernel,
        in_specs=[SMEM(), HBM, HBM],
        out_specs=[VMEM] * 3,
        out_shape=[jax.ShapeDtypeStruct((TILE, TILE), BF16)] * 3,
        scratch_shapes=[pltpu.VMEM((TILE, TILE), F32)]
        + [pltpu.VMEM((1088, TILE), BF16)] * 3
        + [pltpu.VMEM((2, STEP, 256), BF16), pltpu.SemaphoreType.DMA((8,))],
        compiler_params=pltpu.CompilerParams(vmem_limit_bytes=22 * MIB),
        name="column",
    )(psf, tile, tile_var)


def row_bands(psf, flats, ends):
    over = 1.0 / jnp.full((16, 256), largest(psf, 0), F32)
    flat = diagonals(tap(psf, 0), PSF, REACH, -1, 256) * over
    edge = corner(tap(psf, 0), PSF, REACH) * over[0:1, :128]
    ends[...] = jnp.zeros(ends.shape, BF16)
    for squared in range(2):
        for m in range(16 if flats is not None else 0):
            flats[squared, pl.ds(16 * m, 16), :] = toeplitz(flat, m, -REACH, REACH).astype(BF16)
        for part in range(ends.shape[1] // 128):
            span = pl.ds(128 * part, 128)
            ends[squared, pl.ds(128 * part, 16), span] = edge[16:].astype(BF16)
            ends[squared, pl.ds(128 * part + 112, 16), span] = edge[:16].astype(BF16)
        flat, edge = flat * flat, edge * edge


def met(along, even, odd, at, start, rows):
    parts = even[start : start + rows, :], odd[start : start + rows, :]
    return choose((along & 1) == 1, *(parts[::-1] if at else parts))


def significance(scale, smooth, variance):
    return scale * smooth * lax.rsqrt(scale * scale * variance + 1.0)


def row_kernel(
    psf, tile_ref, var_ref, v_high, v_low, v_var, row_even, row_odd, out_ref, part_ref,
    img_in, var_in, frame, bands, flats, ends, v_rim, out, in_sems, out_sems,
):
    row, rows_n = lax.axis_index("trow"), lax.axis_size("trow")
    copies = []
    for i, start in enumerate((0, TILE - 2 * RIM)):
        rows = pl.ds(start, 2 * RIM)
        copies.append(pltpu.make_async_copy(tile_ref.at[rows, :], img_in.at[i], in_sems.at[2 * i]))
        copies.append(pltpu.make_async_copy(var_ref.at[rows, :], var_in.at[i], in_sems.at[2 * i + 1]))
    for copy in copies:
        copy.start()
    scale = largest(psf, 0) * largest(psf, 1)
    column_bands(psf, bands)
    row_bands(psf, flats, ends)
    for copy in copies:
        copy.wait()
    for i in range(2):
        mine, theirs = (pl.ds(RIM, 2 * RIM), pl.ds(0, RIM)) if i == 0 else (pl.ds(0, 2 * RIM), pl.ds(2 * RIM, RIM))
        frame[0, mine, :], frame[1, mine, :] = split(img_in[i])
        frame[2, mine, :] = var_in[i]
        inside = row < rows_n - 1 if i else row > 0
        for j in range(3):
            frame[j, theirs, :] = jnp.where(inside, met(row, row_even, row_odd, i, RIM * j, RIM), 0.0).astype(BF16)
            frame[j, pl.ds(3 * RIM, RIM), :] = jnp.zeros((RIM, TILE), BF16)
        value = dot(bands[0, :RIM, 0:64], frame[0]) + dot(bands[0, :RIM, 0:64], frame[1])
        v_rim[0, i], v_rim[1, i] = split(value)
        v_rim[2, i] = dot(bands[1, :RIM, 0:64], frame[2]).astype(BF16)

    columns = (v_high, v_low, v_var)

    def read(i, q, start, width):
        span = pl.ds(start, width)
        if q == 0:
            return jnp.concatenate([v_rim[i, 0, :, span], columns[i][RIM:256, span]], 0)
        if q == 3:
            return jnp.concatenate([columns[i][768 : TILE - RIM, span], v_rim[i, 1, :, span]], 0)
        return columns[i][256 * q : 256 * q + 256, span]

    near = lax.broadcasted_iota(jnp.int32, (256, 128), 1) < 64
    inner = pl.ds(128, TILE - 256)
    for q in range(4):
        rows = pl.ds(256 * q, 256)
        results = []
        for squared, parts in ((0, (0, 1)), (1, (2,))):
            def about(i, w):
                return jnp.where(near, read(i, q, 256 * w, 128), read(i, q, 256 * w - 128, 128))

            both = sum(dot(jnp.concatenate([about(i, 1), about(i, 2)], 1), ends[squared]) for i in parts)
            last = sum(dot(about(i, 3), ends[squared, 0:128, 0:128]) for i in parts)
            fixes = [None, both[:, :128], both[:, 128:], last, None]
            values = []
            for c in range(4):
                main = sum(dot(read(i, q, 256 * c, 256), flats[squared]) for i in parts)
                values.append(main[:, :128] + jnp.where(near, fixes[c], 0.0) if c > 0 else main[:, :128])
                values.append(main[:, 128:] + jnp.where(near, 0.0, fixes[c + 1]) if c < 3 else main[:, 128:])
            results.append(values)
            part_ref[squared, rows, 0:128] = values[0]
            part_ref[squared, rows, 128:256] = values[7]
        for c in range(1, 7):
            out[rows, pl.ds(128 * c, 128)] = significance(scale, results[0][c], results[1][c])
        pltpu.make_async_copy(out.at[rows, inner], out_ref.at[rows, inner], out_sems.at[q]).start()
    for q in range(4):
        rows = pl.ds(256 * q, 256)
        pltpu.make_async_copy(out.at[rows, inner], out_ref.at[rows, inner], out_sems.at[q]).wait()


def row_pass(psf, tile, tile_var, columns, *rims):
    return pl.pallas_call(
        row_kernel,
        in_specs=[SMEM(), HBM, HBM] + [VMEM] * 5,
        out_specs=[HBM, VMEM],
        out_shape=[jax.ShapeDtypeStruct((TILE, TILE), F32), jax.ShapeDtypeStruct((2, TILE, 256), F32)],
        scratch_shapes=[
            pltpu.VMEM((2, 2 * RIM, TILE), F32),
            pltpu.VMEM((2, 2 * RIM, TILE), BF16),
            pltpu.VMEM((3, 4 * RIM, TILE), BF16),
            pltpu.VMEM((2, STEP, 256), BF16),
            pltpu.VMEM((2, 256, 256), BF16),
            pltpu.VMEM((2, 256, 256), BF16),
            pltpu.VMEM((3, 2, RIM, TILE), BF16),
            pltpu.VMEM((TILE, TILE), F32),
            pltpu.SemaphoreType.DMA((4,)),
            pltpu.SemaphoreType.DMA((4,)),
        ],
        compiler_params=pltpu.CompilerParams(vmem_limit_bytes=24 * MIB),
        name="row",
    )(psf, tile, tile_var, *columns, *rims)


def side_kernel(psf, held, part_ref, col_odd, col_even, out_ref, sides, bands, ends, v_side, out, out_sems):
    col, cols_n = lax.axis_index("tcol"), lax.axis_size("tcol")
    scale = largest(psf, 0) * largest(psf, 1)
    column_bands(psf, bands)
    row_bands(psf, None, ends)
    lanes = lax.broadcasted_iota(jnp.int32, (128, 128), 1)
    at_west, at_east = (lanes >= 128 - RIM) & (col > 0), (lanes < RIM) & (col < cols_n - 1)
    for i in range(3):
        sides[i, pl.ds(2 * RIM + TILE, 2 * RIM), :] = jnp.zeros((2 * RIM, 128), BF16)
        west, east = (met(col, col_even, col_odd, at, 128 * i, 128) for at in range(2))
        for g in range(8):
            near = pltpu.roll(east, 128 - RIM * g, 1) if g else east
            far = pltpu.roll(west, (112 - RIM * g) % 128, 1) if g != 7 else west
            sides[i, pl.ds(RIM + 128 * g, 128), :] = jnp.where(at_east, near, jnp.where(at_west, far, 0.0)).astype(BF16)
        for at, start in ((0, 384), (RIM + TILE, 432)):
            far, near = (met(col, col_even, col_odd, side, start + RIM * i, RIM) for side in range(2))
            sides[i, pl.ds(at, RIM), :] = jnp.where(at_east[:RIM], near, jnp.where(at_west[:RIM], far, 0.0)).astype(BF16)
    for t in range(5):
        count = min(STEP, TILE - STEP * t)
        window = pl.ds(STEP * t, 256)
        target = pl.ds(STEP * t, count)
        value = dot(bands[0], sides[0, window, :]) + dot(bands[0], sides[1, window, :])
        v_side[0, target, :], v_side[1, target, :] = split(value[:count])
        v_side[2, target, :] = dot(bands[1], sides[2, window, :])[:count].astype(BF16)
    near = lax.broadcasted_iota(jnp.int32, (256, 128), 1) < 64
    copies = []
    for q in range(4):
        rows = pl.ds(256 * q, 256)
        smooth = dot(v_side[0, rows, :], ends[0]) + dot(v_side[1, rows, :], ends[0])
        variance = dot(v_side[2, rows, :], ends[1])
        for side, start in ((0, 0), (1, TILE - 128)):
            fixes = [jnp.where(near, 0.0, x) if side else jnp.where(near, x, 0.0) for x in (smooth, variance)]
            span = pl.ds(128 * side, 128)
            sums = [part_ref[squared, rows, span] + fixes[squared] for squared in range(2)]
            out[rows, span] = significance(scale, *sums)
            copy = pltpu.make_async_copy(out.at[rows, span], out_ref.at[rows, pl.ds(start, 128)], out_sems.at[2 * q + side])
            copy.start()
            copies.append(copy)
    for copy in copies:
        copy.wait()


def side_pass(psf, held, part, *rims):
    return pl.pallas_call(
        side_kernel,
        in_specs=[SMEM(), HBM] + [VMEM] * 3,
        out_specs=HBM,
        out_shape=jax.ShapeDtypeStruct((TILE, TILE), F32),
        scratch_shapes=[
            pltpu.VMEM((3, 1088, 128), BF16),
            pltpu.VMEM((2, STEP, 256), BF16),
            pltpu.VMEM((2, 128, 128), BF16),
            pltpu.VMEM((3, TILE, 128), BF16),
            pltpu.VMEM((TILE, 256), F32),
            pltpu.SemaphoreType.DMA((8,)),
        ],
        input_output_aliases={1: 0},
        compiler_params=pltpu.CompilerParams(vmem_limit_bytes=12 * MIB),
        name="side",
    )(psf, held, part, *rims)


def shards(ccd_image, ccd_variance, basis_taps, coef_table, coef_pick, block_visit, visit_weight, patch_place, psf_taps):
    place = patch_place.reshape(NP)
    taps = basis_taps.astype(F32).reshape(-1)
    psf = psf_taps.reshape(-1)
    pin = lambda x: pltpu.with_memory_space_constraint(x, pltpu.HBM)
    small = (*map(pin, (coef_table, coef_pick, block_visit, visit_weight, patch_place)), taps)

    *parcels, own_image = match(False, *small, pin(ccd_image.reshape(2, BLOCK, BLOCK)))
    ahead = first_stage(parcels)
    taps_var, own_image = lax.optimization_barrier((taps, own_image))
    *parcels_var, own_var = match(True, *small[:-1], taps_var, pin(ccd_variance.reshape(2, BLOCK, BLOCK)))
    behind = first_stage(parcels_var)
    base_var = own_sum("own_var", place, own_var)
    *ahead, base_var = lax.optimization_barrier((*ahead, base_var))
    arrived = second_stage(parcels, *ahead)
    *behind, east, west = lax.optimization_barrier((*behind, *arrived[2:]))
    arrived_var = second_stage(parcels_var, *behind)
    tile, *rims = gather(True, place, own_image, *arrived[:2], east, west)
    tile_var, up, down, first, last = gather(False, place, base_var, *arrived_var, rims)
    rows = swap(up, "trow", False), swap(down, "trow", True)
    tile_read = pin(tile)
    columns = list(column_pass(psf, tile_read, tile_var))
    *rows, columns[0] = lax.optimization_barrier((*rows, columns[0]))
    sides = turn(first, last, *rows)
    met_sides = swap(sides[1], "tcol", True), swap(sides[0], "tcol", False)
    held, part = row_pass(psf, tile_read, tile_var, columns, *rows)
    *met_sides, part = lax.optimization_barrier((*met_sides, part))
    return tile, side_pass(psf, held, part, *met_sides)


def solution(mesh):
    place = P("trow", "tcol", None)
    blocks = P("trow", "tcol", None, None, None)
    in_specs = (blocks, blocks, P(), P(), place, place, P(), place, P())
    out_specs = (P("trow", "tcol"), P("trow", "tcol"))
    return jax.shard_map(shards, mesh=mesh, in_specs=in_specs, out_specs=out_specs, check_vma=False)
```

```python
import functools
import jax
import jax.numpy as jnp
from jax import lax
from jax.experimental import pallas as pl
from jax.experimental.pallas import tpu as pltpu
from jax.sharding import PartitionSpec as P

F32 = jnp.float32
BF16 = jnp.bfloat16
BLOCK = 512
PATCH = 128
TAPS = 21
RADIUS = 10
PSF = 31
REACH = 15
NBASIS = 6
NP = 32
CAP = 4
GROUP = CAP * PATCH + 16
TILE = 1024
RIM = 16
STEP = 208
MIB = 1 << 20

HBM = pl.BlockSpec(memory_space=pltpu.HBM)
VMEM = pl.BlockSpec(memory_space=pltpu.VMEM)
SMEM = functools.partial(pl.BlockSpec, memory_space=pltpu.SMEM)


def iotas(shape):
    return (lax.broadcasted_iota(jnp.int32, shape, 0), lax.broadcasted_iota(jnp.int32, shape, 1))


def dot(a, b):
    return jnp.dot(a, b, preferred_element_type=F32)


def split(x):
    high = x.astype(BF16)
    return high, (x - high.astype(F32)).astype(BF16)


def diagonals(read, count, first, step, lanes):
    rows, cols = iotas((16, lanes))
    offset = (cols - rows) & (lanes - 1)
    out = jnp.zeros((16, lanes), F32)
    for t in range(count):
        out = jnp.where(offset == (first + step * t) % lanes, read(t), out)
    return out


def toeplitz(base, m, low, high):
    lanes = base.shape[1]
    turned = pltpu.roll(base, (16 * m) % lanes, 1) if (16 * m) % lanes else base
    rows, cols = iotas(base.shape)
    offset = cols - rows - 16 * m
    return jnp.where((offset >= low) & (offset <= high), turned, 0.0)


def corner(read, count, reach):
    rows, cols = iotas((32, 128))
    left = rows < 16
    tap = rows + 112 - cols + reach - jnp.where(left, 128, 0)
    tap = jnp.where(left == (cols < 64), tap, -1)
    out = jnp.zeros((32, 128), F32)
    for t in range(count):
        out = jnp.where(tap == t, read(t), out)
    return out


def via(d):
    vertical = ((d * 11) >> 5) - 1
    sideways = d - 3 * ((d * 11) >> 5) - 1
    vertical = jnp.where((lax.axis_index("trow") & 1) == 0, -vertical, vertical)
    sideways = jnp.where((lax.axis_index("tcol") & 1) == 0, -sideways, sideways)
    return 3 * vertical + sideways + 4


def match_kernel(
    squared, table_in, pick_in, visit_in, weight_in, place_in, taps, x_in,
    up_ref, down_ref, left_ref, right_ref, own_ref,
    across, edges, down, rows_ref, total, leaving, count, slot, slots,
    table, pick, visit, weight, place, x_ref, sems, x_sem,
):
    small = [(table_in, table), (pick_in, pick), (visit_in, visit), (weight_in, weight), (place_in, place)]
    small = [pltpu.make_async_copy(a, b, sems.at[i]) for i, (a, b) in enumerate(small)]
    pixels = [pltpu.make_async_copy(x_in.at[b], x_ref.at[b], x_sem.at[b]) for b in range(2)]
    for copy in small + pixels:
        copy.start()

    def read(k, axis):
        return lambda t: taps[(2 * k + axis) * TAPS + t]

    def kept(x):
        return (x * x if squared else x).astype(BF16)

    def build(k):
        base = diagonals(read(k, 0), TAPS, RADIUS, -1, 256)
        for m in range(16):
            across[k, pl.ds(16 * m, 16), :] = kept(toeplitz(base, m, -RADIUS, RADIUS))
        edges[k // 2, pl.ds(112, 32), pl.ds(k % 2 * 128, 128)] = kept(corner(read(k, 0), TAPS, RADIUS))
        base = diagonals(read(k, 1), TAPS, -26, 1, 256)
        for m in range(18):
            down[k, pl.ds(16 * m, 16), :] = kept(toeplitz(base, m, -26, -6))

    for g in range(9):
        count[g] = 0
    for s in range(8 * CAP):
        slots[s] = -1
    edges[...] = jnp.zeros(edges.shape, BF16)
    for k in range(NBASIS // 2):
        build(k)
    for copy in small:
        copy.wait()
    for n in range(NP):
        entry = place[0, 0, n]
        d = via(entry >> 6)
        r = count[d]
        count[d] = r + 1
        s = jnp.where(d == 4, 8 * CAP, jnp.where(d > 4, d - 1, d) * CAP + r)
        slot[n] = s
        slots[s] = entry & 63
    for k in range(NBASIS // 2, NBASIS):
        build(k)
    _, lanes = iotas((16, 128))
    parcels = [(up_ref, 0), (up_ref, 1), (up_ref, 2), (left_ref, 0), (right_ref, 0), (down_ref, 0), (down_ref, 1), (down_ref, 2)]
    for g, (ref, at) in enumerate(parcels):
        line = jnp.full((16, 128), -1.0, F32)
        for s in range(CAP):
            line = jnp.where(lanes == s, slots[g * CAP + s].astype(F32), line)
        ref[at, pl.ds(CAP * PATCH, 16), :] = line.astype(BF16)

    def one(block, _):
        pltpu.make_async_copy(x_in.at[block], x_ref.at[block], x_sem.at[block]).wait()
        lanes = lax.broadcasted_iota(jnp.int32, (BLOCK, 128), 1)
        for pair in range(NBASIS // 2):
            fix = dot(x_ref[block, :, 128:384], edges[pair])
            for half in range(2):
                k = 2 * pair + half
                part = fix[:, 128 * half : 128 * half + 128]
                first = dot(x_ref[block, :, :256], across[k])
                rows_ref[k, :, 0:128] = first[:, :128].astype(BF16)
                rows_ref[k, :, 128:256] = (first[:, 128:] + jnp.where(lanes >= 64, part, 0.0)).astype(BF16)
                second = dot(x_ref[block, :, 256:], across[k])
                rows_ref[k, :, 256:384] = (second[:, :128] + jnp.where(lanes < 64, part, 0.0)).astype(BF16)
                rows_ref[k, :, 384:512] = second[:, 128:].astype(BF16)
        scale = weight[visit[0, 0, block]].astype(F32)
        if squared:
            scale = scale * scale
        for side in range(2):
            span = pl.ds(256 * side, 256)
            for k in range(NBASIS):
                coef = table[pick[0, 0, block], k]
                if squared:
                    coef = coef * coef
                top = dot(down[k, 16:288, :], rows_ref[k, 0:256, span])
                low = dot(down[k, 0:272, :], rows_ref[k, 256:512, span])
                middle = top[240:] + low[:32]
                if k == 0:
                    total[0:240, span] = coef * top[:240]
                    total[240:272, span] = coef * middle
                    total[272:512, span] = coef * low[32:]
                else:
                    total[0:240, span] += coef * top[:240]
                    total[240:272, span] += coef * middle
                    total[272:512, span] += coef * low[32:]
        for i in range(4):
            for j in range(4):
                n = block * 16 + 4 * i + j
                square = (scale * total[128 * i : 128 * i + 128, 128 * j : 128 * j + 128]).astype(BF16)
                own_ref[n] = square
                leaving[slot[n]] = square

    lax.fori_loop(0, 2, one, None)
    for g, (ref, at) in enumerate(parcels):
        for s in range(CAP):
            ref[at, pl.ds(s * PATCH, PATCH), :] = leaving[g * CAP + s]


def match(squared, table, pick, visit, weight, place, taps, blocks):
    shapes = ((3, GROUP, 128), (3, GROUP, 128), (1, GROUP, 128), (1, GROUP, 128), (NP, PATCH, PATCH))
    return pl.pallas_call(
        functools.partial(match_kernel, squared),
        in_specs=[HBM] * 5 + [SMEM(), HBM],
        out_specs=[VMEM] * 5,
        out_shape=[jax.ShapeDtypeStruct(s, BF16) for s in shapes],
        scratch_shapes=[
            pltpu.VMEM((NBASIS, 256, 256), BF16),
            pltpu.VMEM((NBASIS // 2, 256, 256), BF16),
            pltpu.VMEM((NBASIS, 288, 256), BF16),
            pltpu.VMEM((NBASIS, BLOCK, BLOCK), BF16),
            pltpu.VMEM((BLOCK, BLOCK), F32),
            pltpu.VMEM((8 * CAP + 1, PATCH, PATCH), BF16),
            pltpu.SMEM((9,), jnp.int32),
            pltpu.SMEM((NP,), jnp.int32),
            pltpu.SMEM((8 * CAP + 1,), jnp.int32),
            pltpu.SMEM(table.shape, F32),
            pltpu.SMEM(pick.shape, jnp.int32),
            pltpu.SMEM(visit.shape, jnp.int32),
            pltpu.SMEM(weight.shape, jnp.int32),
            pltpu.SMEM(place.shape, jnp.int32),
            pltpu.VMEM((2, BLOCK, BLOCK), BF16),
            pltpu.SemaphoreType.DMA((5,)),
            pltpu.SemaphoreType.DMA((2,)),
        ],
        compiler_params=pltpu.CompilerParams(vmem_limit_bytes=24 * MIB),
        name="match_var" if squared else "match_img",
    )(table, pick, visit, weight, place, taps, blocks)


def swap(value, axis, odd):
    rows, cols = lax.axis_size("trow"), lax.axis_size("tcol")
    pairs = []
    for r in range(rows):
        for c in range(cols):
            at, count = (r, rows) if axis == "trow" else (c, cols)
            to = ((at + 1) ^ 1) - 1 if odd else at ^ 1
            if axis == "trow":
                target = (to, c) if 0 <= to < count else (r, c ^ 1)
            else:
                target = (r, to) if 0 <= to < count else (r ^ 1, c)
            pairs.append((r * cols + c, target[0] * cols + target[1]))
    return lax.ppermute(value, ("trow", "tcol"), pairs)


def first_stage(parcels):
    return swap(parcels[0], "trow", False), swap(parcels[1], "trow", True)


def second_stage(parcels, below, above):
    _, _, left, right = parcels
    leftward = jnp.concatenate([left, below[0:1], above[0:1]], 0)
    rightward = jnp.concatenate([right, below[2:3], above[2:3]], 0)
    return below, above, swap(leftward, "tcol", False), swap(rightward, "tcol", True)


def pack(read, first):
    lanes = lax.broadcasted_iota(jnp.int32, (128, 128), 1)
    out = jnp.zeros((128, 128), F32)
    for g in range(8):
        rows = read(pl.ds(128 * g, 128))
        rows = jnp.where(lanes < RIM if first else lanes >= 128 - RIM, rows, 0.0)
        turn = RIM * g if first else (RIM * g + RIM) % 128
        out = out + (pltpu.roll(rows, turn, 1) if turn else rows)
    return out


def add(tile_ref, spot, square):
    rows = pl.ds(pl.multiple_of((spot >> 3) * PATCH, PATCH), PATCH)
    cols = pl.ds(pl.multiple_of((spot & 7) * PATCH, PATCH), PATCH)
    tile_ref[rows, cols] += square.astype(F32)


def add_own(place, own_ref, tile_ref):
    tile_ref[...] = jnp.zeros(tile_ref.shape, F32)

    def own(n, _):
        entry = place[n]

        @pl.when((entry >> 6) == 4)
        def _():
            add(tile_ref, entry & 63, own_ref[n])

    lax.fori_loop(0, NP, own, None)


def own_sum(name, place, own):
    return pl.pallas_call(
        add_own,
        in_specs=[SMEM(), VMEM],
        out_specs=VMEM,
        out_shape=jax.ShapeDtypeStruct((TILE, TILE), F32),
        compiler_params=pltpu.CompilerParams(vmem_limit_bytes=12 * MIB),
        name=name,
    )(place, own)


def gather_kernel(image, place, start_ref, below_ref, above_ref, east_ref, west_ref, *rest):
    if image:
        tile_ref, up_ref, down_ref, first_ref, last_ref, lines, spots, sem = rest
    else:
        up_in, down_in, first_in, last_in, out_ref, up_ref, down_ref, first_ref, last_ref, lines, spots, sem, tile_ref = rest
    groups = [(below_ref, 1), (above_ref, 1)] + [(east_ref, g) for g in range(3)] + [(west_ref, g) for g in range(3)]
    for g, (ref, at) in enumerate(groups):
        lines[pl.ds(g, 1), :] = ref[at, CAP * PATCH :, :].astype(F32)[0:1].astype(jnp.int32)
    copy = pltpu.make_async_copy(lines, spots, sem)
    copy.start()
    if image:
        add_own(place, start_ref, tile_ref)
    else:
        tile_ref[...] = start_ref[...]
    copy.wait()
    for g, (ref, at) in enumerate(groups):
        for s in range(CAP):
            spot = spots[g, s]

            @pl.when(spot >= 0)
            def _():
                add(tile_ref, spot, ref[at, s * PATCH : (s + 1) * PATCH, :])

    first = pack(lambda rows: tile_ref[rows, :128], True)
    last = pack(lambda rows: tile_ref[rows, TILE - 128 :], False)
    even = (lax.axis_index("trow") & 1) == 0
    ends = [tile_ref[pl.ds(pl.multiple_of(jnp.where(even, a, TILE - RIM - a), RIM), RIM), :] for a in (TILE - RIM, 0)]
    if image:
        for ref, value, n in ((up_ref, ends[0], RIM), (down_ref, ends[1], RIM), (first_ref, first, 128), (last_ref, last, 128)):
            ref[pl.ds(0, n), :], ref[pl.ds(n, n), :] = split(value)
    else:
        out_ref[...] = tile_ref[...].astype(BF16)
        for ref, old, value, n in (
            (up_ref, up_in, ends[0], RIM), (down_ref, down_in, ends[1], RIM),
            (first_ref, first_in, first, 128), (last_ref, last_in, last, 128),
        ):
            ref[pl.ds(0, 2 * n), :] = old[...]
            ref[pl.ds(2 * n, n), :] = value.astype(BF16)


def gather(image, place, start, below, above, east, west, rims=()):
    count = 2 if image else 3
    shapes = [(TILE, TILE), (count * RIM, TILE), (count * RIM, TILE), (count * 128, 128), (count * 128, 128)]
    return pl.pallas_call(
        functools.partial(gather_kernel, image),
        in_specs=[SMEM()] + [VMEM] * (5 + len(rims)),
        out_specs=[VMEM] * len(shapes),
        out_shape=[jax.ShapeDtypeStruct(s, F32 if image and i == 0 else BF16) for i, s in enumerate(shapes)],
        scratch_shapes=[pltpu.VMEM((8, 128), jnp.int32), pltpu.SMEM((8, 128), jnp.int32), pltpu.SemaphoreType.DMA]
        + ([] if image else [pltpu.VMEM((TILE, TILE), F32)]),
        compiler_params=pltpu.CompilerParams(vmem_limit_bytes=20 * MIB),
        name="gather_img" if image else "gather_var",
    )(place, start, below, above, east, west, *rims)


def choose(first, a, b):
    return jnp.where(first, a.astype(F32), b.astype(F32))


def turn_kernel(first_ref, last_ref, even_first, odd_first, even_last, odd_last, even_out, odd_out):
    here, count = lax.axis_index("trow"), lax.axis_size("trow")
    row_odd, col_odd = (here & 1) == 1, (lax.axis_index("tcol") & 1) == 1
    for out, flip in ((even_out, col_odd), (odd_out, jnp.logical_not(col_odd))):
        out[pl.ds(0, 384), :] = choose(flip, first_ref[...], last_ref[...]).astype(BF16)
        met = [choose(flip, a[...], b[...]) for a, b in ((even_first, even_last), (odd_first, odd_last))]
        out[pl.ds(384, 48), :] = jnp.where(here > 0, choose(row_odd, *met), 0.0).astype(BF16)
        out[pl.ds(432, 48), :] = jnp.where(here < count - 1, choose(row_odd, *met[::-1]), 0.0).astype(BF16)


def turn(first, last, even, odd):
    whole = pl.BlockSpec((384, 128), lambda i: (0, 0))
    near = pl.BlockSpec((48, 128), lambda i: (0, 0))
    far = pl.BlockSpec((48, 128), lambda i: (0, 7))
    return pl.pallas_call(
        turn_kernel,
        grid=(1,),
        in_specs=[whole, whole, near, near, far, far],
        out_specs=[pl.BlockSpec((480, 128), lambda i: (0, 0))] * 2,
        out_shape=[jax.ShapeDtypeStruct((480, 128), BF16)] * 2,
        compiler_params=pltpu.CompilerParams(vmem_limit_bytes=8 * MIB),
        name="turn",
    )(first, last, even, odd, even, odd)


def tap(psf, axis):
    return lambda t: psf[axis * PSF + t]


def largest(psf, axis):
    peak = psf[axis * PSF]
    for t in range(1, PSF):
        peak = jnp.maximum(peak, psf[axis * PSF + t])
    return peak


def column_bands(psf, bands):
    column = diagonals(tap(psf, 1), PSF, 1, 1, 256) / jnp.full((16, 256), largest(psf, 1), F32)
    for squared in range(2):
        for m in range(STEP // 16):
            bands[squared, pl.ds(16 * m, 16), :] = toeplitz(column, m, 1, PSF).astype(BF16)
        column = column * column


def column_kernel(psf, tile_ref, var_ref, v_high, v_low, v_var, img_in, high, low, var, bands, in_sems):
    copies = []
    for q in range(4):
        rows = pl.ds(256 * q, 256)
        inside = pl.ds(256 * q + RIM, 256)
        copies.append((
            pltpu.make_async_copy(tile_ref.at[rows, :], img_in.at[rows, :], in_sems.at[2 * q]),
            pltpu.make_async_copy(var_ref.at[rows, :], var.at[inside, :], in_sems.at[2 * q + 1]),
        ))
    for pair in copies:
        for copy in pair:
            copy.start()
    column_bands(psf, bands)
    for ref in (high, low, var):
        ref[pl.ds(0, RIM), :] = jnp.zeros((RIM, TILE), BF16)
        ref[pl.ds(RIM + TILE, 3 * RIM), :] = jnp.zeros((3 * RIM, TILE), BF16)
    ready = 0
    for t in range(5):
        count = min(STEP, TILE - STEP * t)
        while ready < 4 and 256 * ready < STEP * t + 240:
            for copy in copies[ready]:
                copy.wait()
            high[pl.ds(RIM + 256 * ready, 256), :], low[pl.ds(RIM + 256 * ready, 256), :] = split(img_in[pl.ds(256 * ready, 256), :])
            ready += 1
        window = pl.ds(STEP * t, 256)
        target = pl.ds(STEP * t, count)
        for c in range(4):
            span = pl.ds(256 * c, 256)
            value = dot(bands[0], high[window, span]) + dot(bands[0], low[window, span])
            v_high[target, span], v_low[target, span] = split(value[:count])
            v_var[target, span] = dot(bands[1], var[window, span])[:count].astype(BF16)


def column_pass(psf, tile, tile_var):
    return pl.pallas_call(
        column_kernel,
        in_specs=[SMEM(), HBM, HBM],
        out_specs=[VMEM] * 3,
        out_shape=[jax.ShapeDtypeStruct((TILE, TILE), BF16)] * 3,
        scratch_shapes=[pltpu.VMEM((TILE, TILE), F32)]
        + [pltpu.VMEM((1088, TILE), BF16)] * 3
        + [pltpu.VMEM((2, STEP, 256), BF16), pltpu.SemaphoreType.DMA((8,))],
        compiler_params=pltpu.CompilerParams(vmem_limit_bytes=22 * MIB),
        name="column",
    )(psf, tile, tile_var)


def row_bands(psf, flats, ends):
    over = 1.0 / jnp.full((16, 256), largest(psf, 0), F32)
    flat = diagonals(tap(psf, 0), PSF, REACH, -1, 256) * over
    edge = corner(tap(psf, 0), PSF, REACH) * over[0:1, :128]
    ends[...] = jnp.zeros(ends.shape, BF16)
    for squared in range(2):
        for m in range(16 if flats is not None else 0):
            flats[squared, pl.ds(16 * m, 16), :] = toeplitz(flat, m, -REACH, REACH).astype(BF16)
        for part in range(ends.shape[1] // 128):
            span = pl.ds(128 * part, 128)
            ends[squared, pl.ds(128 * part, 16), span] = edge[16:].astype(BF16)
            ends[squared, pl.ds(128 * part + 112, 16), span] = edge[:16].astype(BF16)
        flat, edge = flat * flat, edge * edge


def met(along, even, odd, at, start, rows):
    parts = even[start : start + rows, :], odd[start : start + rows, :]
    return choose((along & 1) == 1, *(parts[::-1] if at else parts))


def significance(scale, smooth, variance):
    return scale * smooth * lax.rsqrt(scale * scale * variance + 1.0)


def row_kernel(
    psf, tile_ref, var_ref, v_high, v_low, v_var, row_even, row_odd, out_ref, part_ref,
    img_in, var_in, frame, bands, flats, ends, v_rim, out, in_sems, out_sems,
):
    row, rows_n = lax.axis_index("trow"), lax.axis_size("trow")
    copies = []
    for i, start in enumerate((0, TILE - 2 * RIM)):
        rows = pl.ds(start, 2 * RIM)
        copies.append(pltpu.make_async_copy(tile_ref.at[rows, :], img_in.at[i], in_sems.at[2 * i]))
        copies.append(pltpu.make_async_copy(var_ref.at[rows, :], var_in.at[i], in_sems.at[2 * i + 1]))
    for copy in copies:
        copy.start()
    scale = largest(psf, 0) * largest(psf, 1)
    column_bands(psf, bands)
    row_bands(psf, flats, ends)
    for copy in copies:
        copy.wait()
    for i in range(2):
        mine, theirs = (pl.ds(RIM, 2 * RIM), pl.ds(0, RIM)) if i == 0 else (pl.ds(0, 2 * RIM), pl.ds(2 * RIM, RIM))
        frame[0, mine, :], frame[1, mine, :] = split(img_in[i])
        frame[2, mine, :] = var_in[i]
        inside = row < rows_n - 1 if i else row > 0
        for j in range(3):
            frame[j, theirs, :] = jnp.where(inside, met(row, row_even, row_odd, i, RIM * j, RIM), 0.0).astype(BF16)
            frame[j, pl.ds(3 * RIM, RIM), :] = jnp.zeros((RIM, TILE), BF16)
        value = dot(bands[0, :RIM, 0:64], frame[0]) + dot(bands[0, :RIM, 0:64], frame[1])
        v_rim[0, i], v_rim[1, i] = split(value)
        v_rim[2, i] = dot(bands[1, :RIM, 0:64], frame[2]).astype(BF16)

    columns = (v_high, v_low, v_var)

    def read(i, q, start, width):
        span = pl.ds(start, width)
        if q == 0:
            return jnp.concatenate([v_rim[i, 0, :, span], columns[i][RIM:256, span]], 0)
        if q == 3:
            return jnp.concatenate([columns[i][768 : TILE - RIM, span], v_rim[i, 1, :, span]], 0)
        return columns[i][256 * q : 256 * q + 256, span]

    near = lax.broadcasted_iota(jnp.int32, (256, 128), 1) < 64
    inner = pl.ds(128, TILE - 256)
    for q in range(4):
        rows = pl.ds(256 * q, 256)
        results = []
        for squared, parts in ((0, (0, 1)), (1, (2,))):
            def about(i, w):
                return jnp.where(near, read(i, q, 256 * w, 128), read(i, q, 256 * w - 128, 128))

            both = sum(dot(jnp.concatenate([about(i, 1), about(i, 2)], 1), ends[squared]) for i in parts)
            last = sum(dot(about(i, 3), ends[squared, 0:128, 0:128]) for i in parts)
            fixes = [None, both[:, :128], both[:, 128:], last, None]
            values = []
            for c in range(4):
                main = sum(dot(read(i, q, 256 * c, 256), flats[squared]) for i in parts)
                values.append(main[:, :128] + jnp.where(near, fixes[c], 0.0) if c > 0 else main[:, :128])
                values.append(main[:, 128:] + jnp.where(near, 0.0, fixes[c + 1]) if c < 3 else main[:, 128:])
            results.append(values)
            part_ref[squared, rows, 0:128] = values[0]
            part_ref[squared, rows, 128:256] = values[7]
        for c in range(1, 7):
            out[rows, pl.ds(128 * c, 128)] = significance(scale, results[0][c], results[1][c])
        pltpu.make_async_copy(out.at[rows, inner], out_ref.at[rows, inner], out_sems.at[q]).start()
    for q in range(4):
        rows = pl.ds(256 * q, 256)
        pltpu.make_async_copy(out.at[rows, inner], out_ref.at[rows, inner], out_sems.at[q]).wait()


def row_pass(psf, tile, tile_var, columns, *rims):
    return pl.pallas_call(
        row_kernel,
        in_specs=[SMEM(), HBM, HBM] + [VMEM] * 5,
        out_specs=[HBM, VMEM],
        out_shape=[jax.ShapeDtypeStruct((TILE, TILE), F32), jax.ShapeDtypeStruct((2, TILE, 256), F32)],
        scratch_shapes=[
            pltpu.VMEM((2, 2 * RIM, TILE), F32),
            pltpu.VMEM((2, 2 * RIM, TILE), BF16),
            pltpu.VMEM((3, 4 * RIM, TILE), BF16),
            pltpu.VMEM((2, STEP, 256), BF16),
            pltpu.VMEM((2, 256, 256), BF16),
            pltpu.VMEM((2, 256, 256), BF16),
            pltpu.VMEM((3, 2, RIM, TILE), BF16),
            pltpu.VMEM((TILE, TILE), F32),
            pltpu.SemaphoreType.DMA((4,)),
            pltpu.SemaphoreType.DMA((4,)),
        ],
        compiler_params=pltpu.CompilerParams(vmem_limit_bytes=24 * MIB),
        name="row",
    )(psf, tile, tile_var, *columns, *rims)


def side_kernel(psf, held, part_ref, col_even, col_odd, out_ref, sides, bands, ends, v_side, out, out_sems):
    col, cols_n = lax.axis_index("tcol"), lax.axis_size("tcol")
    scale = largest(psf, 0) * largest(psf, 1)
    column_bands(psf, bands)
    row_bands(psf, None, ends)
    lanes = lax.broadcasted_iota(jnp.int32, (128, 128), 1)
    at_west, at_east = (lanes >= 128 - RIM) & (col > 0), (lanes < RIM) & (col < cols_n - 1)
    for i in range(3):
        sides[i, pl.ds(2 * RIM + TILE, 2 * RIM), :] = jnp.zeros((2 * RIM, 128), BF16)
        west, east = (met(col, col_even, col_odd, at, 128 * i, 128) for at in range(2))
        for g in range(8):
            near = pltpu.roll(east, 128 - RIM * g, 1) if g else east
            far = pltpu.roll(west, (112 - RIM * g) % 128, 1) if g != 7 else west
            sides[i, pl.ds(RIM + 128 * g, 128), :] = jnp.where(at_east, near, jnp.where(at_west, far, 0.0)).astype(BF16)
        for at, start in ((0, 384), (RIM + TILE, 432)):
            far, near = (met(col, col_even, col_odd, side, start + RIM * i, RIM) for side in range(2))
            sides[i, pl.ds(at, RIM), :] = jnp.where(at_east[:RIM], near, jnp.where(at_west[:RIM], far, 0.0)).astype(BF16)
    for t in range(5):
        count = min(STEP, TILE - STEP * t)
        window = pl.ds(STEP * t, 256)
        target = pl.ds(STEP * t, count)
        value = dot(bands[0], sides[0, window, :]) + dot(bands[0], sides[1, window, :])
        v_side[0, target, :], v_side[1, target, :] = split(value[:count])
        v_side[2, target, :] = dot(bands[1], sides[2, window, :])[:count].astype(BF16)
    near = lax.broadcasted_iota(jnp.int32, (256, 128), 1) < 64
    copies = []
    for q in range(4):
        rows = pl.ds(256 * q, 256)
        smooth = dot(v_side[0, rows, :], ends[0]) + dot(v_side[1, rows, :], ends[0])
        variance = dot(v_side[2, rows, :], ends[1])
        for side, start in ((0, 0), (1, TILE - 128)):
            fixes = [jnp.where(near, 0.0, x) if side else jnp.where(near, x, 0.0) for x in (smooth, variance)]
            span = pl.ds(128 * side, 128)
            sums = [part_ref[squared, rows, span] + fixes[squared] for squared in range(2)]
            out[rows, span] = significance(scale, *sums)
            copy = pltpu.make_async_copy(out.at[rows, span], out_ref.at[rows, pl.ds(start, 128)], out_sems.at[2 * q + side])
            copy.start()
            copies.append(copy)
    for copy in copies:
        copy.wait()


def side_pass(psf, held, part, *rims):
    return pl.pallas_call(
        side_kernel,
        in_specs=[SMEM(), HBM] + [VMEM] * 3,
        out_specs=HBM,
        out_shape=jax.ShapeDtypeStruct((TILE, TILE), F32),
        scratch_shapes=[
            pltpu.VMEM((3, 1088, 128), BF16),
            pltpu.VMEM((2, STEP, 256), BF16),
            pltpu.VMEM((2, 128, 128), BF16),
            pltpu.VMEM((3, TILE, 128), BF16),
            pltpu.VMEM((TILE, 256), F32),
            pltpu.SemaphoreType.DMA((8,)),
        ],
        input_output_aliases={1: 0},
        compiler_params=pltpu.CompilerParams(vmem_limit_bytes=12 * MIB),
        name="side",
    )(psf, held, part, *rims)


def shards(ccd_image, ccd_variance, basis_taps, coef_table, coef_pick, block_visit, visit_weight, patch_place, psf_taps):
    place = patch_place.reshape(NP)
    taps = basis_taps.astype(F32).reshape(-1)
    psf = psf_taps.reshape(-1)
    pin = lambda x: pltpu.with_memory_space_constraint(x, pltpu.HBM)
    place, psf = pin(place), pin(psf)
    small = (*map(pin, (coef_table, coef_pick, block_visit, visit_weight, patch_place)), taps)

    *parcels, own_image = match(False, *small, pin(ccd_image.reshape(2, BLOCK, BLOCK)))
    ahead = first_stage(parcels)
    taps_var, own_image = lax.optimization_barrier((taps, own_image))
    *parcels_var, own_var = match(True, *small[:-1], taps_var, pin(ccd_variance.reshape(2, BLOCK, BLOCK)))
    behind = first_stage(parcels_var)
    base_var = own_sum("own_var", place, own_var)
    *ahead, base_var = lax.optimization_barrier((*ahead, base_var))
    arrived = second_stage(parcels, *ahead)
    *behind, east, west = lax.optimization_barrier((*behind, *arrived[2:]))
    arrived_var = second_stage(parcels_var, *behind)
    tile, *rims = gather(True, place, own_image, *arrived[:2], east, west)
    tile_var, up, down, first, last = gather(False, place, base_var, *arrived_var, rims)
    rows = swap(up, "trow", False), swap(down, "trow", True)
    tile_read = pin(tile)
    columns = list(column_pass(psf, tile_read, tile_var))
    *rows, columns[0] = lax.optimization_barrier((*rows, columns[0]))
    sides = turn(first, last, *rows)
    met_sides = swap(sides[0], "tcol", False), swap(sides[1], "tcol", True)
    held, part = row_pass(psf, tile_read, tile_var, columns, *rows)
    *met_sides, part = lax.optimization_barrier((*met_sides, part))
    return tile, side_pass(psf, held, part, *met_sides)


def solution(mesh):
    place = P("trow", "tcol", None)
    blocks = P("trow", "tcol", None, None, None)
    in_specs = (blocks, blocks, P(), P(), place, place, P(), place, P())
    out_specs = (P("trow", "tcol"), P("trow", "tcol"))
    return jax.shard_map(shards, mesh=mesh, in_specs=in_specs, out_specs=out_specs, check_vma=False)
```
